32 devices in a mesh: groups: 2 (over y), sec: 4 (over z), col: 2 (over x), rep: 2 (over core).
Axes of the slice: x: 2, y: 2, z: 4, core: 2. Of those that a mesh axis runs over, the one named last changes fastest.
Arguments:
- h_core: bfloat16 [10240, 5120], P(('groups', 'sec'), ('col', 'rep')), parts along dimension 0, may hold values from -2 to 2
- centers: float32 [3, 10240], P(None, 'groups'), parts along dimension 1, may hold values from 7 to 13
- mm_coords: float32 [3, 16384], P(None, ('groups', 'sec', 'col', 'rep')), parts along dimension 1, may hold values from 0 to 20
- mm_charges: float32 [16384], P(('groups', 'sec', 'col', 'rep')), parts along dimension 0, may hold values from -0.53033006 to 0.53033006
Outputs:
- density: float32 [10240, 5120], P(('groups', 'sec'), ('col', 'rep')), parts along dimension 0
- forces: float32 [3, 16384], P(None, ('groups', 'sec', 'col', 'rep')), parts along dimension 1
The draws below stay inside these ranges and needn't reach their ends.
There are 2 independent parts, one for each index of `groups`. The reference program is written for one: setup_inputs(seed, part) draws one part's arguments, and reference() takes and returns one part's arrays. A program takes and returns all parts, laid end to end along the dimension named above; each array names one. Nothing has to cross between parts.
All inputs are finite; a program needn't handle non-finite values.
Results may differ from the reference program's by a relative error of at most 0.0054.
Values may be sent and summed in bfloat16 or wider, within the bound.
No kernel may reach another device: no remote copies, remote signals or barrier semaphores. Data moves between devices by JAX's collectives and lax.ppermute only.
A program may use at most 128 MiB of HBM per device.

```python
import math
import jax
import jax.numpy as jnp
from jax import lax

NB = 5120
MM_DEV = 512
MM = 8192


def draw_h_core(key, part):
    key = jax.random.fold_in(key, 7)
    keys = jax.random.split(key, 3)
    rows = jnp.arange(NB, dtype=jnp.int32)[:, None]
    cols = jnp.arange(NB, dtype=jnp.int32)[None, :]
    upper_tri = rows < cols
    ramp = 1.0 + 2.0 * jnp.arange(NB, dtype=jnp.float32) / (NB - 1)
    level_top, off_gain, diag_low, diag_high, diag_gain = (math.log(3.2), 0.15, -1.0, 2.0, 0.25)
    levels = jnp.exp(jax.random.uniform(keys[0], (NB,), jnp.float32, 0.0, level_top))
    row_scale = jnp.sqrt(ramp * levels)
    noise = jax.random.uniform(keys[1], (NB, NB), jnp.float32, -1.0, 1.0)
    noise = jnp.where(upper_tri, noise, noise.T)
    off_vals = off_gain / NB ** 0.5 * row_scale[:, None] * row_scale[None, :] * noise
    diag_vals = diag_gain * ramp * jax.random.uniform(keys[2], (NB,), jnp.float32, diag_low, diag_high)
    matrix = jnp.where(rows == cols, diag_vals[:, None], off_vals)
    return matrix.astype(jnp.bfloat16)


def block_scale(own_key, extent, shards, smallest, top_value):
    def one(position, parts):
        draws = jax.random.uniform(jax.random.fold_in(jax.random.fold_in(own_key, 6), position), (parts,), jnp.float32, smallest / len(shards), top_value / len(shards))
        return jnp.repeat(jnp.exp(draws), extent[position] // parts).reshape((-1,) + (1,) * (len(extent) - position - 1))

    gain = one(*shards[0])
    for cut in shards[1:]:
        gain = gain * one(*cut)
    return gain


def scatter_about(own_key, extent, scale, reach, shards=(), held_as=jnp.bfloat16):
    values = scale * jax.random.normal(own_key, extent, jnp.float32)
    if shards:
        values = values * block_scale(own_key, extent, shards, -0.22, 0.18)
    return jnp.clip(values, -reach, reach).astype(held_as)


def setup_inputs(seed: int = 0, part: int = 0) -> dict:
    splits = jax.random.split(jax.random.key(seed), 5)
    part_keys = jax.random.split(jax.random.fold_in(splits[4], part), 5)
    return {
        "h_core": draw_h_core(jax.random.fold_in(jax.random.fold_in(splits[4], part), 71), part),
        "centers": jnp.clip(jax.random.uniform(part_keys[1], (3, NB), jnp.float32, 7.0, 13.0), 7.0, 13.0),
        "mm_coords": jnp.clip(20.0 * jax.random.uniform(part_keys[2], (3, MM), jnp.float32) ** block_scale(part_keys[2], (3, MM), ((1, 16),), -0.2, 0.2), 0.0, 20.0),
        "mm_charges": scatter_about(part_keys[3], (MM,), (8.0 * MM ** -0.5), 0.53033006, ((0, 16),), jnp.float32),
    }


def reference(h_core, centers, mm_coords, mm_charges):
    block_count = MM // MM_DEV

    def potential_step(total, index):
        coords = lax.dynamic_slice_in_dim(mm_coords, index * MM_DEV, MM_DEV, 1)
        charge = lax.dynamic_slice_in_dim(mm_charges, index * MM_DEV, MM_DEV, 0)
        dist = lax.optimization_barrier(jnp.sum((centers[:, :, None] - coords[:, None, :]) ** 2, 0)) + 1.0
        return (total + lax.optimization_barrier(jnp.sum(charge[None, :] * lax.rsqrt(dist), 1)), None)
    potential, _ = lax.scan(potential_step, jnp.zeros((NB,), jnp.float32), jnp.arange(block_count, dtype=jnp.int32))
    eye_mask = jnp.eye(NB, dtype=bool)
    eye_float = jnp.eye(NB, dtype=jnp.float32)
    ham = h_core.astype(jnp.float32) + jnp.where(eye_mask, potential[:, None], 0.0)
    off_sq = jnp.sum(jnp.where(eye_mask, 0.0, ham * ham))
    diag_vals = lax.optimization_barrier(jnp.sum(jnp.where(eye_mask, ham, 0.0), 1))
    mean_level = jnp.sum(diag_vals) / NB
    dev_sq = jnp.sum((diag_vals - mean_level) ** 2)
    spread = jnp.sqrt((off_sq + dev_sq) / NB + 1e-05)
    scale = 2.0 / (3.0 * spread)
    start_x = (0.5 * scale * (mean_level * eye_float - ham) + 0.5 * eye_float).astype(jnp.bfloat16)
    square = jnp.dot(start_x, start_x, preferred_element_type=jnp.float32)
    square_b = square.astype(jnp.bfloat16)
    cube = jnp.dot(square_b, start_x, preferred_element_type=jnp.float32)
    density = 3.0 * square - 2.0 * cube
    occupation = lax.optimization_barrier(jnp.sum(jnp.where(eye_mask, density, 0.0), 1))

    def force_block(index):
        coords = lax.dynamic_slice_in_dim(mm_coords, index * MM_DEV, MM_DEV, 1)
        charge = lax.dynamic_slice_in_dim(mm_charges, index * MM_DEV, MM_DEV, 0)
        diff = coords[:, None, :] - centers[:, :, None]
        dist = lax.optimization_barrier(jnp.sum(diff * diff, 0)) + 1.0
        weight = occupation[:, None] * lax.rsqrt(dist) / dist
        return -charge[None, :] * lax.optimization_barrier(jnp.sum(diff * weight[None], 1))
    blocks = lax.map(force_block, jnp.arange(block_count, dtype=jnp.int32))
    forces = jnp.transpose(blocks, (1, 0, 2)).reshape(3, MM)
    return (density, forces)
```

```python
import functools

import jax
import jax.numpy as jnp
from jax import lax
from jax.experimental import pallas as pl
from jax.experimental.pallas import tpu as pltpu
from jax.sharding import PartitionSpec as P

PART = ("sec", "col", "rep")


def potential_kernel(spots_ref, points_ref, out_ref):
    count = points_ref.shape[0]
    width = spots_ref.shape[1]
    sx, sy, sz = (spots_ref[k : k + 1, :] for k in range(3))

    def step(index, accum):
        rows = points_ref[pl.ds(pl.multiple_of(index * 8, 8), 8), :]
        dx = sx - rows[:, 0:1]
        dy = sy - rows[:, 1:2]
        dz = sz - rows[:, 2:3]
        dist = dx * dx + dy * dy + dz * dz + 1.0
        return accum + rows[:, 3:4] * lax.rsqrt(dist)

    total = lax.fori_loop(0, count // 8, step, jnp.zeros((8, width), jnp.float32), unroll=4)
    out_ref[...] = jnp.sum(total, 0, keepdims=True)


def potential_terms(centers, mm_coords, mm_charges):
    total = centers.shape[1]
    count = mm_coords.shape[1]
    width = 1024 if total % 1024 == 0 else total
    points = jnp.concatenate([mm_coords, mm_charges[None]], 0).T
    return pl.pallas_call(
        potential_kernel,
        grid=(total // width,),
        out_shape=jax.ShapeDtypeStruct((1, total), jnp.float32),
        in_specs=[
            pl.BlockSpec((3, width), lambda i: (0, i)),
            pl.BlockSpec((count, 4), lambda i: (0, 0)),
        ],
        out_specs=pl.BlockSpec((1, width), lambda i: (0, i)),
        name="potential",
    )(centers, points)


def force_kernel(spots_ref, occ_ref, points_ref, out_ref):
    total = spots_ref.shape[1]
    rows = points_ref[...]
    px, py, pz, charge = (rows[:, k : k + 1] for k in range(4))
    count = rows.shape[0]

    def step(index, accum):
        lanes = pl.ds(pl.multiple_of(index * 128, 128), 128)
        dx = px - spots_ref[0:1, lanes]
        dy = py - spots_ref[1:2, lanes]
        dz = pz - spots_ref[2:3, lanes]
        inv = lax.rsqrt(dx * dx + dy * dy + dz * dz + 1.0)
        weight = occ_ref[:, lanes] * inv * (inv * inv)
        return (accum[0] + dx * weight, accum[1] + dy * weight, accum[2] + dz * weight)

    zero = jnp.zeros((count, 128), jnp.float32)
    sums = lax.fori_loop(0, total // 128, step, (zero, zero, zero), unroll=4)
    for k in range(3):
        out_ref[:, k : k + 1] = -charge * jnp.sum(sums[k], 1, keepdims=True)


def force_terms(centers, occupation, mm_coords, mm_charges):
    total = centers.shape[1]
    count = mm_coords.shape[1]
    width = 32
    points = jnp.concatenate([mm_coords, mm_charges[None]], 0).T
    summed = pl.pallas_call(
        force_kernel,
        grid=(count // width,),
        out_shape=jax.ShapeDtypeStruct((count, 4), jnp.float32),
        in_specs=[
            pl.BlockSpec((3, total), lambda i: (0, 0)),
            pl.BlockSpec((1, total), lambda i: (0, 0)),
            pl.BlockSpec((width, 4), lambda i: (i, 0)),
        ],
        out_specs=pl.BlockSpec((width, 4), lambda i: (i, 0)),
        name="forces",
    )(centers, occupation, points)
    return summed[:, :3].T


def butterfly_sum(value, sizes):
    for axis in ("rep", "col", "sec"):
        size = sizes[axis]
        if size & (size - 1):
            value = lax.psum(value, axis)
            continue
        hop = 1
        while hop < size:
            value = value + lax.ppermute(value, axis, [(i, i ^ hop) for i in range(size)])
            hop *= 2
    return value


def fold_with(left, piece):
    return jnp.dot(left, piece, preferred_element_type=jnp.float32)


def shards(sizes, h_core, centers, mm_coords, mm_charges):
    row_count, col_count = h_core.shape
    total = centers.shape[1]
    row_start = lax.axis_index("sec") * row_count
    col_start = lax.axis_index(("col", "rep")) * col_count
    rows_glob = row_start + lax.broadcasted_iota(jnp.int32, (row_count, col_count), 0)
    cols_glob = col_start + lax.broadcasted_iota(jnp.int32, (row_count, col_count), 1)
    on_diag = rows_glob == cols_glob
    off = jnp.where(on_diag, jnp.zeros((), h_core.dtype), h_core)
    row_panel = lax.all_gather(off, ("col", "rep"), axis=1, tiled=True)
    col_panel = lax.all_gather(off, "sec", axis=0, tiled=True)

    wide = h_core.astype(jnp.float32)
    own_diag = jnp.sum(jnp.where(on_diag, wide, 0.0), 0)
    own_off = jnp.sum(jnp.where(on_diag, 0.0, wide * wide))
    terms = potential_terms(centers, mm_coords, mm_charges)[0]
    own_cols = lax.dynamic_slice_in_dim(terms, col_start, col_count, 0) + own_diag
    terms = lax.dynamic_update_slice_in_dim(terms, own_cols, col_start, 0)
    sums = butterfly_sum(jnp.concatenate([terms, jnp.full((128,), own_off)]), sizes)
    diag_vals, off_total = sums[:total], sums[total]
    mean_level = jnp.sum(diag_vals) / total
    level = diag_vals - mean_level
    spread = jnp.sqrt((off_total + jnp.sum(level * level)) / total + 1e-05)
    gain = 1.0 / (3.0 * spread)

    level_rows = lax.dynamic_slice_in_dim(level, row_start, row_count, 0)[:, None]
    level_cols = lax.dynamic_slice_in_dim(level, col_start, col_count, 0)[None, :]
    off_wide = off.astype(jnp.float32)
    square = fold_with(row_panel, col_panel)
    square = square + off_wide * (level_rows + level_cols) + jnp.where(on_diag, level_rows * level_rows, 0.0)
    shifted = off_wide + jnp.where(on_diag, level_rows, 0.0)
    square_b = square.astype(jnp.bfloat16)
    square_panel = lax.all_gather(square_b, ("col", "rep"), axis=1, tiled=True)
    own_cube = jnp.sum(square * shifted, 0)
    cube_diag = lax.dynamic_update_slice_in_dim(jnp.zeros((total,), jnp.float32), own_cube, col_start, 0)
    cube_diag = butterfly_sum(cube_diag, sizes)
    occupation = 0.5 - 1.5 * gain * level + 2.0 * gain**3 * cube_diag
    forces = force_terms(centers, occupation[None], mm_coords, mm_charges)

    cube = fold_with(square_panel, col_panel) + square_b.astype(jnp.float32) * level_cols
    density = jnp.where(on_diag, 0.5, 0.0) - 1.5 * gain * shifted + 2.0 * gain**3 * cube
    return (density, forces)


def solution(mesh):
    in_specs = (
        P(("groups", "sec"), ("col", "rep")),
        P(None, "groups"),
        P(None, ("groups", "sec", "col", "rep")),
        P(("groups", "sec", "col", "rep")),
    )
    out_specs = (P(("groups", "sec"), ("col", "rep")), P(None, ("groups", "sec", "col", "rep")))
    body = functools.partial(shards, dict(mesh.shape))
    return jax.shard_map(body, mesh=mesh, in_specs=in_specs, out_specs=out_specs, check_vma=False)
```

```python
import functools

import jax
import jax.numpy as jnp
from jax import lax
from jax.experimental import pallas as pl
from jax.experimental.pallas import tpu as pltpu
from jax.sharding import PartitionSpec as P

PART = ("sec", "col", "rep")


def potential_kernel(spots_ref, points_ref, out_ref):
    count = points_ref.shape[0]
    width = spots_ref.shape[1]
    sx, sy, sz = (spots_ref[k : k + 1, :] for k in range(3))

    def step(index, accum):
        rows = points_ref[pl.ds(pl.multiple_of(index * 8, 8), 8), :]
        dx = sx - rows[:, 0:1]
        dy = sy - rows[:, 1:2]
        dz = sz - rows[:, 2:3]
        dist = dx * dx + dy * dy + dz * dz + 1.0
        return accum + rows[:, 3:4] * lax.rsqrt(dist)

    total = lax.fori_loop(0, count // 8, step, jnp.zeros((8, width), jnp.float32), unroll=4)
    out_ref[...] = jnp.sum(total, 0, keepdims=True)


def potential_terms(centers, mm_coords, mm_charges):
    total = centers.shape[1]
    count = mm_coords.shape[1]
    width = 1024 if total % 1024 == 0 else total
    points = jnp.concatenate([mm_coords, mm_charges[None]], 0).T
    return pl.pallas_call(
        potential_kernel,
        grid=(total // width,),
        out_shape=jax.ShapeDtypeStruct((1, total), jnp.float32),
        in_specs=[
            pl.BlockSpec((3, width), lambda i: (0, i)),
            pl.BlockSpec((count, 4), lambda i: (0, 0)),
        ],
        out_specs=pl.BlockSpec((1, width), lambda i: (0, i)),
        name="potential",
    )(centers, points)


def force_kernel(spots_ref, occ_ref, points_ref, out_ref):
    total = spots_ref.shape[1]
    rows = points_ref[...]
    px, py, pz, charge = (rows[:, k : k + 1] for k in range(4))
    count = rows.shape[0]

    def step(index, accum):
        lanes = pl.ds(pl.multiple_of(index * 128, 128), 128)
        dx = px - spots_ref[0:1, lanes]
        dy = py - spots_ref[1:2, lanes]
        dz = pz - spots_ref[2:3, lanes]
        inv = lax.rsqrt(dx * dx + dy * dy + dz * dz + 1.0)
        weight = occ_ref[:, lanes] * inv * (inv * inv)
        return (accum[0] + dx * weight, accum[1] + dy * weight, accum[2] + dz * weight)

    zero = jnp.zeros((count, 128), jnp.float32)
    sums = lax.fori_loop(0, total // 128, step, (zero, zero, zero), unroll=4)
    for k in range(3):
        out_ref[:, k : k + 1] = -charge * jnp.sum(sums[k], 1, keepdims=True)


def force_terms(centers, occupation, mm_coords, mm_charges):
    total = centers.shape[1]
    count = mm_coords.shape[1]
    width = 32
    points = jnp.concatenate([mm_coords, mm_charges[None]], 0).T
    summed = pl.pallas_call(
        force_kernel,
        grid=(count // width,),
        out_shape=jax.ShapeDtypeStruct((count, 4), jnp.float32),
        in_specs=[
            pl.BlockSpec((3, total), lambda i: (0, 0)),
            pl.BlockSpec((1, total), lambda i: (0, 0)),
            pl.BlockSpec((width, 4), lambda i: (i, 0)),
        ],
        out_specs=pl.BlockSpec((width, 4), lambda i: (i, 0)),
        name="forces",
    )(centers, occupation, points)
    return summed[:, :3].T


def butterfly_sum(value, sizes, axes=("rep", "col", "sec")):
    for axis in axes:
        size = sizes[axis]
        if size & (size - 1):
            value = lax.psum(value, axis)
            continue
        hop = 1
        while hop < size:
            value = value + lax.ppermute(value, axis, [(i, i ^ hop) for i in range(size)])
            hop *= 2
    return value


def fold_with(left, piece):
    return jnp.dot(left, piece, preferred_element_type=jnp.float32)


def gather_shards(sizes, h_core, centers, mm_coords, mm_charges):
    row_count, col_count = h_core.shape
    total = centers.shape[1]
    row_start = lax.axis_index("sec") * row_count
    col_start = lax.axis_index(("col", "rep")) * col_count
    rows_glob = row_start + lax.broadcasted_iota(jnp.int32, (row_count, col_count), 0)
    cols_glob = col_start + lax.broadcasted_iota(jnp.int32, (row_count, col_count), 1)
    on_diag = rows_glob == cols_glob
    off = jnp.where(on_diag, jnp.zeros((), h_core.dtype), h_core)
    row_panel = lax.all_gather(off, ("col", "rep"), axis=1, tiled=True)
    col_panel = lax.all_gather(off, "sec", axis=0, tiled=True)

    wide = h_core.astype(jnp.float32)
    own_diag = jnp.sum(jnp.where(on_diag, wide, 0.0), 0)
    own_off = jnp.sum(jnp.where(on_diag, 0.0, wide * wide))
    terms = potential_terms(centers, mm_coords, mm_charges)[0]
    own_cols = lax.dynamic_slice_in_dim(terms, col_start, col_count, 0) + own_diag
    terms = lax.dynamic_update_slice_in_dim(terms, own_cols, col_start, 0)
    sums = butterfly_sum(jnp.concatenate([terms, jnp.full((128,), own_off)]), sizes)
    diag_vals, off_total = sums[:total], sums[total]
    mean_level = jnp.sum(diag_vals) / total
    level = diag_vals - mean_level
    spread = jnp.sqrt((off_total + jnp.sum(level * level)) / total + 1e-05)
    gain = 1.0 / (3.0 * spread)

    level_rows = lax.dynamic_slice_in_dim(level, row_start, row_count, 0)[:, None]
    level_cols = lax.dynamic_slice_in_dim(level, col_start, col_count, 0)[None, :]
    off_wide = off.astype(jnp.float32)
    square = fold_with(row_panel, col_panel)
    square = square + off_wide * (level_rows + level_cols) + jnp.where(on_diag, level_rows * level_rows, 0.0)
    shifted = off_wide + jnp.where(on_diag, level_rows, 0.0)
    square_b = square.astype(jnp.bfloat16)
    square_panel = lax.all_gather(square_b, ("col", "rep"), axis=1, tiled=True)
    own_cube = jnp.sum(square * shifted, 0)
    cube_diag = lax.dynamic_update_slice_in_dim(jnp.zeros((total,), jnp.float32), own_cube, col_start, 0)
    cube_diag = butterfly_sum(cube_diag, sizes)
    occupation = 0.5 - 1.5 * gain * level + 2.0 * gain**3 * cube_diag
    forces = force_terms(centers, occupation[None], mm_coords, mm_charges)

    cube = fold_with(square_panel, col_panel) + square_b.astype(jnp.float32) * level_cols
    density = jnp.where(on_diag, 0.5, 0.0) - 1.5 * gain * shifted + 2.0 * gain**3 * cube
    return (density, forces)


ROUND = ((0, 1), (1, 2), (2, 3), (3, 0))
BACK = ((0, 3), (3, 2), (2, 1), (1, 0))
Z_MOVES = ((ROUND, BACK), (BACK, ROUND), (ROUND, BACK), (ROUND, BACK))
OWN0, OWN1, X1, Z1, X2, Z2, X3, Z3, X4, Z4 = range(10)
X_SENDS = ((OWN1, OWN0, OWN1, OWN0), (OWN0, OWN1, OWN0, OWN1), (Z2,) * 4, (Z3, Z1, Z1, Z3))
Z_SENDS = ((OWN0, OWN1, OWN0, OWN1), (OWN1, X1, X1, OWN0), (X2,) * 4, (Z3, Z1, Z1, Z3))
SLOT_STAGE = (0, 0, 0, 0, 1, 1, 2, 2, 3, 3)
LEFT_SLOTS = (OWN0, OWN1, X1, X2)
LEFT_STAGE = (0, 0, 0, 1)
FIELDS = 8
NOTHING, MULTIPLY, FINISH, LEVEL = range(4)
BLOCK_BIT, LEFT_BIT, TOTAL_BIT = 0, 8, 16


def block_places():
    chips = [(z, x) for z in range(4) for x in range(2)]
    held = {(z, x): [(z, 2 * x), (z, 2 * x + 1)] for z, x in chips}
    for step in range(4):
        arrived = {}
        for z, x in chips:
            before = next(start for start, to in Z_MOVES[step][x] if to == z)
            arrived[(z, x)] = [held[(z, 1 - x)][X_SENDS[step][z]], held[(before, x)][Z_SENDS[step][before]]]
        for chip in chips:
            held[chip] = held[chip] + arrived[chip]
    return [held[chip] for chip in chips]


def rows_of(products, length):
    seen, rows = set(), []
    for kind, left, block, flip, total, column in products:
        bits = [LEFT_BIT + left, TOTAL_BIT + total]
        if kind == MULTIPLY:
            bits.append(BLOCK_BIT + block)
        waits = sum(1 << bit for bit in bits if bit not in seen)
        seen.update(bits)
        rows.append([kind, left, block, flip, total, waits, column, 0])
    rows += [[NOTHING] + [0] * (FIELDS - 1)] * (length - len(rows))
    rest = sum(1 << bit for bit in range(24) if bit not in seen)
    return rows + [[NOTHING, 0, 0, 0, 0, rest, 0, 0]]


def device_lists():
    devices = []
    for chip, slots in enumerate(block_places()):
        assert len({tuple(sorted(place)) for place in slots}) == 10
        row, col = divmod(chip, 2)
        assert all(slots[s][0] == row for s in LEFT_SLOTS)
        lefts = [slots[s][1] for s in LEFT_SLOTS]
        stages = [[], [], [], []]
        for slot, (first, second) in enumerate(slots):
            for inner, outer, flip in [(first, second, 0), (second, first, 1)][: 1 if first == second else 2]:
                left = lefts.index(inner)
                stage = max(LEFT_STAGE[left], SLOT_STAGE[slot])
                base = (0, 0, X3, X4)[stage]
                key = max(slot, LEFT_SLOTS[left])
                stages[stage].append((key, (MULTIPLY, left, slot - base, flip, outer, 0)))
        stages = [[product for _, product in sorted(stage)] for stage in stages]
        open_columns = sorted({product[4] for product in stages[3]})
        done_columns = [column for column in range(4) if column not in open_columns]
        assert len(open_columns) == 2

        def find(inner, outer):
            if (inner, outer) in slots:
                return slots.index((inner, outer)), 0
            return slots.index((outer, inner)), 1

        for core in range(2):
            early, early_slots = [], []
            for k, column in enumerate(done_columns):
                early.append((FINISH, 4 + k, lefts.index(column), int(column == row), column, column))
            for k, column in enumerate(done_columns):
                for which in range(2):
                    slot, flip = find(column, 2 * col + which)
                    early.append((MULTIPLY, 4 + k, 2 + len(early_slots), flip, 4 + which, 0))
                    early_slots.append(slot)
                    if column == 2 * col + which:
                        early.append((LEVEL, 4 + k, 0, 0, 4 + which, column))
            tails = []
            for which in (1 - core, core):
                tail, tail_slots = [], []
                last = which == core
                for k, column in enumerate(open_columns):
                    slot, flip = find(column, 2 * col + which)
                    position, left = (k, k) if last else (2 + k, 4 + k)
                    tail.append((MULTIPLY, left, position, flip, 0 if last else 2, 0))
                    tail_slots.append(slot)
                    if column == 2 * col + which:
                        tail.append((LEVEL, left, 0, 0, 0 if last else 2, column))
                tails.append((tail, tail_slots))
            late = [product[:4] + (open_columns.index(product[4]), 0) for product in stages[3]]
            late += [
                (FINISH, 4 + k, lefts.index(column), int(column == row), k, column)
                for k, column in enumerate(open_columns)
            ]
            devices.append(
                dict(
                    kernels=[stages[0], stages[1], stages[2], early, late, tails[0][0], tails[1][0]],
                    slots=[early_slots, tails[0][1], tails[1][1]],
                    open=open_columns,
                )
            )
    return devices


def device_tables():
    devices = device_lists()
    steps, rows = [], [[] for _ in devices]
    for kernel in range(7):
        length = max(len(device["kernels"][kernel]) for device in devices)
        steps.append((len(rows[0]), length))
        for row, device in zip(rows, devices):
            for fields in rows_of(device["kernels"][kernel], length):
                row += fields
    slots = []
    for kernel in range(3):
        slots.append(len(rows[0]))
        for row, device in zip(rows, devices):
            row += device["slots"][kernel]
    opened = len(rows[0])
    for row, device in zip(rows, devices):
        row += device["open"]
    return rows, steps, slots, opened


def bit_set(mask, bit):
    return lax.rem(lax.div(mask, jnp.int32(1 << bit)), jnp.int32(2)) == 1


class Worker:
    def __init__(self, table_ref, core, half, block_ref, block_sem, left_ref, left_sem, total_ref, total_sem):
        self.table_ref, self.core, self.half = table_ref, core, half
        self.block_ref, self.block_sem = block_ref, block_sem
        self.left_ref, self.left_sem = left_ref, left_sem
        self.total_ref, self.total_sem = total_ref, total_sem
        self.near = pl.ds(pl.multiple_of(core * half, half), half)
        self.far = pl.ds(pl.multiple_of((1 - core) * half, half), half)
        self.blocks, self.lefts, self.totals = [], [], []
        self.levels = None

    def load_halves(self, position, near_ref, far_ref):
        pltpu.make_async_copy(near_ref, self.block_ref.at[position, self.near], self.block_sem.at[position, 0]).start()
        pltpu.make_async_copy(far_ref, self.block_ref.at[position, self.far], self.block_sem.at[position, 1]).start()

    def load_block(self, position, slot, sources):
        self.blocks.append(position)
        whole_ref, got_ref, other_ref = sources["own"] if "own" in sources else (None, None, None)
        fixed = isinstance(slot, int)
        if whole_ref is not None and (not fixed or slot <= OWN1):
            @pl.when(slot == self.core)
            def _():
                self.load_halves(position, whole_ref.at[self.near], whole_ref.at[self.far])

            @pl.when(slot == 1 - self.core)
            def _():
                self.load_halves(position, got_ref, other_ref)

        if not fixed:
            for number, halves in sources.items():
                if number != "own":
                    pl.when(slot == number)(functools.partial(self.load_halves, position, *halves))
        if fixed and slot > OWN1:
            self.load_halves(position, *sources[slot])

    def load_left(self, index, ref, to=None):
        self.lefts.append(index)
        to = index if to is None else to
        pltpu.make_async_copy(ref, self.left_ref.at[to], self.left_sem.at[to]).start()

    def load_rows(self, refs):
        self.load_left(0, refs[0], self.core)
        self.load_left(1, refs[1], 1 - self.core)
        for k in range(2, len(refs)):
            self.load_left(k, refs[k])

    def load_total(self, index, ref):
        self.totals.append(index)
        pltpu.make_async_copy(ref, self.total_ref.at[index], self.total_sem.at[index]).start()

    def wait(self, mask):
        half_block = self.block_ref.at[0, pl.ds(0, self.half)]
        for position in self.blocks:
            @pl.when(bit_set(mask, BLOCK_BIT + position))
            def _():
                for part in range(2):
                    pltpu.make_async_copy(half_block, half_block, self.block_sem.at[position, part]).wait()
        for index in self.lefts:
            @pl.when(bit_set(mask, LEFT_BIT + index))
            def _():
                pltpu.make_async_copy(self.left_ref.at[0], self.left_ref.at[0], self.left_sem.at[index]).wait()
        for index in self.totals:
            @pl.when(bit_set(mask, TOTAL_BIT + index))
            def _():
                pltpu.make_async_copy(self.total_ref.at[0], self.total_ref.at[0], self.total_sem.at[index]).wait()

    def multiply(self, field):
        total, left, block = self.total_ref.at[field[4]], self.left_ref.at[field[1]], self.block_ref.at[field[2]]

        @pl.when(field[3] == 0)
        def _():
            total[...] += jnp.dot(left[...], block[...], preferred_element_type=jnp.float32)

        @pl.when(field[3] == 1)
        def _():
            total[...] += lax.dot_general(
                left[...], block[...], (((1,), (1,)), ((), ())), preferred_element_type=jnp.float32
            )

    def finish(self, field):
        rows_ref, cols_ref, diag_ref = self.levels
        half, width = self.half, self.block_ref.shape[2]
        total, left, made = self.total_ref.at[field[4]], self.left_ref.at[field[2]], self.left_ref.at[field[1]]
        cols = cols_ref[:, pl.ds(pl.multiple_of(field[6] * width, width), width)]
        chunk = 16

        def pass_rows(with_diag):
            def one(index, carry):
                rows = pl.ds(pl.multiple_of(index * chunk, chunk), chunk)
                level = rows_ref[rows, :]
                shifted = left[rows, :].astype(jnp.float32)
                square = total[rows, :] + shifted * (level + cols)
                if with_diag:
                    in_block = lax.broadcasted_iota(jnp.int32, (chunk, width), 1)
                    own = lax.broadcasted_iota(jnp.int32, (chunk, width), 0) + (self.core * half + index * chunk)
                    on_diag = in_block == own
                    square = square + jnp.where(on_diag, level * level, 0.0)
                    shifted = shifted + jnp.where(on_diag, level, 0.0)
                made[rows, :] = square.astype(jnp.bfloat16)
                diag_ref[rows, :] += jnp.sum(square * shifted, 1, keepdims=True)
                return carry

            lax.fori_loop(0, half // chunk, one, 0, unroll=2)

        @pl.when(field[3] == 0)
        def _():
            pass_rows(False)

        @pl.when(field[3] == 1)
        def _():
            pass_rows(True)

    def add_level(self, field):
        _, cols_ref, _ = self.levels
        width = self.block_ref.shape[2]
        total, left = self.total_ref.at[field[4]], self.left_ref.at[field[1]]
        cols = cols_ref[:, pl.ds(pl.multiple_of(field[6] * width, width), width)]
        chunk = 16

        def one(index, carry):
            rows = pl.ds(pl.multiple_of(index * chunk, chunk), chunk)
            total[rows, :] += left[rows, :].astype(jnp.float32) * cols
            return carry

        lax.fori_loop(0, self.half // chunk, one, 0, unroll=2)

    def run(self, start_count):
        start, count = start_count

        def step(index, carry):
            field = [self.table_ref[start + index * FIELDS + k] for k in range(7)]
            self.wait(field[5])
            pl.when(field[0] == MULTIPLY)(functools.partial(self.multiply, field))
            if self.levels is not None:
                if self.levels[0] is not None:
                    pl.when(field[0] == FINISH)(functools.partial(self.finish, field))
                pl.when(field[0] == LEVEL)(functools.partial(self.add_level, field))
            return carry

        lax.fori_loop(0, count, step, 0)

    def wait_rest(self, start_count):
        start, count = start_count
        self.wait(self.table_ref[start + count * FIELDS + 5])


def copy_all(pairs, sem):
    copies = [pltpu.make_async_copy(source, to, sem.at[k]) for k, (source, to) in enumerate(pairs)]
    for copy in copies:
        copy.start()
    return copies


def square_kernel(first, steps, left_count, slots, own, table_ref, place_ref, *refs):
    refs = list(refs)
    row_refs = [refs.pop(0) for _ in range(left_count)]
    sources = {"own": [refs.pop(0) for _ in range(3)]} if own else {}
    for slot in slots:
        if slot > OWN1:
            sources[slot] = (refs.pop(0), refs.pop(0))
    old_ref = None if first else refs.pop(0)
    new_ref, block_ref, block_sem, left_ref, left_sem, total_ref, total_sem, new_sem = refs
    half = left_ref.shape[1]
    worker = Worker(table_ref, place_ref[0], half, block_ref, block_sem, left_ref, left_sem, total_ref, total_sem)
    worker.load_rows(row_refs)
    for position, slot in enumerate(slots):
        worker.load_block(position, slot, sources)
        if position == 0 and not first:
            for k in range(4):
                worker.load_total(k, old_ref.at[k])
    if first:
        total_ref[...] = jnp.zeros_like(total_ref)
    worker.run(steps)
    worker.wait_rest(steps)
    for copy in copy_all([(total_ref.at[k], new_ref.at[k]) for k in range(4)], new_sem):
        copy.wait()


def early_kernel(steps, more, slots_at, open_at, table_ref, place_ref, *refs):
    refs = list(refs)
    row_refs = [refs.pop(0) for _ in range(4)]
    sources = {"own": [refs.pop(0) for _ in range(3)]}
    for slot in range(X1, Z3 + 1):
        sources[slot] = (refs.pop(0), refs.pop(0))
    old_ref, level_rows_ref, level_ref, open_ref, cube_ref, diag_ref = (refs.pop(0) for _ in range(6))
    block_ref, block_sem, left_ref, left_sem, total_ref, total_sem, out_sem = refs
    half = left_ref.shape[1]
    worker = Worker(table_ref, place_ref[0], half, block_ref, block_sem, left_ref, left_sem, total_ref, total_sem)
    worker.levels = (level_rows_ref, level_ref, diag_ref)
    worker.load_rows(row_refs)
    worker.load_block(0, X3, sources)
    for k in range(4):
        worker.load_total(k, old_ref.at[k])
    worker.load_block(1, Z3, sources)
    worker.run(steps)
    worker.wait_rest(steps)
    done = [
        (total_ref.at[table_ref[open_at + k]], open_ref.at[k]) for k in range(2)
    ]
    copies = copy_all(done, out_sem)
    worker.blocks, worker.lefts, worker.totals = [], [], []
    for k in range(4):
        worker.load_block(2 + k, table_ref[slots_at + k], sources)
    diag_ref[...] = jnp.zeros_like(diag_ref)
    total_ref[4:6] = jnp.zeros_like(total_ref[4:6])
    worker.run(more)
    worker.wait_rest(more)
    copies += copy_all([(total_ref.at[4 + k], cube_ref.at[k]) for k in range(2)], out_sem.at[pl.ds(2, 2)])
    for copy in copies:
        copy.wait()


def late_kernel(steps, more, slots_at, table_ref, place_ref, *refs):
    refs = list(refs)
    row_refs = [refs.pop(0) for _ in range(4)]
    sources = {"own": [refs.pop(0) for _ in range(3)]}
    for slot in range(X1, Z4 + 1):
        sources[slot] = (refs.pop(0), refs.pop(0))
    open_ref, cubes_ref, old_diag_ref, level_rows_ref, level_ref, made_ref, cube_ref, diag_ref = (
        refs.pop(0) for _ in range(8)
    )
    block_ref, block_sem, left_ref, left_sem, total_ref, total_sem, out_sem = refs
    half = left_ref.shape[1]
    core = place_ref[0]
    worker = Worker(table_ref, core, half, block_ref, block_sem, left_ref, left_sem, total_ref, total_sem)
    worker.levels = (level_rows_ref, level_ref, diag_ref)
    worker.load_rows(row_refs)
    worker.load_block(0, X4, sources)
    worker.load_block(1, Z4, sources)
    for k in range(2):
        worker.load_total(k, open_ref.at[k])
    diag_ref[...] = old_diag_ref[...]
    worker.run(steps)
    worker.wait_rest(steps)
    copies = copy_all([(left_ref.at[4 + k], made_ref.at[k]) for k in range(2)], out_sem)
    worker.blocks, worker.lefts, worker.totals = [], [], []
    for k in range(2):
        worker.load_block(2 + k, table_ref[slots_at + k], sources)
    worker.load_total(2, cubes_ref.at[1 - core])
    worker.run(more)
    worker.wait_rest(more)
    cube_ref[...] = total_ref[2].astype(cube_ref.dtype)
    for copy in copies:
        copy.wait()


def own_kernel(steps, slots_at, table_ref, place_ref, *refs):
    refs = list(refs)
    sources = {"own": [refs.pop(0) for _ in range(3)]}
    for slot in range(X1, Z4 + 1):
        sources[slot] = (refs.pop(0), refs.pop(0))
    made_ref, cubes_ref, level_ref, cube_ref = (refs.pop(0) for _ in range(4))
    block_ref, block_sem, left_ref, left_sem, total_ref, total_sem = refs
    half = left_ref.shape[1]
    core = place_ref[0]
    worker = Worker(table_ref, core, half, block_ref, block_sem, left_ref, left_sem, total_ref, total_sem)
    worker.levels = (None, level_ref, None)
    for k in range(2):
        worker.load_left(k, made_ref.at[k])
        worker.load_block(k, table_ref[slots_at + k], sources)
        if k == 0:
            worker.load_total(0, cubes_ref.at[core])
    worker.run(steps)
    worker.wait_rest(steps)
    cube_ref[...] = total_ref[0]


HERE = pl.BlockSpec(memory_space=pl.ANY)
SCALARS = pl.BlockSpec(memory_space=pltpu.SMEM)
VMEM = pl.BlockSpec(memory_space=pltpu.VMEM)
VMEM_BYTES = 60 * 2**20


def work_scratch(half, width, blocks, lefts, totals, outs):
    return [
        pltpu.VMEM((blocks, 2 * half, width), jnp.bfloat16),
        pltpu.SemaphoreType.DMA((blocks, 2)),
        pltpu.VMEM((lefts, half, width), jnp.bfloat16),
        pltpu.SemaphoreType.DMA((lefts,)),
        pltpu.VMEM((totals, half, width), jnp.float32),
        pltpu.SemaphoreType.DMA((totals,)),
    ] + ([pltpu.SemaphoreType.DMA((outs,))] if outs else [])


def call_kernel(name, kernel, scalars, operands, in_vmem, out_shape, out_specs, scratch):
    return pl.pallas_call(
        kernel,
        out_shape=out_shape,
        in_specs=[SCALARS] * len(scalars) + [HERE] * len(operands) + [VMEM] * len(in_vmem),
        out_specs=out_specs,
        scratch_shapes=scratch,
        compiler_params=pltpu.CompilerParams(vmem_limit_bytes=VMEM_BYTES),
        name=name,
    )(*scalars, *operands, *in_vmem)


def pick_kernel(whole_rows, count, choice_ref, *refs):
    sources, refs = refs[:count], refs[count:]
    outs, held_ref, in_sem, out_sem = refs[:-3], refs[-3], refs[-2], refs[-1]
    parts = in_sem.shape[1]
    size = held_ref.shape[1] // parts
    for part in range(parts):
        for k in range(len(outs)):
            to = held_ref.at[k, pl.ds(part * size, size)]
            for number, source in enumerate(sources):
                @pl.when(choice_ref[k] == number)
                def _():
                    first = part * size
                    if number == 0 and whole_rows:
                        first = pl.multiple_of(choice_ref[len(outs)] + first, size)
                    pltpu.make_async_copy(source.at[pl.ds(first, size)], to, in_sem.at[k, part]).start()
    for part in range(parts):
        for k, out_ref in enumerate(outs):
            rows = pl.ds(part * size, size)
            pltpu.make_async_copy(held_ref.at[k, rows], held_ref.at[k, rows], in_sem.at[k, part]).wait()
            pltpu.make_async_copy(held_ref.at[k, rows], out_ref.at[rows], out_sem.at[k, part]).start()
    for part in range(parts):
        for k, out_ref in enumerate(outs):
            rows = pl.ds(part * size, size)
            pltpu.make_async_copy(held_ref.at[k, rows], out_ref.at[rows], out_sem.at[k, part]).wait()


def pick(choices, sources, whole_rows=0, first=None):
    shape, dtype = sources[-1].shape, sources[-1].dtype
    numbers = jnp.stack(list(choices) + ([first] if whole_rows else [])).astype(jnp.int32)
    parts = 4
    return pl.pallas_call(
        functools.partial(pick_kernel, whole_rows, len(sources)),
        out_shape=[jax.ShapeDtypeStruct(shape, dtype)] * len(choices),
        in_specs=[SCALARS] + [HERE] * len(sources),
        out_specs=[HERE] * len(choices),
        scratch_shapes=[
            pltpu.VMEM((len(choices),) + shape, dtype),
            pltpu.SemaphoreType.DMA((len(choices), parts)),
            pltpu.SemaphoreType.DMA((len(choices), parts)),
        ],
        compiler_params=pltpu.CompilerParams(vmem_limit_bytes=VMEM_BYTES),
        name="pick",
    )(numbers, *sources)


def pairs_kernel(spots_ref, points_ref, out_ref, high_ref, low_ref, wide_ref):
    count, total = points_ref.shape[0], spots_ref.shape[1]
    tiles = 4
    for k in range(4):
        wide_ref[k] = jnp.broadcast_to(points_ref[:, k : k + 1], (count, 128))

    def one(index, carry):
        lanes = [pl.ds(pl.multiple_of((index * tiles + m) * 128, 128), 128) for m in range(tiles)]
        spots = [[jnp.broadcast_to(spots_ref[k : k + 1, at], (16, 128)) for k in range(3)] for at in lanes]

        def step(group, sums):
            rows = pl.ds(pl.multiple_of(group * 16, 16), 16)
            px, py, pz, charge = (wide_ref[k, rows, :] for k in range(4))
            sums = list(sums)
            for m, at in enumerate(lanes):
                dx, dy, dz = spots[m][0] - px, spots[m][1] - py, spots[m][2] - pz
                inv = lax.rsqrt(dx * dx + dy * dy + dz * dz + 1.0)
                sums[m] = sums[m] + charge * inv
                weight = inv * (inv * inv)
                high = weight.astype(jnp.bfloat16)
                high_ref[rows, at] = high
                low_ref[rows, at] = (weight - high.astype(jnp.float32)).astype(jnp.bfloat16)
            return tuple(sums)

        zeros = tuple(jnp.zeros((16, 128), jnp.float32) for _ in range(tiles))
        sums = lax.fori_loop(0, count // 16, step, zeros, unroll=2)
        for m, at in enumerate(lanes):
            out_ref[:, at] = jnp.sum(sums[m], 0, keepdims=True)
        return carry

    lax.fori_loop(0, total // (128 * tiles), one, 0)


def pair_terms(centers, points):
    total, count = centers.shape[1], points.shape[0]
    part = jax.ShapeDtypeStruct((count, total), jnp.bfloat16)
    return pl.pallas_call(
        pairs_kernel,
        out_shape=(jax.ShapeDtypeStruct((1, total), jnp.float32), part, part),
        scratch_shapes=[pltpu.VMEM((4, count, 128), jnp.float32)],
        compiler_params=pltpu.CompilerParams(vmem_limit_bytes=VMEM_BYTES),
        name="pairs",
    )(centers, points)


MIDDLE = 10.0


def pull_kernel(spots_ref, occ_ref, high_ref, low_ref, coords_ref, charge_ref, out_ref, total_ref):
    index = pl.program_id(0)
    occ = occ_ref[...]
    weights = [occ] + [occ * (spots_ref[k : k + 1, :] - MIDDLE) for k in range(3)]
    width = occ.shape[1]
    stacked = jnp.concatenate(weights + [jnp.zeros((4, width), jnp.float32)], 0)
    high = stacked.astype(jnp.bfloat16)
    low = (stacked - high.astype(jnp.float32)).astype(jnp.bfloat16)
    blank = jnp.zeros((128 - 16, width), jnp.bfloat16)
    both = jnp.concatenate([high, low, blank], 0)
    first = jnp.concatenate([high, jnp.zeros_like(low), blank], 0)
    dims = (((1,), (1,)), ((), ()))
    part = lax.dot_general(high_ref[...], both, dims, preferred_element_type=jnp.float32)
    part = part + lax.dot_general(low_ref[...], first, dims, preferred_element_type=jnp.float32)

    @pl.when(index == 0)
    def _():
        total_ref[...] = part

    @pl.when(index > 0)
    def _():
        total_ref[...] += part

    @pl.when(index == pl.num_programs(0) - 1)
    def _():
        sums = total_ref[...].T
        sums = sums[0:8] + sums[8:16]
        for k in range(3):
            pull = (coords_ref[k : k + 1, :] - MIDDLE) * sums[0:1] - sums[k + 1 : k + 2]
            out_ref[k : k + 1, :] = -charge_ref[...] * pull


def pull_terms(centers, occupation, high, low, mm_coords, mm_charges):
    total, count = centers.shape[1], mm_coords.shape[1]
    width = 1024
    return pl.pallas_call(
        pull_kernel,
        grid=(total // width,),
        out_shape=jax.ShapeDtypeStruct((3, count), jnp.float32),
        in_specs=[
            pl.BlockSpec((3, width), lambda i: (0, i)),
            pl.BlockSpec((1, width), lambda i: (0, i)),
            pl.BlockSpec((count, width), lambda i: (0, i)),
            pl.BlockSpec((count, width), lambda i: (0, i)),
            pl.BlockSpec((3, count), lambda i: (0, 0)),
            pl.BlockSpec((1, count), lambda i: (0, 0)),
        ],
        out_specs=pl.BlockSpec((3, count), lambda i: (0, 0)),
        scratch_shapes=[pltpu.VMEM((count, 128), jnp.float32)],
        name="pull",
    )(centers, occupation, high, low, mm_coords, mm_charges[None])


def density_kernel(steps, place_ref, gain_ref, ham_ref, near_ref, far_ref, level_ref, out_ref):
    index = pl.program_id(0)
    core, row, col = place_ref[0], place_ref[1], place_ref[2]
    gain = gain_ref[0]
    height, width = out_ref.shape
    chunk = 16
    linear, cubic = -1.5 * gain, 2.0 * (gain * gain * gain)

    def pass_rows(cube_ref, with_diag):
        def one(k, carry):
            rows = pl.ds(pl.multiple_of(k * chunk, chunk), chunk)
            value = linear * ham_ref[rows, :].astype(jnp.float32) + cubic * cube_ref[rows, :].astype(jnp.float32)
            if with_diag:
                own = lax.broadcasted_iota(jnp.int32, (chunk, width), 0) + (index * height + k * chunk)
                on_diag = own == lax.broadcasted_iota(jnp.int32, (chunk, width), 1)
                value = value + jnp.where(on_diag, 0.5 + linear * level_ref[...], 0.0)
            out_ref[rows, :] = value
            return carry

        lax.fori_loop(0, height // chunk, one, 0, unroll=2)

    in_near = lax.div(index, jnp.int32(steps)) == core
    holds_diag = row == 2 * col + core
    for cube_ref, here in ((near_ref, in_near), (far_ref, jnp.logical_not(in_near))):
        for with_diag, diag_here in ((True, holds_diag), (False, jnp.logical_not(holds_diag))):
            pl.when(jnp.logical_and(here, diag_here))(functools.partial(pass_rows, cube_ref, with_diag))


def density_block(place, gain, ham, near, far, level_cols):
    height, width = ham.shape
    chunk = 320
    steps = near.shape[0] // chunk
    part = pl.BlockSpec((chunk, width), lambda i: (lax.rem(i, steps), 0))
    return pl.pallas_call(
        functools.partial(density_kernel, steps),
        grid=(height // chunk,),
        out_shape=jax.ShapeDtypeStruct((height, width), jnp.float32),
        in_specs=[SCALARS, SCALARS, pl.BlockSpec((chunk, width), lambda i: (i, 0)), part, part]
        + [pl.BlockSpec((1, width), lambda i: (0, 0))],
        out_specs=pl.BlockSpec((chunk, width), lambda i: (i, 0)),
        name="density",
    )(place, gain, ham, near, far, level_cols)


def gossip_shards(sizes, h_core, centers, mm_coords, mm_charges):
    height, width = h_core.shape
    half = height // 2
    total, count = centers.shape[1], mm_coords.shape[1]
    row, col, core = (lax.axis_index(name) for name in ("sec", "col", "rep"))
    row_start = row * height
    col_start = (2 * col + core) * width
    rows, steps, slots_at, open_at = device_tables()
    table = lax.dynamic_index_in_dim(jnp.asarray(rows, jnp.int32), 4 * row + 2 * col + core, 0, keepdims=False)
    place = jnp.stack([core, row, col]).astype(jnp.int32)

    def of_row(values):
        return lax.dynamic_index_in_dim(jnp.asarray(values, jnp.int32), row, 0, keepdims=False)

    def over_rep(value):
        return lax.ppermute(value, "rep", [(0, 1), (1, 0)])

    def over_col(value):
        return lax.ppermute(value, "col", [(0, 1), (1, 0)])

    def over_sec(value, step):
        moves = [(2 * start + x, 2 * to + x) for x in range(2) for start, to in Z_MOVES[step][x]]
        return lax.ppermute(value, ("sec", "col"), moves)

    def swap_all(values):
        return [(value, over_rep(value)) for value in values]

    def flat(groups):
        return [value for group in groups for value in group]

    def after(arrived, work):
        return lax.optimization_barrier((arrived, work))

    def own_source(slot):
        return (slot != core).astype(jnp.int32)

    far = lax.dynamic_slice_in_dim(h_core, (1 - core) * half, half, 0)
    got = over_rep(far)
    x_first, z_first = of_row(X_SENDS[0]), of_row(Z_SENDS[0])
    sends = pick(
        (own_source(x_first), own_source(z_first), own_source(1 - x_first), jnp.int32(0)),
        (h_core, got), half, core * half,
    )
    x1 = over_col(sends[0])
    z1 = over_sec(sends[1], 0)
    x_second, near = sends[2], sends[3]
    other = over_rep(near)
    points = jnp.concatenate([mm_coords, mm_charges[None]], 0).T
    terms, high, low = pair_terms(centers, points)
    rows_glob = row_start + lax.broadcasted_iota(jnp.int32, (height, width), 0)
    cols_glob = col_start + lax.broadcasted_iota(jnp.int32, (height, width), 1)
    on_diag = rows_glob == cols_glob
    wide = h_core.astype(jnp.float32)
    own_diag = jnp.sum(jnp.where(on_diag, wide, 0.0), 0)
    own_off = jnp.sum(jnp.where(on_diag, 0.0, wide * wide))
    diag = lax.dynamic_update_slice_in_dim(jnp.zeros((total,), jnp.float32), own_diag, col_start, 0)
    packed = jnp.concatenate([terms[0], diag, jnp.full((128,), own_off)])
    packed = packed + over_rep(packed)
    (x1, z1), (packed, high, low, x_second, other, table) = after(
        (x1, z1), (packed, high, low, x_second, other, table)
    )
    z_second = of_row(Z_SENDS[1])
    source = jnp.where(z_second == X1, 2, own_source(z_second))
    z2 = over_sec(pick((source,), (near, got, x1))[0], 1)
    x2 = over_col(x_second)
    own_parts = (h_core, got, other)
    pairs = dict(zip((X1, Z1), swap_all((x1, z1))))
    shape = (half, width)

    def grow_square(stage, lefts, slots, old):
        operands = list(lefts) + list(own_parts) + flat(pairs[slot] for slot in slots) + ([] if old is None else [old])
        kernel = functools.partial(square_kernel, old is None, steps[stage], len(lefts), (OWN0, OWN1) + slots, True)
        return call_kernel(
            f"square_{stage}", kernel, (table, place), operands, (),
            jax.ShapeDtypeStruct((4,) + shape, jnp.float32), HERE,
            work_scratch(half, width, 2 + len(slots), 4, 4, 4),
        )

    lefts = [near, got, x1]
    square = grow_square(0, lefts, (X1, Z1), None)
    col_packed = over_col(packed)
    (x2, z2, col_packed), (square, packed) = after((x2, z2, col_packed), (square, packed))
    x3 = over_col(z2)
    z3 = over_sec(x2, 2)
    pairs.update(zip((X2, Z2), swap_all((x2, z2))))
    lefts.append(x2)
    square = grow_square(1, lefts, (X1, Z1, X2, Z2), square)
    packed = packed + col_packed
    others = [lax.ppermute(packed, "sec", [(i, (i + hop) % 4) for i in range(4)]) for hop in (1, 2, 3)]
    (x3, z3, others), (square, packed) = after((x3, z3, others), (square, packed))
    source = (of_row(X_SENDS[3]) == Z3).astype(jnp.int32)
    last_send = pick((source,), (z1, z3))[0]
    x4 = over_col(last_send)
    z4 = over_sec(last_send, 3)
    pairs.update(zip((X3, Z3), swap_all((x3, z3))))
    sums = packed + others[0] + others[1] + others[2]
    potential, diag, off_total = sums[:total], sums[total : 2 * total], sums[2 * total]
    diag_vals = potential + diag
    mean_level = jnp.sum(diag_vals) / total
    above = diag_vals - mean_level
    level = potential - mean_level
    spread = jnp.sqrt((off_total + jnp.sum(above * above)) / total + 1e-05)
    gain = 1.0 / (3.0 * spread)
    level_rows = lax.dynamic_slice_in_dim(level, row_start + core * half, half, 0)[:, None]
    level_cols = lax.dynamic_slice_in_dim(level, col_start, width, 0)[None]
    open_square, cubes, cube_diag = call_kernel(
        "early_cube", functools.partial(early_kernel, steps[2], steps[3], slots_at[0], open_at), (table, place),
        lefts + list(own_parts) + flat(pairs[slot] for slot in range(X1, Z3 + 1)) + [square],
        (level_rows, level[None]),
        (
            jax.ShapeDtypeStruct((2,) + shape, jnp.float32),
            jax.ShapeDtypeStruct((2,) + shape, jnp.float32),
            jax.ShapeDtypeStruct((half, 1), jnp.float32),
        ),
        (HERE, HERE, VMEM), work_scratch(half, width, 6, 6, 6, 4),
    )
    (x4, z4), (open_square, cubes, cube_diag, above, level_rows, level, level_cols, gain) = after(
        (x4, z4), (open_square, cubes, cube_diag, above, level_rows, level, level_cols, gain)
    )
    pairs.update(zip((X4, Z4), swap_all((x4, z4))))
    blocks = list(own_parts) + flat(pairs[slot] for slot in range(X1, Z4 + 1))
    made, sibling, cube_diag = call_kernel(
        "late_cube", functools.partial(late_kernel, steps[4], steps[5], slots_at[1]), (table, place),
        lefts + blocks + [open_square, cubes], (cube_diag, level_rows, level[None]),
        (
            jax.ShapeDtypeStruct((2,) + shape, jnp.bfloat16),
            jax.ShapeDtypeStruct(shape, jnp.bfloat16),
            jax.ShapeDtypeStruct((half, 1), jnp.float32),
        ),
        (HERE, VMEM, VMEM), work_scratch(half, width, 4, 6, 3, 2),
    )
    sibling = over_rep(sibling)
    cube_diag = lax.dynamic_update_slice_in_dim(
        jnp.zeros((total,), jnp.float32), cube_diag[:, 0], row_start + core * half, 0
    )
    cube_diag = butterfly_sum(cube_diag, sizes, ("rep", "sec"))
    mine = call_kernel(
        "own_cube", functools.partial(own_kernel, steps[6], slots_at[2]), (table, place),
        blocks + [made, cubes], (level[None],), jax.ShapeDtypeStruct(shape, jnp.float32), VMEM,
        work_scratch(half, width, 2, 2, 1, 0),
    )
    density = density_block(place, gain[None], h_core, mine, sibling, level_cols)
    occupation = 0.5 - 1.5 * gain * above + 2.0 * gain**3 * cube_diag
    forces = pull_terms(centers, occupation[None], high, low, mm_coords, mm_charges)
    return (density, forces)


def solution(mesh):
    in_specs = (
        P(("groups", "sec"), ("col", "rep")),
        P(None, "groups"),
        P(None, ("groups", "sec", "col", "rep")),
        P(("groups", "sec", "col", "rep")),
    )
    out_specs = (P(("groups", "sec"), ("col", "rep")), P(None, ("groups", "sec", "col", "rep")))
    sizes = dict(mesh.shape)
    small = (sizes["sec"], sizes["col"], sizes["rep"]) == (4, 2, 2)
    body = functools.partial(gossip_shards if small else gather_shards, sizes)
    return jax.shard_map(body, mesh=mesh, in_specs=in_specs, out_specs=out_specs, check_vma=False)
```

```python
import functools

import jax
import jax.numpy as jnp
from jax import lax
from jax.experimental import pallas as pl
from jax.experimental.pallas import tpu as pltpu
from jax.sharding import PartitionSpec as P

PART = ("sec", "col", "rep")


def potential_kernel(spots_ref, points_ref, out_ref):
    count = points_ref.shape[0]
    width = spots_ref.shape[1]
    sx, sy, sz = (spots_ref[k : k + 1, :] for k in range(3))

    def step(index, accum):
        rows = points_ref[pl.ds(pl.multiple_of(index * 8, 8), 8), :]
        dx = sx - rows[:, 0:1]
        dy = sy - rows[:, 1:2]
        dz = sz - rows[:, 2:3]
        dist = dx * dx + dy * dy + dz * dz + 1.0
        return accum + rows[:, 3:4] * lax.rsqrt(dist)

    total = lax.fori_loop(0, count // 8, step, jnp.zeros((8, width), jnp.float32), unroll=4)
    out_ref[...] = jnp.sum(total, 0, keepdims=True)


def potential_terms(centers, mm_coords, mm_charges):
    total = centers.shape[1]
    count = mm_coords.shape[1]
    width = 1024 if total % 1024 == 0 else total
    points = jnp.concatenate([mm_coords, mm_charges[None]], 0).T
    return pl.pallas_call(
        potential_kernel,
        grid=(total // width,),
        out_shape=jax.ShapeDtypeStruct((1, total), jnp.float32),
        in_specs=[
            pl.BlockSpec((3, width), lambda i: (0, i)),
            pl.BlockSpec((count, 4), lambda i: (0, 0)),
        ],
        out_specs=pl.BlockSpec((1, width), lambda i: (0, i)),
        name="potential",
    )(centers, points)


def force_kernel(spots_ref, occ_ref, points_ref, out_ref):
    total = spots_ref.shape[1]
    rows = points_ref[...]
    px, py, pz, charge = (rows[:, k : k + 1] for k in range(4))
    count = rows.shape[0]

    def step(index, accum):
        lanes = pl.ds(pl.multiple_of(index * 128, 128), 128)
        dx = px - spots_ref[0:1, lanes]
        dy = py - spots_ref[1:2, lanes]
        dz = pz - spots_ref[2:3, lanes]
        inv = lax.rsqrt(dx * dx + dy * dy + dz * dz + 1.0)
        weight = occ_ref[:, lanes] * inv * (inv * inv)
        return (accum[0] + dx * weight, accum[1] + dy * weight, accum[2] + dz * weight)

    zero = jnp.zeros((count, 128), jnp.float32)
    sums = lax.fori_loop(0, total // 128, step, (zero, zero, zero), unroll=4)
    for k in range(3):
        out_ref[:, k : k + 1] = -charge * jnp.sum(sums[k], 1, keepdims=True)


def force_terms(centers, occupation, mm_coords, mm_charges):
    total = centers.shape[1]
    count = mm_coords.shape[1]
    width = 32
    points = jnp.concatenate([mm_coords, mm_charges[None]], 0).T
    summed = pl.pallas_call(
        force_kernel,
        grid=(count // width,),
        out_shape=jax.ShapeDtypeStruct((count, 4), jnp.float32),
        in_specs=[
            pl.BlockSpec((3, total), lambda i: (0, 0)),
            pl.BlockSpec((1, total), lambda i: (0, 0)),
            pl.BlockSpec((width, 4), lambda i: (i, 0)),
        ],
        out_specs=pl.BlockSpec((width, 4), lambda i: (i, 0)),
        name="forces",
    )(centers, occupation, points)
    return summed[:, :3].T


def butterfly_sum(value, sizes, axes=("rep", "col", "sec")):
    for axis in axes:
        size = sizes[axis]
        if size & (size - 1):
            value = lax.psum(value, axis)
            continue
        hop = 1
        while hop < size:
            value = value + lax.ppermute(value, axis, [(i, i ^ hop) for i in range(size)])
            hop *= 2
    return value


def fold_with(left, piece):
    return jnp.dot(left, piece, preferred_element_type=jnp.float32)


def gather_shards(sizes, h_core, centers, mm_coords, mm_charges):
    row_count, col_count = h_core.shape
    total = centers.shape[1]
    row_start = lax.axis_index("sec") * row_count
    col_start = lax.axis_index(("col", "rep")) * col_count
    rows_glob = row_start + lax.broadcasted_iota(jnp.int32, (row_count, col_count), 0)
    cols_glob = col_start + lax.broadcasted_iota(jnp.int32, (row_count, col_count), 1)
    on_diag = rows_glob == cols_glob
    off = jnp.where(on_diag, jnp.zeros((), h_core.dtype), h_core)
    row_panel = lax.all_gather(off, ("col", "rep"), axis=1, tiled=True)
    col_panel = lax.all_gather(off, "sec", axis=0, tiled=True)

    wide = h_core.astype(jnp.float32)
    own_diag = jnp.sum(jnp.where(on_diag, wide, 0.0), 0)
    own_off = jnp.sum(jnp.where(on_diag, 0.0, wide * wide))
    terms = potential_terms(centers, mm_coords, mm_charges)[0]
    own_cols = lax.dynamic_slice_in_dim(terms, col_start, col_count, 0) + own_diag
    terms = lax.dynamic_update_slice_in_dim(terms, own_cols, col_start, 0)
    sums = butterfly_sum(jnp.concatenate([terms, jnp.full((128,), own_off)]), sizes)
    diag_vals, off_total = sums[:total], sums[total]
    mean_level = jnp.sum(diag_vals) / total
    level = diag_vals - mean_level
    spread = jnp.sqrt((off_total + jnp.sum(level * level)) / total + 1e-05)
    gain = 1.0 / (3.0 * spread)

    level_rows = lax.dynamic_slice_in_dim(level, row_start, row_count, 0)[:, None]
    level_cols = lax.dynamic_slice_in_dim(level, col_start, col_count, 0)[None, :]
    off_wide = off.astype(jnp.float32)
    square = fold_with(row_panel, col_panel)
    square = square + off_wide * (level_rows + level_cols) + jnp.where(on_diag, level_rows * level_rows, 0.0)
    shifted = off_wide + jnp.where(on_diag, level_rows, 0.0)
    square_b = square.astype(jnp.bfloat16)
    square_panel = lax.all_gather(square_b, ("col", "rep"), axis=1, tiled=True)
    own_cube = jnp.sum(square * shifted, 0)
    cube_diag = lax.dynamic_update_slice_in_dim(jnp.zeros((total,), jnp.float32), own_cube, col_start, 0)
    cube_diag = butterfly_sum(cube_diag, sizes)
    occupation = 0.5 - 1.5 * gain * level + 2.0 * gain**3 * cube_diag
    forces = force_terms(centers, occupation[None], mm_coords, mm_charges)

    cube = fold_with(square_panel, col_panel) + square_b.astype(jnp.float32) * level_cols
    density = jnp.where(on_diag, 0.5, 0.0) - 1.5 * gain * shifted + 2.0 * gain**3 * cube
    return (density, forces)


ROUND = ((0, 1), (1, 2), (2, 3), (3, 0))
BACK = ((0, 3), (3, 2), (2, 1), (1, 0))
Z_MOVES = ((ROUND, BACK), (BACK, ROUND), (ROUND, BACK), (ROUND, BACK))
OWN0, OWN1, X1, Z1, X2, Z2, X3, Z3, X4, Z4 = range(10)
X_SENDS = ((OWN1, OWN0, OWN1, OWN0), (OWN0, OWN1, OWN0, OWN1), (Z2,) * 4, (Z3, Z1, Z1, Z3))
Z_SENDS = ((OWN0, OWN1, OWN0, OWN1), (OWN1, X1, X1, OWN0), (X2,) * 4, (Z3, Z1, Z1, Z3))
SLOT_STAGE = (0, 0, 0, 0, 1, 1, 2, 2, 3, 3)
LEFT_SLOTS = (OWN0, OWN1, X1, X2)
LEFT_STAGE = (0, 0, 0, 1)
FIELDS = 10
NOTHING, MULTIPLY, FINISH, LEVEL, SEND, ZERO = range(6)
BLOCK_BIT, LEFT_BIT = 0, 8


def block_places():
    chips = [(z, x) for z in range(4) for x in range(2)]
    held = {(z, x): [(z, 2 * x), (z, 2 * x + 1)] for z, x in chips}
    for step in range(4):
        arrived = {}
        for z, x in chips:
            before = next(start for start, to in Z_MOVES[step][x] if to == z)
            arrived[(z, x)] = [held[(z, 1 - x)][X_SENDS[step][z]], held[(before, x)][Z_SENDS[step][before]]]
        for chip in chips:
            held[chip] = held[chip] + arrived[chip]
    return [held[chip] for chip in chips]


def rows_of(products, length, lefts, ahead):
    seen, firsts = set(), []
    for kind, left, block, flip, total, column in products:
        bits = []
        if kind in (MULTIPLY, FINISH, LEVEL):
            loaded_left = block if kind == FINISH else left
            if loaded_left in lefts:
                bits.append(LEFT_BIT + loaded_left)
        if kind == MULTIPLY:
            bits.append(BLOCK_BIT + block)
        firsts.append([bit for bit in dict.fromkeys(bits) if bit not in seen])
        seen.update(bits)
    mask = lambda bits: sum(1 << bit for bit in bits)
    waves = [k for k, first in enumerate(firsts) if first]
    starts = [[] for _ in products]
    for number, k in enumerate(waves):
        at = 0 if number <= ahead else waves[number - ahead]
        starts[at] += firsts[k]
    rows = []
    for k, (kind, left, block, flip, total, column) in enumerate(products):
        rows.append([kind, left, block, flip, total, mask(firsts[k]), column, mask(starts[k]), 0, 0])
    return rows + [[NOTHING] + [0] * (FIELDS - 1)] * (length - len(rows))


def device_lists():
    devices = []
    for chip, slots in enumerate(block_places()):
        assert len({tuple(sorted(place)) for place in slots}) == 10
        row, col = divmod(chip, 2)
        assert all(slots[s][0] == row for s in LEFT_SLOTS)
        lefts = [slots[s][1] for s in LEFT_SLOTS]
        stages = [[], [], [], []]
        for slot, (first, second) in enumerate(slots):
            for inner, outer, flip in [(first, second, 0), (second, first, 1)][: 1 if first == second else 2]:
                left = lefts.index(inner)
                stage = max(LEFT_STAGE[left], SLOT_STAGE[slot])
                base = (0, 0, X3, X4)[stage]
                key = max(slot, LEFT_SLOTS[left])
                stages[stage].append((key, (MULTIPLY, left, slot - base, flip, outer, 0)))
        stages = [[product for _, product in sorted(stage)] for stage in stages]
        first, touched = [], set()
        for product in stages[0]:
            if product[4] not in touched:
                first.append((ZERO, 0, 0, 0, product[4], 0))
            touched.add(product[4])
            first.append(product)
        first += [(ZERO, 0, 0, 0, total, 0) for total in range(4) if total not in touched]
        open_columns = sorted({product[4] for product in stages[3]})
        done_columns = [column for column in range(4) if column not in open_columns]
        assert len(open_columns) == 2

        def find(inner, outer):
            if (inner, outer) in slots:
                return slots.index((inner, outer)), 0
            return slots.index((outer, inner)), 1

        for core in range(2):
            early, early_slots = list(stages[2]), []
            early += [(ZERO, 0, 0, 0, 4 + which, 0) for which in range(2)]
            for k, column in enumerate(done_columns):
                early.append((FINISH, 4 + k, lefts.index(column), int(column == row), column, column))
            for which in range(2):
                for k, column in enumerate(done_columns):
                    slot, flip = find(column, 2 * col + which)
                    early.append((MULTIPLY, 4 + k, 2 + len(early_slots), flip, 4 + which, 0))
                    early_slots.append(slot)
                    if column == 2 * col + which:
                        early.append((LEVEL, 4 + k, 0, 0, 4 + which, column))
            late, late_slots = [], []
            for product in stages[3]:
                left = open_columns.index(lefts[product[1]])
                late.append((MULTIPLY, left) + product[2:])
            for k, column in enumerate(open_columns):
                late.append((FINISH, 2 + k, k, int(column == row), column, column))
            for k, which in enumerate((1 - core, core)):
                for m, column in enumerate(open_columns):
                    slot, flip = find(column, 2 * col + which)
                    late.append((MULTIPLY, 2 + m, 2 + len(late_slots), flip, 4 + which, 0))
                    late_slots.append(slot)
                    if column == 2 * col + which:
                        late.append((LEVEL, 2 + m, 0, 0, 4 + which, column))
                if k == 0:
                    late.append((SEND, 0, 0, 0, 4 + which, 0))
            own_rows = lambda slot: int(slot != core)
            second = Z_SENDS[1][row]
            info = [
                core, row, col, core * 640,
                own_rows(X_SENDS[0][row]), own_rows(Z_SENDS[0][row]), own_rows(X_SENDS[1][row]), 0,
                2 if second == X1 else own_rows(second), int(X_SENDS[3][row] == Z3),
            ] + [lefts.index(column) for column in open_columns] + open_columns
            devices.append(
                dict(
                    kernels=[first, stages[1], early, late],
                    slots=[early_slots, late_slots],
                    info=info,
                )
            )
    return devices


CORE, ROW, COL, FIRST_ROW, SEND_X1, SEND_Z1, SEND_X2, NEAR, SEND_Z2, SEND_LAST, OPEN_LEFT, OPEN = (*range(11), 12)


def device_tables(half):
    devices = device_lists()
    steps, rows = [], [[] for _ in devices]
    for kernel, (lefts, ahead) in enumerate((((0, 1, 2), 2), (range(4), 2), (range(4), 2), ((0, 1), 1))):
        length = max(len(device["kernels"][kernel]) for device in devices)
        steps.append((len(rows[0]), length))
        for row, device in zip(rows, devices):
            for fields in rows_of(device["kernels"][kernel], length, lefts, ahead):
                row += fields
    slots = []
    for kernel in range(2):
        slots.append(len(rows[0]))
        for row, device in zip(rows, devices):
            row += device["slots"][kernel]
    for device in devices:
        device["info"][FIRST_ROW] = device["info"][CORE] * half
    return [device["info"] for device in devices], rows, steps, slots


def bit_set(mask, bit):
    return jnp.bitwise_and(mask, jnp.int32(1 << bit)) != 0


class Worker:
    def __init__(self, table_ref, core, half, block_ref, block_sem, left_ref, left_sem, total_ref):
        self.table_ref, self.core, self.half = table_ref, core, half
        self.block_ref, self.block_sem = block_ref, block_sem
        self.left_ref, self.left_sem = left_ref, left_sem
        self.total_ref = total_ref
        self.near = pl.ds(pl.multiple_of(core * half, half), half)
        self.far = pl.ds(pl.multiple_of((1 - core) * half, half), half)
        self.blocks, self.lefts, self.send = {}, {}, None
        self.levels = None

    def load_halves(self, position, near_ref, far_ref):
        pltpu.make_async_copy(near_ref, self.block_ref.at[position, self.near], self.block_sem.at[position, 0]).start()
        pltpu.make_async_copy(far_ref, self.block_ref.at[position, self.far], self.block_sem.at[position, 1]).start()

    def load_block(self, position, slot, sources):
        self.blocks[position] = functools.partial(self.start_block, position, slot, sources)

    def start_block(self, position, slot, sources):
        fixed = isinstance(slot, int)
        if "own" in sources and (not fixed or slot <= OWN1):
            for at, ref in zip((self.core, 1 - self.core), sources["own"]):
                @pl.when(slot == at)
                def _():
                    self.load_halves(position, ref.at[self.near], ref.at[self.far])

        if not fixed:
            for number, halves in sources.items():
                if number != "own":
                    pl.when(slot == number)(functools.partial(self.load_halves, position, *halves))
        elif slot > OWN1:
            self.load_halves(position, *sources[slot])

    def left_places(self, refs):
        own = [(self.core, refs[0].at[self.near]), (1 - self.core, refs[1].at[self.near])]
        return own + list(enumerate(refs))[2:]

    def load_left(self, index, number, refs):
        self.lefts[index] = functools.partial(self.start_left, index, number, refs)

    def start_left(self, index, number, refs):
        for at, ref in self.left_places(refs):
            if isinstance(at, int) and isinstance(number, int):
                if at == number:
                    self.copy_left(index, ref)
            else:
                pl.when(at == number)(functools.partial(self.copy_left, index, ref))

    def copy_left(self, index, ref):
        pltpu.make_async_copy(ref, self.left_ref.at[index], self.left_sem.at[index]).start()

    def load_rows(self, refs):
        for k in range(len(refs)):
            self.load_left(k, k, refs)

    def start(self, mask):
        for base, loads in ((LEFT_BIT, self.lefts), (BLOCK_BIT, self.blocks)):
            for index, load in loads.items():
                pl.when(bit_set(mask, base + index))(load)

    def wait(self, mask):
        half_block = self.block_ref.at[0, pl.ds(0, self.half)]
        for position in self.blocks:
            @pl.when(bit_set(mask, BLOCK_BIT + position))
            def _():
                for part in range(2):
                    pltpu.make_async_copy(half_block, half_block, self.block_sem.at[position, part]).wait()
        for index in self.lefts:
            @pl.when(bit_set(mask, LEFT_BIT + index))
            def _():
                pltpu.make_async_copy(self.left_ref.at[0], self.left_ref.at[0], self.left_sem.at[index]).wait()

    def multiply(self, field):
        total, left, block = self.total_ref.at[field[4]], self.left_ref.at[field[1]], self.block_ref.at[field[2]]

        @pl.when(field[3] == 0)
        def _():
            total[...] += jnp.dot(left[...], block[...], preferred_element_type=jnp.float32)

        @pl.when(field[3] == 1)
        def _():
            total[...] += lax.dot_general(
                left[...], block[...], (((1,), (1,)), ((), ())), preferred_element_type=jnp.float32
            )

    def tiles(self, cols_ref, column):
        width = self.block_ref.shape[2]
        base = column * width
        return [
            jnp.broadcast_to(cols_ref[:, pl.ds(pl.multiple_of(base + m * 128, 128), 128)], (16, 128))
            for m in range(width // 128)
        ]

    def finish(self, field):
        rows_ref, cols_ref, diag_ref = self.levels
        half = self.half
        total, left, made = self.total_ref.at[field[4]], self.left_ref.at[field[2]], self.left_ref.at[field[1]]
        cols = self.tiles(cols_ref, field[6])

        def one(index, carry):
            rows = pl.ds(pl.multiple_of(index * 16, 16), 16)
            level = rows_ref[rows, :]
            share = jnp.zeros((16, 128), jnp.float32)
            for m, col in enumerate(cols):
                at = slice(m * 128, (m + 1) * 128)
                ham = left[rows, at].astype(jnp.float32)
                square = total[rows, at] + ham * (level + col)
                made[rows, at] = square.astype(jnp.bfloat16)
                share = share + square * ham
            diag_ref[rows, :] += share
            return carry

        lax.fori_loop(0, half // 16, one, 0, unroll=2)

        @pl.when(field[3] == 1)
        def _():
            eye = lax.broadcasted_iota(jnp.int32, (128, 128), 0) == lax.broadcasted_iota(jnp.int32, (128, 128), 1)

            def fix(index, carry):
                rows = pl.ds(pl.multiple_of(index * 128, 128), 128)
                at = pl.ds(pl.multiple_of(self.core * half + index * 128, 128), 128)
                col = cols_ref[:, pl.ds(pl.multiple_of(field[6] * (2 * half) + self.core * half + index * 128, 128), 128)]
                level = rows_ref[rows, :]
                ham = left[rows, at].astype(jnp.float32)
                square = total[rows, at] + ham * (level + col)
                full = square + jnp.where(eye, level * level, 0.0)
                made[rows, at] = full.astype(jnp.bfloat16)
                diag_ref[rows, :] += jnp.where(eye, full * (ham + level) - square * ham, 0.0)
                return carry

            lax.fori_loop(0, half // 128, fix, 0)

    def add_level(self, field):
        cols = self.tiles(self.levels[1], field[6])
        total, left = self.total_ref.at[field[4]], self.left_ref.at[field[1]]

        def one(index, carry):
            rows = pl.ds(pl.multiple_of(index * 16, 16), 16)
            for m, col in enumerate(cols):
                at = slice(m * 128, (m + 1) * 128)
                total[rows, at] += left[rows, at].astype(jnp.float32) * col
            return carry

        lax.fori_loop(0, self.half // 16, one, 0, unroll=2)

    def clear(self, field):
        self.total_ref[field[4]] = jnp.zeros_like(self.total_ref[0])

    def run(self, start_count):
        start, count = start_count
        works = [(MULTIPLY, self.multiply), (ZERO, self.clear)]
        if self.levels is not None:
            works += [(FINISH, self.finish), (LEVEL, self.add_level)]
        if self.send is not None:
            works.append((SEND, self.send))

        def step(index, carry):
            field = [self.table_ref[start + index * FIELDS + k] for k in range(8)]
            pl.when(field[7] != 0)(functools.partial(self.start, field[7]))
            pl.when(field[5] != 0)(functools.partial(self.wait, field[5]))
            for kind, work in works:
                pl.when(field[0] == kind)(functools.partial(work, field))
            return carry

        lax.fori_loop(0, count, step, 0)


def square_kernel(first, steps, left_count, slots, table_ref, info_ref, *refs):
    refs = list(refs)
    row_refs = [refs.pop(0) for _ in range(left_count)]
    sources = {"own": [refs.pop(0) for _ in range(2)]}
    for slot in slots:
        if slot > OWN1:
            sources[slot] = (refs.pop(0), refs.pop(0))
    refs = refs[0 if first else 2 :]
    total_ref, token_ref, block_ref, block_sem, left_ref, left_sem = refs
    half = left_ref.shape[1]
    worker = Worker(table_ref, info_ref[CORE], half, block_ref, block_sem, left_ref, left_sem, total_ref)
    worker.load_rows(row_refs)
    for position, slot in enumerate(slots):
        worker.load_block(position, slot, sources)
    worker.run(steps)
    token_ref[...] = jnp.zeros_like(token_ref)


def early_kernel(steps, slots_at, table_ref, info_ref, *refs):
    refs = list(refs)
    row_refs = [refs.pop(0) for _ in range(4)]
    sources = {"own": [refs.pop(0) for _ in range(2)]}
    for slot in range(X1, Z3 + 1):
        sources[slot] = (refs.pop(0), refs.pop(0))
    _, _, level_rows_ref, level_ref, total_ref, diag_ref = (refs.pop(0) for _ in range(6))
    block_ref, block_sem, left_ref, left_sem = refs
    half = left_ref.shape[1]
    worker = Worker(table_ref, info_ref[CORE], half, block_ref, block_sem, left_ref, left_sem, total_ref)
    worker.levels = (level_rows_ref, level_ref, diag_ref)
    worker.load_rows(row_refs)
    worker.load_block(0, X3, sources)
    worker.load_block(1, Z3, sources)
    for k in range(4):
        worker.load_block(2 + k, table_ref[slots_at + k], sources)
    diag_ref[...] = jnp.zeros_like(diag_ref)
    worker.run(steps)


def late_kernel(steps, slots_at, table_ref, info_ref, gain_ref, *refs):
    refs = list(refs)
    row_refs = [refs.pop(0) for _ in range(4)]
    sources = {"own": [refs.pop(0) for _ in range(2)]}
    for slot in range(X1, Z4 + 1):
        sources[slot] = (refs.pop(0), refs.pop(0))
    _, old_diag_ref, level_rows_ref, level_ref, total_ref, cube_ref, density_ref, diag_ref = (
        refs.pop(0) for _ in range(8)
    )
    block_ref, block_sem, left_ref, left_sem, out_sem, sent_ref, ham_ref, ham_sem = refs
    half, width = left_ref.shape[1:]
    core, row, col = info_ref[CORE], info_ref[ROW], info_ref[COL]
    worker = Worker(table_ref, core, half, block_ref, block_sem, left_ref, left_sem, total_ref)
    worker.levels = (level_rows_ref, level_ref, diag_ref)
    worker.load_block(0, X4, sources)
    worker.load_block(1, Z4, sources)
    for k in range(2):
        worker.load_left(k, info_ref[OPEN_LEFT + k], row_refs)
    for k in range(4):
        worker.load_block(2 + k, table_ref[slots_at + k], sources)
    ham_copy = pltpu.make_async_copy(row_refs[0].at[worker.near], ham_ref, ham_sem)
    sent_copy = pltpu.make_async_copy(sent_ref, cube_ref, out_sem.at[0])
    density_copy = pltpu.make_async_copy(total_ref.at[4 + core], density_ref.at[worker.near], out_sem.at[1])

    def send(field):
        sent_ref[...] = total_ref[field[4]].astype(sent_ref.dtype)
        sent_copy.start()
        ham_copy.start()

    worker.send = send
    diag_ref[...] = old_diag_ref[...]
    worker.run(steps)
    ham_copy.wait()
    gain = gain_ref[0]
    linear, cubic = -1.5 * gain, 2.0 * (gain * gain * gain)

    def one(index, carry):
        rows = pl.ds(pl.multiple_of(index * 16, 16), 16)
        for m in range(width // 128):
            at = slice(m * 128, (m + 1) * 128)
            cube = total_ref[4 + core, rows, at]
            total_ref[4 + core, rows, at] = linear * ham_ref[rows, at].astype(jnp.float32) + cubic * cube
        return carry

    lax.fori_loop(0, half // 16, one, 0, unroll=2)

    @pl.when(row == 2 * col + core)
    def _():
        eye = lax.broadcasted_iota(jnp.int32, (128, 128), 0) == lax.broadcasted_iota(jnp.int32, (128, 128), 1)

        def fix(index, carry):
            rows = pl.ds(pl.multiple_of(index * 128, 128), 128)
            at = pl.ds(pl.multiple_of(core * half + index * 128, 128), 128)
            total_ref[4 + core, rows, at] += jnp.where(eye, 0.5 + linear * level_rows_ref[rows, :], 0.0)
            return carry

        lax.fori_loop(0, half // 128, fix, 0)

    density_copy.start()
    sent_copy.wait()
    density_copy.wait()


HERE = pl.BlockSpec(memory_space=pltpu.HBM)
SCALARS = pl.BlockSpec(memory_space=pltpu.SMEM)
VMEM = pl.BlockSpec(memory_space=pltpu.VMEM)
VMEM_BYTES = 38 * 2**20


def in_hbm(values):
    return [pltpu.with_memory_space_constraint(value, pltpu.HBM) for value in values]


def work_scratch(half, width, blocks, lefts):
    return [
        pltpu.VMEM((blocks, 2 * half, width), jnp.bfloat16),
        pltpu.SemaphoreType.DMA((blocks, 2)),
        pltpu.VMEM((lefts, half, width), jnp.bfloat16),
        pltpu.SemaphoreType.DMA((lefts,)),
    ]


def call_kernel(name, kernel, shape, scalars, operands, totals, in_vmem, out_shape, out_specs, scratch):
    first = len(scalars) + len(operands)
    held = [] if totals is None else [pltpu.with_memory_space_constraint(totals, pltpu.VMEM)]
    return pl.pallas_call(
        kernel,
        out_shape=(pltpu.VMEM((6,) + shape, jnp.float32),) + tuple(out_shape),
        in_specs=[SCALARS] * len(scalars) + [HERE] * len(operands) + [VMEM] * (len(held) + len(in_vmem)),
        out_specs=(VMEM,) + tuple(out_specs),
        scratch_shapes=scratch,
        input_output_aliases={first: 0} if held else {},
        compiler_params=pltpu.CompilerParams(vmem_limit_bytes=VMEM_BYTES),
        name=name,
    )(*scalars, *in_hbm(operands), *held, *in_vmem)


def pick_kernel(choices, whole, count, info_ref, *refs):
    sources, refs = refs[:count], refs[count:]
    outs, held_ref, in_sem, out_sem = refs[:-3], refs[-3], refs[-2], refs[-1]
    parts = in_sem.shape[1]
    size = held_ref.shape[1] // parts
    for part in range(parts):
        for k, choice in enumerate(choices):
            to = held_ref.at[k, pl.ds(part * size, size)]
            for number, source in enumerate(sources):
                @pl.when(info_ref[choice] == number)
                def _():
                    first = part * size
                    if number < whole:
                        first = pl.multiple_of(info_ref[FIRST_ROW] + first, size)
                    pltpu.make_async_copy(source.at[pl.ds(first, size)], to, in_sem.at[k, part]).start()
    for part in range(parts):
        for k, out_ref in enumerate(outs):
            rows = pl.ds(part * size, size)
            pltpu.make_async_copy(held_ref.at[k, rows], held_ref.at[k, rows], in_sem.at[k, part]).wait()
            pltpu.make_async_copy(held_ref.at[k, rows], out_ref.at[rows], out_sem.at[k, part]).start()
    for part in range(parts):
        for k, out_ref in enumerate(outs):
            rows = pl.ds(part * size, size)
            pltpu.make_async_copy(held_ref.at[k, rows], out_ref.at[rows], out_sem.at[k, part]).wait()


def pick(info, choices, sources, whole, shape):
    dtype = sources[0].dtype
    parts = 4
    return pl.pallas_call(
        functools.partial(pick_kernel, choices, whole, len(sources)),
        out_shape=[jax.ShapeDtypeStruct(shape, dtype)] * len(choices),
        in_specs=[SCALARS] + [HERE] * len(sources),
        out_specs=[HERE] * len(choices),
        scratch_shapes=[
            pltpu.VMEM((len(choices),) + shape, dtype),
            pltpu.SemaphoreType.DMA((len(choices), parts)),
            pltpu.SemaphoreType.DMA((len(choices), parts)),
        ],
        compiler_params=pltpu.CompilerParams(vmem_limit_bytes=VMEM_BYTES),
        name="pick",
    )(info, *in_hbm(sources))


def pairs_kernel(spots_ref, points_ref, out_ref, high_ref, low_ref, wide_ref):
    count, width = points_ref.shape[0], spots_ref.shape[1]
    tiles = width // 128

    @pl.when(pl.program_id(0) == 0)
    def _():
        for k in range(4):
            wide_ref[k] = jnp.broadcast_to(points_ref[:, k : k + 1], (count, 128))

    lanes = [slice(m * 128, (m + 1) * 128) for m in range(tiles)]
    spots = [[jnp.broadcast_to(spots_ref[k : k + 1, at], (16, 128)) for k in range(3)] for at in lanes]

    def step(group, sums):
        rows = pl.ds(pl.multiple_of(group * 16, 16), 16)
        px, py, pz, charge = (wide_ref[k, rows, :] for k in range(4))
        sums = list(sums)
        for m, at in enumerate(lanes):
            dx, dy, dz = spots[m][0] - px, spots[m][1] - py, spots[m][2] - pz
            inv = lax.rsqrt(dx * dx + dy * dy + dz * dz + 1.0)
            sums[m] = sums[m] + charge * inv
            weight = inv * (inv * inv)
            high = weight.astype(jnp.bfloat16)
            high_ref[rows, at] = high
            low_ref[rows, at] = (weight - high.astype(jnp.float32)).astype(jnp.bfloat16)
        return tuple(sums)

    zeros = tuple(jnp.zeros((16, 128), jnp.float32) for _ in range(tiles))
    sums = lax.fori_loop(0, count // 16, step, zeros, unroll=2)
    for m, at in enumerate(lanes):
        out_ref[:, at] = jnp.sum(sums[m], 0, keepdims=True)


def pair_terms(centers, points):
    total, count = centers.shape[1], points.shape[0]
    width = 512
    part = jax.ShapeDtypeStruct((count, total), jnp.bfloat16)
    return pl.pallas_call(
        pairs_kernel,
        grid=(total // width,),
        out_shape=(jax.ShapeDtypeStruct((1, total), jnp.float32), part, part),
        in_specs=[pl.BlockSpec((3, width), lambda i: (0, i)), pl.BlockSpec((count, 4), lambda i: (0, 0))],
        out_specs=[pl.BlockSpec((1, width), lambda i: (0, i))] + [pl.BlockSpec((count, width), lambda i: (0, i))] * 2,
        scratch_shapes=[pltpu.VMEM((4, count, 128), jnp.float32)],
        compiler_params=pltpu.CompilerParams(vmem_limit_bytes=VMEM_BYTES),
        name="pairs",
    )(centers, points)


MIDDLE = 10.0


def pull_kernel(spots_ref, occ_ref, high_ref, low_ref, coords_ref, charge_ref, out_ref, total_ref):
    index = pl.program_id(0)
    occ = occ_ref[...]
    weights = [occ] + [occ * (spots_ref[k : k + 1, :] - MIDDLE) for k in range(3)]
    width = occ.shape[1]
    stacked = jnp.concatenate(weights + [jnp.zeros((4, width), jnp.float32)], 0)
    high = stacked.astype(jnp.bfloat16)
    low = (stacked - high.astype(jnp.float32)).astype(jnp.bfloat16)
    blank = jnp.zeros((128 - 16, width), jnp.bfloat16)
    both = jnp.concatenate([high, low, blank], 0)
    first = jnp.concatenate([high, jnp.zeros_like(low), blank], 0)
    dims = (((1,), (1,)), ((), ()))
    part = lax.dot_general(high_ref[...], both, dims, preferred_element_type=jnp.float32)
    part = part + lax.dot_general(low_ref[...], first, dims, preferred_element_type=jnp.float32)

    @pl.when(index == 0)
    def _():
        total_ref[...] = part

    @pl.when(index > 0)
    def _():
        total_ref[...] += part

    @pl.when(index == pl.num_programs(0) - 1)
    def _():
        sums = total_ref[...].T
        sums = sums[0:8] + sums[8:16]
        for k in range(3):
            pull = (coords_ref[k : k + 1, :] - MIDDLE) * sums[0:1] - sums[k + 1 : k + 2]
            out_ref[k : k + 1, :] = -charge_ref[...] * pull


def pull_terms(centers, occupation, high, low, mm_coords, mm_charges):
    total, count = centers.shape[1], mm_coords.shape[1]
    width = 1024
    return pl.pallas_call(
        pull_kernel,
        grid=(total // width,),
        out_shape=jax.ShapeDtypeStruct((3, count), jnp.float32),
        in_specs=[
            pl.BlockSpec((3, width), lambda i: (0, i)),
            pl.BlockSpec((1, width), lambda i: (0, i)),
            pl.BlockSpec((count, width), lambda i: (0, i)),
            pl.BlockSpec((count, width), lambda i: (0, i)),
            pl.BlockSpec((3, count), lambda i: (0, 0)),
            pl.BlockSpec((1, count), lambda i: (0, 0)),
        ],
        out_specs=pl.BlockSpec((3, count), lambda i: (0, 0)),
        scratch_shapes=[pltpu.VMEM((count, 128), jnp.float32)],
        name="pull",
    )(centers, occupation, high, low, mm_coords, mm_charges[None])


def density_kernel(steps, info_ref, gain_ref, ham_ref, far_ref, level_ref, _, out_ref):
    index = pl.program_id(0)
    core, row, col = info_ref[CORE], info_ref[ROW], info_ref[COL]
    gain = gain_ref[0]
    height, width = out_ref.shape
    linear, cubic = -1.5 * gain, 2.0 * (gain * gain * gain)
    first = ((1 - core) * steps + index) * height

    def one(k, carry):
        rows = pl.ds(pl.multiple_of(k * 16, 16), 16)
        for m in range(width // 128):
            at = slice(m * 128, (m + 1) * 128)
            cube = far_ref[rows, at].astype(jnp.float32)
            out_ref[rows, at] = linear * ham_ref[rows, at].astype(jnp.float32) + cubic * cube
        return carry

    lax.fori_loop(0, height // 16, one, 0, unroll=2)

    @pl.when(row == 2 * col + core)
    def _():
        eye = lax.broadcasted_iota(jnp.int32, (128, 128), 0) == lax.broadcasted_iota(jnp.int32, (128, 128), 1)

        def fix(k, carry):
            rows = pl.ds(pl.multiple_of(k * 128, 128), 128)
            at = pl.ds(pl.multiple_of(first + k * 128, 128), 128)
            out_ref[rows, at] += jnp.where(eye, 0.5 + linear * level_ref[:, at], 0.0)
            return carry

        lax.fori_loop(0, height // 128, fix, 0)


def density_rest(info, gain, ham, far, level_cols, density):
    height, width = ham.shape
    steps = 1
    chunk = far.shape[0] // steps
    return pl.pallas_call(
        functools.partial(density_kernel, steps),
        grid_spec=pltpu.PrefetchScalarGridSpec(
            num_scalar_prefetch=1,
            grid=(steps,),
            in_specs=[
                SCALARS,
                pl.BlockSpec((chunk, width), lambda i, info: ((1 - info[CORE]) * steps + i, 0)),
                pl.BlockSpec((chunk, width), lambda i, info: (i, 0)),
                pl.BlockSpec((1, width), lambda i, info: (0, 0)),
                HERE,
            ],
            out_specs=pl.BlockSpec((chunk, width), lambda i, info: ((1 - info[CORE]) * steps + i, 0)),
        ),
        out_shape=jax.ShapeDtypeStruct((height, width), jnp.float32),
        input_output_aliases={5: 0},
        compiler_params=pltpu.CompilerParams(vmem_limit_bytes=VMEM_BYTES),
        name="density",
    )(info, gain, ham, far, level_cols, density)


def gossip_shards(sizes, h_core, centers, mm_coords, mm_charges):
    height, width = h_core.shape
    half = height // 2
    total, count = centers.shape[1], mm_coords.shape[1]
    row, col, core = (lax.axis_index(name) for name in ("sec", "col", "rep"))
    row_start = row * height
    col_start = (2 * col + core) * width
    infos, rows, steps, slots_at = device_tables(half)
    device = 4 * row + 2 * col + core
    info, table = (
        lax.dynamic_index_in_dim(jnp.asarray(values, jnp.int32), device, 0, keepdims=False) for values in (infos, rows)
    )

    def over_rep(value):
        return lax.ppermute(value, "rep", [(0, 1), (1, 0)])

    def over_col(value):
        return lax.ppermute(value, "col", [(0, 1), (1, 0)])

    def over_sec(value, step):
        moves = [(2 * start + x, 2 * to + x) for x in range(2) for start, to in Z_MOVES[step][x]]
        return lax.ppermute(value, ("sec", "col"), moves)

    def swap_all(values):
        return [(value, over_rep(value)) for value in values]

    def flat(groups):
        return [value for group in groups for value in group]

    def after(arrived, work):
        return lax.optimization_barrier((arrived, work))

    shape = (half, width)
    own_parts = (h_core, over_rep(h_core))
    sends = pick(info, (SEND_X1, SEND_Z1), own_parts, 2, shape)
    x1 = over_col(sends[0])
    z1 = over_sec(sends[1], 0)
    points = jnp.concatenate([mm_coords, mm_charges[None]], 0).T
    terms, high, low = pair_terms(centers, points)
    rows_glob = row_start + lax.broadcasted_iota(jnp.int32, (height, width), 0)
    cols_glob = col_start + lax.broadcasted_iota(jnp.int32, (height, width), 1)
    on_diag = rows_glob == cols_glob
    wide = h_core.astype(jnp.float32)
    own_diag = jnp.sum(jnp.where(on_diag, wide, 0.0), 0)
    own_off = jnp.sum(jnp.where(on_diag, 0.0, wide * wide))
    diag = lax.dynamic_update_slice_in_dim(jnp.zeros((total,), jnp.float32), own_diag, col_start, 0)
    packed = jnp.concatenate([terms[0], diag, jnp.full((128,), own_off)])
    packed = packed + over_rep(packed)
    (x1, z1), (packed, high, low, table) = after((x1, z1), (packed, high, low, table))
    sends = pick(info, (SEND_X2, SEND_Z2), own_parts + (x1,), 2, shape)
    x2 = over_col(sends[0])
    z2 = over_sec(sends[1], 1)
    pairs = dict(zip((X1, Z1), swap_all((x1, z1))))

    def grow_square(stage, lefts, slots, totals, token):
        operands = list(lefts) + list(own_parts) + flat(pairs[slot] for slot in slots)
        operands += [] if token is None else [token]
        kernel = functools.partial(square_kernel, totals is None, steps[stage], len(lefts), (OWN0, OWN1) + slots)
        return call_kernel(
            f"square_{stage}", kernel, shape, (table, info), operands, totals, (),
            (jax.ShapeDtypeStruct((8, 128), jnp.float32),), (VMEM,), work_scratch(half, width, 2 + len(slots), 4),
        )

    lefts = list(own_parts) + [x1]
    totals, token = grow_square(0, lefts, (X1, Z1), None, None)
    col_packed = over_col(packed)
    (x2, z2, col_packed), (token, packed) = after((x2, z2, col_packed), (token, packed))
    x3 = over_col(z2)
    z3 = over_sec(x2, 2)
    pairs.update(zip((X2, Z2), swap_all((x2, z2))))
    lefts.append(x2)
    totals, token = grow_square(1, lefts, (X1, Z1, X2, Z2), totals, token)
    packed = packed + col_packed
    others = [lax.ppermute(packed, "sec", [(i, (i + hop) % 4) for i in range(4)]) for hop in (1, 2, 3)]
    (x3, z3, others), (token, packed) = after((x3, z3, others), (token, packed))
    last_send = pick(info, (SEND_LAST,), (z1, z3), 0, shape)[0]
    x4 = over_col(last_send)
    z4 = over_sec(last_send, 3)
    pairs.update(zip((X3, Z3), swap_all((x3, z3))))
    sums = packed + others[0] + others[1] + others[2]
    potential, diag, off_total = sums[:total], sums[total : 2 * total], sums[2 * total]
    diag_vals = potential + diag
    mean_level = jnp.sum(diag_vals) / total
    above = diag_vals - mean_level
    level = potential - mean_level
    spread = jnp.sqrt((off_total + jnp.sum(above * above)) / total + 1e-05)
    gain = 1.0 / (3.0 * spread)
    level_rows = lax.dynamic_slice_in_dim(level, row_start + core * half, half, 0)
    level_rows = jnp.broadcast_to(level_rows[:, None], (half, 128))
    level_cols = lax.dynamic_slice_in_dim(level, col_start, width, 0)[None]
    share = jax.ShapeDtypeStruct((half, 128), jnp.float32)
    totals, cube_diag = call_kernel(
        "early_cube", functools.partial(early_kernel, steps[2], slots_at[0]), shape, (table, info),
        lefts + list(own_parts) + flat(pairs[slot] for slot in range(X1, Z3 + 1)) + [token], totals, (level_rows, level[None]),
        (share,), (VMEM,), work_scratch(half, width, 6, 6),
    )
    (x4, z4), (cube_diag, above, level_rows, level, level_cols, gain) = after(
        (x4, z4), (cube_diag, above, level_rows, level, level_cols, gain)
    )
    pairs.update(zip((X4, Z4), swap_all((x4, z4))))
    blocks = list(own_parts) + flat(pairs[slot] for slot in range(X1, Z4 + 1))
    _, sibling, density, cube_diag = call_kernel(
        "late_cube", functools.partial(late_kernel, steps[3], slots_at[1]), shape, (table, info, gain[None]),
        lefts + blocks, totals, (cube_diag, level_rows, level[None]),
        (jax.ShapeDtypeStruct(shape, jnp.bfloat16), jax.ShapeDtypeStruct((height, width), jnp.float32), share),
        (HERE, HERE, VMEM),
        work_scratch(half, width, 6, 4)
        + [
            pltpu.SemaphoreType.DMA((2,)),
            pltpu.VMEM(shape, jnp.bfloat16),
            pltpu.VMEM(shape, jnp.bfloat16),
            pltpu.SemaphoreType.DMA,
        ],
    )
    sibling = over_rep(sibling)
    cube_diag = lax.dynamic_update_slice_in_dim(
        jnp.zeros((total,), jnp.float32), jnp.sum(cube_diag, 1), row_start + core * half, 0
    )
    cube_diag = cube_diag + over_rep(cube_diag)
    others = [lax.ppermute(cube_diag, "sec", [(i, (i + hop) % 4) for i in range(4)]) for hop in (1, 2, 3)]
    density = density_rest(info, gain[None], h_core, sibling, level_cols, density)
    others, density = after(others, density)
    cube_diag = cube_diag + others[0] + others[1] + others[2]
    occupation = 0.5 - 1.5 * gain * above + 2.0 * gain**3 * cube_diag
    forces = pull_terms(centers, occupation[None], high, low, mm_coords, mm_charges)
    return (density, forces)


def solution(mesh):
    in_specs = (
        P(("groups", "sec"), ("col", "rep")),
        P(None, "groups"),
        P(None, ("groups", "sec", "col", "rep")),
        P(("groups", "sec", "col", "rep")),
    )
    out_specs = (P(("groups", "sec"), ("col", "rep")), P(None, ("groups", "sec", "col", "rep")))
    sizes = dict(mesh.shape)
    small = (sizes["sec"], sizes["col"], sizes["rep"]) == (4, 2, 2)
    body = functools.partial(gossip_shards if small else gather_shards, sizes)
    return jax.shard_map(body, mesh=mesh, in_specs=in_specs, out_specs=out_specs, check_vma=False)
```

```python
import functools

import jax
import jax.numpy as jnp
from jax import lax
from jax.experimental import pallas as pl
from jax.experimental.pallas import tpu as pltpu
from jax.sharding import PartitionSpec as P

PART = ("sec", "col", "rep")


def potential_kernel(spots_ref, points_ref, out_ref):
    count = points_ref.shape[0]
    width = spots_ref.shape[1]
    sx, sy, sz = (spots_ref[k : k + 1, :] for k in range(3))

    def step(index, accum):
        rows = points_ref[pl.ds(pl.multiple_of(index * 8, 8), 8), :]
        dx = sx - rows[:, 0:1]
        dy = sy - rows[:, 1:2]
        dz = sz - rows[:, 2:3]
        dist = dx * dx + dy * dy + dz * dz + 1.0
        return accum + rows[:, 3:4] * lax.rsqrt(dist)

    total = lax.fori_loop(0, count // 8, step, jnp.zeros((8, width), jnp.float32), unroll=4)
    out_ref[...] = jnp.sum(total, 0, keepdims=True)


def potential_terms(centers, mm_coords, mm_charges):
    total = centers.shape[1]
    count = mm_coords.shape[1]
    width = 1024 if total % 1024 == 0 else total
    points = jnp.concatenate([mm_coords, mm_charges[None]], 0).T
    return pl.pallas_call(
        potential_kernel,
        grid=(total // width,),
        out_shape=jax.ShapeDtypeStruct((1, total), jnp.float32),
        in_specs=[
            pl.BlockSpec((3, width), lambda i: (0, i)),
            pl.BlockSpec((count, 4), lambda i: (0, 0)),
        ],
        out_specs=pl.BlockSpec((1, width), lambda i: (0, i)),
        name="potential",
    )(centers, points)


def force_kernel(spots_ref, occ_ref, points_ref, out_ref):
    total = spots_ref.shape[1]
    rows = points_ref[...]
    px, py, pz, charge = (rows[:, k : k + 1] for k in range(4))
    count = rows.shape[0]

    def step(index, accum):
        lanes = pl.ds(pl.multiple_of(index * 128, 128), 128)
        dx = px - spots_ref[0:1, lanes]
        dy = py - spots_ref[1:2, lanes]
        dz = pz - spots_ref[2:3, lanes]
        inv = lax.rsqrt(dx * dx + dy * dy + dz * dz + 1.0)
        weight = occ_ref[:, lanes] * inv * (inv * inv)
        return (accum[0] + dx * weight, accum[1] + dy * weight, accum[2] + dz * weight)

    zero = jnp.zeros((count, 128), jnp.float32)
    sums = lax.fori_loop(0, total // 128, step, (zero, zero, zero), unroll=4)
    for k in range(3):
        out_ref[:, k : k + 1] = -charge * jnp.sum(sums[k], 1, keepdims=True)


def force_terms(centers, occupation, mm_coords, mm_charges):
    total = centers.shape[1]
    count = mm_coords.shape[1]
    width = 32
    points = jnp.concatenate([mm_coords, mm_charges[None]], 0).T
    summed = pl.pallas_call(
        force_kernel,
        grid=(count // width,),
        out_shape=jax.ShapeDtypeStruct((count, 4), jnp.float32),
        in_specs=[
            pl.BlockSpec((3, total), lambda i: (0, 0)),
            pl.BlockSpec((1, total), lambda i: (0, 0)),
            pl.BlockSpec((width, 4), lambda i: (i, 0)),
        ],
        out_specs=pl.BlockSpec((width, 4), lambda i: (i, 0)),
        name="forces",
    )(centers, occupation, points)
    return summed[:, :3].T


def butterfly_sum(value, sizes, axes=("rep", "col", "sec")):
    for axis in axes:
        size = sizes[axis]
        if size & (size - 1):
            value = lax.psum(value, axis)
            continue
        hop = 1
        while hop < size:
            value = value + lax.ppermute(value, axis, [(i, i ^ hop) for i in range(size)])
            hop *= 2
    return value


def fold_with(left, piece):
    return jnp.dot(left, piece, preferred_element_type=jnp.float32)


def gather_shards(sizes, h_core, centers, mm_coords, mm_charges):
    row_count, col_count = h_core.shape
    total = centers.shape[1]
    row_start = lax.axis_index("sec") * row_count
    col_start = lax.axis_index(("col", "rep")) * col_count
    rows_glob = row_start + lax.broadcasted_iota(jnp.int32, (row_count, col_count), 0)
    cols_glob = col_start + lax.broadcasted_iota(jnp.int32, (row_count, col_count), 1)
    on_diag = rows_glob == cols_glob
    off = jnp.where(on_diag, jnp.zeros((), h_core.dtype), h_core)
    row_panel = lax.all_gather(off, ("col", "rep"), axis=1, tiled=True)
    col_panel = lax.all_gather(off, "sec", axis=0, tiled=True)

    wide = h_core.astype(jnp.float32)
    own_diag = jnp.sum(jnp.where(on_diag, wide, 0.0), 0)
    own_off = jnp.sum(jnp.where(on_diag, 0.0, wide * wide))
    terms = potential_terms(centers, mm_coords, mm_charges)[0]
    own_cols = lax.dynamic_slice_in_dim(terms, col_start, col_count, 0) + own_diag
    terms = lax.dynamic_update_slice_in_dim(terms, own_cols, col_start, 0)
    sums = butterfly_sum(jnp.concatenate([terms, jnp.full((128,), own_off)]), sizes)
    diag_vals, off_total = sums[:total], sums[total]
    mean_level = jnp.sum(diag_vals) / total
    level = diag_vals - mean_level
    spread = jnp.sqrt((off_total + jnp.sum(level * level)) / total + 1e-05)
    gain = 1.0 / (3.0 * spread)

    level_rows = lax.dynamic_slice_in_dim(level, row_start, row_count, 0)[:, None]
    level_cols = lax.dynamic_slice_in_dim(level, col_start, col_count, 0)[None, :]
    off_wide = off.astype(jnp.float32)
    square = fold_with(row_panel, col_panel)
    square = square + off_wide * (level_rows + level_cols) + jnp.where(on_diag, level_rows * level_rows, 0.0)
    shifted = off_wide + jnp.where(on_diag, level_rows, 0.0)
    square_b = square.astype(jnp.bfloat16)
    square_panel = lax.all_gather(square_b, ("col", "rep"), axis=1, tiled=True)
    own_cube = jnp.sum(square * shifted, 0)
    cube_diag = lax.dynamic_update_slice_in_dim(jnp.zeros((total,), jnp.float32), own_cube, col_start, 0)
    cube_diag = butterfly_sum(cube_diag, sizes)
    occupation = 0.5 - 1.5 * gain * level + 2.0 * gain**3 * cube_diag
    forces = force_terms(centers, occupation[None], mm_coords, mm_charges)

    cube = fold_with(square_panel, col_panel) + square_b.astype(jnp.float32) * level_cols
    density = jnp.where(on_diag, 0.5, 0.0) - 1.5 * gain * shifted + 2.0 * gain**3 * cube
    return (density, forces)


ROUND = ((0, 1), (1, 2), (2, 3), (3, 0))
BACK = ((0, 3), (3, 2), (2, 1), (1, 0))
Z_MOVES = ((ROUND, BACK), (BACK, ROUND), (ROUND, BACK), (ROUND, BACK))
OWN0, OWN1, X1, Z1, X2, Z2, X3, Z3, X4, Z4 = range(10)
X_SENDS = ((OWN1, OWN0, OWN1, OWN0), (OWN0, OWN1, OWN0, OWN1), (Z2,) * 4, (Z3, Z1, Z1, Z3))
Z_SENDS = ((OWN0, OWN1, OWN0, OWN1), (OWN1, X1, X1, OWN0), (X2,) * 4, (Z3, Z1, Z1, Z3))
SLOT_STAGE = (0, 0, 0, 0, 1, 1, 2, 2, 3, 3)
LEFT_SLOTS = (OWN0, OWN1, X1, X2)
LEFT_STAGE = (0, 0, 0, 1)
FIELDS = 10
NOTHING, MULTIPLY, FINISH, LEVEL, SEND, ZERO = range(6)
BLOCK_BIT, LEFT_BIT = 0, 8


def block_places():
    chips = [(z, x) for z in range(4) for x in range(2)]
    held = {(z, x): [(z, 2 * x), (z, 2 * x + 1)] for z, x in chips}
    for step in range(4):
        arrived = {}
        for z, x in chips:
            before = next(start for start, to in Z_MOVES[step][x] if to == z)
            arrived[(z, x)] = [held[(z, 1 - x)][X_SENDS[step][z]], held[(before, x)][Z_SENDS[step][before]]]
        for chip in chips:
            held[chip] = held[chip] + arrived[chip]
    return [held[chip] for chip in chips]


def rows_of(products, length, lefts, ahead):
    seen, firsts = set(), []
    for kind, left, block, flip, total, column in products:
        bits = []
        if kind in (MULTIPLY, FINISH, LEVEL):
            loaded_left = block if kind == FINISH else left
            if loaded_left in lefts:
                bits.append(LEFT_BIT + loaded_left)
        if kind == MULTIPLY:
            bits.append(BLOCK_BIT + block)
        firsts.append([bit for bit in dict.fromkeys(bits) if bit not in seen])
        seen.update(bits)
    mask = lambda bits: sum(1 << bit for bit in bits)
    waves = [k for k, first in enumerate(firsts) if first]
    starts = [[] for _ in products]
    for number, k in enumerate(waves):
        at = 0 if number <= ahead else waves[number - ahead]
        starts[at] += firsts[k]
    rows = []
    for k, (kind, left, block, flip, total, column) in enumerate(products):
        rows.append([kind, left, block, flip, total, mask(firsts[k]), column, mask(starts[k]), 0, 0])
    return rows + [[NOTHING] + [0] * (FIELDS - 1)] * (length - len(rows))


def device_lists():
    devices = []
    for chip, slots in enumerate(block_places()):
        assert len({tuple(sorted(place)) for place in slots}) == 10
        row, col = divmod(chip, 2)
        assert all(slots[s][0] == row for s in LEFT_SLOTS)
        lefts = [slots[s][1] for s in LEFT_SLOTS]
        stages = [[], [], [], []]
        for slot, (first, second) in enumerate(slots):
            for inner, outer, flip in [(first, second, 0), (second, first, 1)][: 1 if first == second else 2]:
                left = lefts.index(inner)
                stage = max(LEFT_STAGE[left], SLOT_STAGE[slot])
                base = (0, 0, X3, X4)[stage]
                key = max(slot, LEFT_SLOTS[left])
                stages[stage].append((key, (MULTIPLY, left, slot - base, flip, outer, 0)))
        stages = [[product for _, product in sorted(stage)] for stage in stages]
        first, touched = [], set()
        for product in stages[0]:
            if product[4] not in touched:
                first.append((ZERO, 0, 0, 0, product[4], 0))
            touched.add(product[4])
            first.append(product)
        first += [(ZERO, 0, 0, 0, total, 0) for total in range(4) if total not in touched]
        open_columns = sorted({product[4] for product in stages[3]})
        done_columns = [column for column in range(4) if column not in open_columns]
        assert len(open_columns) == 2

        def find(inner, outer):
            if (inner, outer) in slots:
                return slots.index((inner, outer)), 0
            return slots.index((outer, inner)), 1

        for core in range(2):
            early, early_slots = list(stages[2]), []
            early += [(ZERO, 0, 0, 0, 4 + which, 0) for which in range(2)]
            for k, column in enumerate(done_columns):
                early.append((FINISH, 4 + k, lefts.index(column), int(column == row), column, column))
            for which in range(2):
                for k, column in enumerate(done_columns):
                    slot, flip = find(column, 2 * col + which)
                    early.append((MULTIPLY, 4 + k, 2 + len(early_slots), flip, 4 + which, 0))
                    early_slots.append(slot)
                    if column == 2 * col + which:
                        early.append((LEVEL, 4 + k, 0, 0, 4 + which, column))
            late, late_slots = [], []
            for product in stages[3]:
                left = open_columns.index(lefts[product[1]])
                late.append((MULTIPLY, left) + product[2:])
            for k, column in enumerate(open_columns):
                late.append((FINISH, 2 + k, k, int(column == row), column, column))
            for k, which in enumerate((1 - core, core)):
                for m, column in enumerate(open_columns):
                    slot, flip = find(column, 2 * col + which)
                    late.append((MULTIPLY, 2 + m, 2 + len(late_slots), flip, 4 + which, 0))
                    late_slots.append(slot)
                    if column == 2 * col + which:
                        late.append((LEVEL, 2 + m, 0, 0, 4 + which, column))
                if k == 0:
                    late.append((SEND, 0, 0, 0, 4 + which, 0))
            own_rows = lambda slot: int(slot != core)
            straight = core == X_SENDS[0][row]
            second, last = Z_SENDS[1][row], X_SENDS[3][row]
            info = [
                core, row, col, core * 640,
                own_rows(X_SENDS[1][row]), (2 if straight else 3) if second == X1 else own_rows(second),
                0 if last == Z3 else (1 if straight else 2), int(straight),
            ] + [lefts.index(column) for column in open_columns] + open_columns
            devices.append(
                dict(
                    kernels=[first, stages[1], early, late],
                    slots=[early_slots, late_slots],
                    info=info,
                )
            )
    return devices


CORE, ROW, COL, FIRST_ROW, SEND_X2, SEND_Z2, SEND_LAST, STRAIGHT, OPEN_LEFT, OPEN = (*range(9), 10)


def device_tables(half):
    devices = device_lists()
    steps, rows = [], [[] for _ in devices]
    for kernel, (lefts, ahead) in enumerate((((0, 1, 2), 2), (range(4), 2), (range(4), 2), ((0, 1), 1))):
        length = max(len(device["kernels"][kernel]) for device in devices)
        steps.append((len(rows[0]), length))
        for row, device in zip(rows, devices):
            for fields in rows_of(device["kernels"][kernel], length, lefts, ahead):
                row += fields
    slots = []
    for kernel in range(2):
        slots.append(len(rows[0]))
        for row, device in zip(rows, devices):
            row += device["slots"][kernel]
    for device in devices:
        device["info"][FIRST_ROW] = device["info"][CORE] * half
    return [device["info"] for device in devices], rows, steps, slots


def bit_set(mask, bit):
    return jnp.bitwise_and(mask, jnp.int32(1 << bit)) != 0


class Worker:
    def __init__(self, table_ref, core, half, block_ref, block_sem, left_ref, left_sem, total_ref):
        self.table_ref, self.core, self.half = table_ref, core, half
        self.block_ref, self.block_sem = block_ref, block_sem
        self.left_ref, self.left_sem = left_ref, left_sem
        self.total_ref = total_ref
        self.near = pl.ds(pl.multiple_of(core * half, half), half)
        self.far = pl.ds(pl.multiple_of((1 - core) * half, half), half)
        self.blocks, self.lefts, self.send = {}, {}, None
        self.levels = None

    def load_halves(self, position, near_ref, far_ref):
        pltpu.make_async_copy(near_ref, self.block_ref.at[position, self.near], self.block_sem.at[position, 0]).start()
        pltpu.make_async_copy(far_ref, self.block_ref.at[position, self.far], self.block_sem.at[position, 1]).start()

    def load_block(self, position, slot, sources):
        self.blocks[position] = functools.partial(self.start_block, position, slot, sources)

    def start_block(self, position, slot, sources):
        for number, choices in sources.items():
            if isinstance(slot, int) and slot != number:
                continue
            for condition, near_ref, far_ref in choices:
                condition = slot == number if condition is None else jnp.logical_and(slot == number, condition)
                load = functools.partial(self.load_halves, position, near_ref, far_ref)
                if isinstance(condition, bool):
                    load()
                else:
                    pl.when(condition)(load)

    def own_sources(self, whole_ref, got_ref, other_ref):
        own = (whole_ref.at[self.near], whole_ref.at[self.far])
        return {
            slot: [(self.core == slot, *own), (self.core != slot, got_ref, other_ref)] for slot in (OWN0, OWN1)
        }

    def first_sources(self, straight, first, second, sibling_first, sibling_second):
        crossed = jnp.logical_not(straight)
        return {
            X1: [(straight, first, sibling_second), (crossed, second, sibling_first)],
            Z1: [(straight, sibling_first, second), (crossed, sibling_second, first)],
        }

    def load_left(self, index, number, refs):
        self.lefts[index] = functools.partial(self.start_left, index, number, refs)

    def left_places(self, refs):
        whole_ref, got_ref, straight, first, second = refs[:5]
        places = [(self.core, None, whole_ref.at[self.near]), (1 - self.core, None, got_ref)]
        places += [(2, straight, first), (2, jnp.logical_not(straight), second)]
        return places + [(3, None, ref) for ref in refs[5:]]

    def start_left(self, index, number, refs):
        for at, condition, ref in self.left_places(refs):
            if isinstance(at, int) and isinstance(number, int) and at != number:
                continue
            here = at == number
            if condition is not None:
                here = jnp.logical_and(here, condition)
            copy = functools.partial(self.copy_left, index, ref)
            if isinstance(here, bool):
                copy()
            else:
                pl.when(here)(copy)

    def copy_left(self, index, ref):
        pltpu.make_async_copy(ref, self.left_ref.at[index], self.left_sem.at[index]).start()

    def load_rows(self, refs):
        for k in range(len(refs) - 2):
            self.load_left(k, k, refs)

    def start(self, mask):
        for base, loads in ((LEFT_BIT, self.lefts), (BLOCK_BIT, self.blocks)):
            for index, load in loads.items():
                pl.when(bit_set(mask, base + index))(load)

    def wait(self, mask):
        half_block = self.block_ref.at[0, pl.ds(0, self.half)]
        for position in self.blocks:
            @pl.when(bit_set(mask, BLOCK_BIT + position))
            def _():
                for part in range(2):
                    pltpu.make_async_copy(half_block, half_block, self.block_sem.at[position, part]).wait()
        for index in self.lefts:
            @pl.when(bit_set(mask, LEFT_BIT + index))
            def _():
                pltpu.make_async_copy(self.left_ref.at[0], self.left_ref.at[0], self.left_sem.at[index]).wait()

    def multiply(self, field):
        total, left, block = self.total_ref.at[field[4]], self.left_ref.at[field[1]], self.block_ref.at[field[2]]

        @pl.when(field[3] == 0)
        def _():
            total[...] += jnp.dot(left[...], block[...], preferred_element_type=jnp.float32)

        @pl.when(field[3] == 1)
        def _():
            total[...] += lax.dot_general(
                left[...], block[...], (((1,), (1,)), ((), ())), preferred_element_type=jnp.float32
            )

    def tiles(self, cols_ref, column):
        lines = self.block_ref.shape[2] // 128
        return [jnp.broadcast_to(cols_ref[pl.ds(column * lines + m, 1), :], (16, 128)) for m in range(lines)]

    def finish(self, field):
        rows_ref, cols_ref, diag_ref = self.levels
        half = self.half
        total, left, made = self.total_ref.at[field[4]], self.left_ref.at[field[2]], self.left_ref.at[field[1]]
        cols = self.tiles(cols_ref, field[6])

        def one(index, carry):
            rows = pl.ds(pl.multiple_of(index * 16, 16), 16)
            level = rows_ref[rows, :]
            share = jnp.zeros((16, 128), jnp.float32)
            for m, col in enumerate(cols):
                at = slice(m * 128, (m + 1) * 128)
                ham = left[rows, at].astype(jnp.float32)
                square = total[rows, at] + ham * (level + col)
                made[rows, at] = square.astype(jnp.bfloat16)
                share = share + square * ham
            diag_ref[rows, :] += share
            return carry

        lax.fori_loop(0, half // 16, one, 0, unroll=2)

        @pl.when(field[3] == 1)
        def _():
            eye = lax.broadcasted_iota(jnp.int32, (128, 128), 0) == lax.broadcasted_iota(jnp.int32, (128, 128), 1)

            def fix(index, carry):
                rows = pl.ds(pl.multiple_of(index * 128, 128), 128)
                at = pl.ds(pl.multiple_of(self.core * half + index * 128, 128), 128)
                col = cols_ref[pl.ds((2 * field[6] + self.core) * (half // 128) + index, 1), :]
                level = rows_ref[rows, :]
                ham = left[rows, at].astype(jnp.float32)
                square = total[rows, at] + ham * (level + col)
                full = square + jnp.where(eye, level * level, 0.0)
                made[rows, at] = full.astype(jnp.bfloat16)
                diag_ref[rows, :] += jnp.where(eye, full * (ham + level) - square * ham, 0.0)
                return carry

            lax.fori_loop(0, half // 128, fix, 0)

    def add_level(self, field):
        cols = self.tiles(self.levels[1], field[6])
        total, left = self.total_ref.at[field[4]], self.left_ref.at[field[1]]

        def one(index, carry):
            rows = pl.ds(pl.multiple_of(index * 16, 16), 16)
            for m, col in enumerate(cols):
                at = slice(m * 128, (m + 1) * 128)
                total[rows, at] += left[rows, at].astype(jnp.float32) * col
            return carry

        lax.fori_loop(0, self.half // 16, one, 0, unroll=2)

    def clear(self, field):
        self.total_ref[field[4]] = jnp.zeros_like(self.total_ref[0])

    def run(self, start_count):
        start, count = start_count
        works = [(MULTIPLY, self.multiply), (ZERO, self.clear)]
        if self.levels is not None:
            works += [(FINISH, self.finish), (LEVEL, self.add_level)]
        if self.send is not None:
            works.append((SEND, self.send))

        def step(index, carry):
            field = [self.table_ref[start + index * FIELDS + k] for k in range(8)]
            pl.when(field[7] != 0)(functools.partial(self.start, field[7]))
            pl.when(field[5] != 0)(functools.partial(self.wait, field[5]))
            for kind, work in works:
                pl.when(field[0] == kind)(functools.partial(work, field))
            return carry

        lax.fori_loop(0, count, step, 0)


def take_inputs(refs, last):
    count = 7 + 2 * max(last - Z1, 0)
    return list(refs[:count]), list(refs[count:])


def use_inputs(worker, info_ref, inputs):
    own, first, rest = inputs[:3], inputs[3:7], inputs[7:]
    straight = info_ref[STRAIGHT] == 1
    sources = {**worker.own_sources(*own), **worker.first_sources(straight, *first)}
    for k in range(len(rest) // 2):
        sources[X2 + k] = [(None, rest[2 * k], rest[2 * k + 1])]
    return [own[0], own[1], straight, first[0], first[1]] + rest[:1], sources


def square_kernel(first, steps, left_count, slots, table_ref, info_ref, *refs):
    inputs, refs = take_inputs(refs, slots[-1])
    refs = refs[0 if first else 2 :]
    total_ref, token_ref, block_ref, block_sem, left_ref, left_sem = refs
    half = left_ref.shape[1]
    worker = Worker(table_ref, info_ref[CORE], half, block_ref, block_sem, left_ref, left_sem, total_ref)
    row_refs, sources = use_inputs(worker, info_ref, inputs)
    worker.load_rows(row_refs[: left_count + 2])
    for position, slot in enumerate(slots):
        worker.load_block(position, slot, sources)
    worker.run(steps)
    token_ref[...] = jnp.zeros_like(token_ref)


def early_kernel(steps, slots_at, table_ref, info_ref, *refs):
    inputs, refs = take_inputs(refs, Z3)
    _, _, level_rows_ref, level_ref, total_ref, diag_ref = (refs.pop(0) for _ in range(6))
    block_ref, block_sem, left_ref, left_sem = refs
    half = left_ref.shape[1]
    worker = Worker(table_ref, info_ref[CORE], half, block_ref, block_sem, left_ref, left_sem, total_ref)
    worker.levels = (level_rows_ref, level_ref, diag_ref)
    row_refs, sources = use_inputs(worker, info_ref, inputs)
    worker.load_rows(row_refs)
    worker.load_block(0, X3, sources)
    worker.load_block(1, Z3, sources)
    for k in range(4):
        worker.load_block(2 + k, table_ref[slots_at + k], sources)
    diag_ref[...] = jnp.zeros_like(diag_ref)
    worker.run(steps)


def late_kernel(steps, slots_at, table_ref, info_ref, gain_ref, *refs):
    inputs, refs = take_inputs(refs, Z4)
    _, old_diag_ref, level_rows_ref, level_ref, total_ref, cube_ref, density_ref, cube_diag_ref = (
        refs.pop(0) for _ in range(8)
    )
    block_ref, block_sem, left_ref, left_sem, out_sem, sent_ref, ham_ref, ham_sem, diag_ref = refs
    half, width = left_ref.shape[1:]
    core, row, col = info_ref[CORE], info_ref[ROW], info_ref[COL]
    worker = Worker(table_ref, core, half, block_ref, block_sem, left_ref, left_sem, total_ref)
    worker.levels = (level_rows_ref, level_ref, diag_ref)
    row_refs, sources = use_inputs(worker, info_ref, inputs)
    worker.load_block(0, X4, sources)
    worker.load_block(1, Z4, sources)
    for k in range(2):
        worker.load_left(k, info_ref[OPEN_LEFT + k], row_refs)
    for k in range(4):
        worker.load_block(2 + k, table_ref[slots_at + k], sources)
    ham_copy = pltpu.make_async_copy(row_refs[0].at[worker.near], ham_ref, ham_sem)
    sent_copy = pltpu.make_async_copy(sent_ref, cube_ref, out_sem.at[0])
    density_copy = pltpu.make_async_copy(total_ref.at[4 + core], density_ref.at[worker.near], out_sem.at[1])

    def send(field):
        sent_ref[...] = total_ref[field[4]].astype(sent_ref.dtype)
        sent_copy.start()
        ham_copy.start()

    worker.send = send
    diag_ref[...] = old_diag_ref[...]
    worker.run(steps)
    ham_copy.wait()
    gain = gain_ref[0]
    linear, cubic = -1.5 * gain, 2.0 * (gain * gain * gain)

    def one(index, carry):
        rows = pl.ds(pl.multiple_of(index * 16, 16), 16)
        for m in range(width // 128):
            at = slice(m * 128, (m + 1) * 128)
            cube = total_ref[4 + core, rows, at]
            total_ref[4 + core, rows, at] = linear * ham_ref[rows, at].astype(jnp.float32) + cubic * cube
        return carry

    lax.fori_loop(0, half // 16, one, 0, unroll=2)

    @pl.when(row == 2 * col + core)
    def _():
        eye = lax.broadcasted_iota(jnp.int32, (128, 128), 0) == lax.broadcasted_iota(jnp.int32, (128, 128), 1)

        def fix(index, carry):
            rows = pl.ds(pl.multiple_of(index * 128, 128), 128)
            at = pl.ds(pl.multiple_of(core * half + index * 128, 128), 128)
            total_ref[4 + core, rows, at] += jnp.where(eye, 0.5 + linear * level_rows_ref[rows, :], 0.0)
            return carry

        lax.fori_loop(0, half // 128, fix, 0)

    density_copy.start()
    lines = half // 128
    cube_diag_ref[...] = jnp.zeros_like(cube_diag_ref)
    for k in range(lines):
        share = jnp.sum(diag_ref[pl.ds(k * 128, 128), :].T, 0, keepdims=True)
        cube_diag_ref[pl.ds((2 * row + core) * lines + k, 1), :] = share
    sent_copy.wait()
    density_copy.wait()


HERE = pl.BlockSpec(memory_space=pltpu.HBM)
SCALARS = pl.BlockSpec(memory_space=pltpu.SMEM)
VMEM = pl.BlockSpec(memory_space=pltpu.VMEM)
VMEM_BYTES = 38 * 2**20


def in_hbm(values):
    return [pltpu.with_memory_space_constraint(value, pltpu.HBM) for value in values]


def work_scratch(half, width, blocks, lefts):
    return [
        pltpu.VMEM((blocks, 2 * half, width), jnp.bfloat16),
        pltpu.SemaphoreType.DMA((blocks, 2)),
        pltpu.VMEM((lefts, half, width), jnp.bfloat16),
        pltpu.SemaphoreType.DMA((lefts,)),
    ]


def call_kernel(name, kernel, shape, scalars, operands, totals, in_vmem, out_shape, out_specs, scratch):
    first = len(scalars) + len(operands)
    held = [] if totals is None else [pltpu.with_memory_space_constraint(totals, pltpu.VMEM)]
    return pl.pallas_call(
        kernel,
        out_shape=(pltpu.VMEM((6,) + shape, jnp.float32),) + tuple(out_shape),
        in_specs=[SCALARS] * len(scalars) + [HERE] * len(operands) + [VMEM] * (len(held) + len(in_vmem)),
        out_specs=(VMEM,) + tuple(out_specs),
        scratch_shapes=scratch,
        input_output_aliases={first: 0} if held else {},
        compiler_params=pltpu.CompilerParams(vmem_limit_bytes=VMEM_BYTES),
        name=name,
    )(*scalars, *in_hbm(operands), *held, *in_vmem)


def pick_kernel(choices, whole, count, info_ref, *refs):
    sources, refs = refs[:count], refs[count:]
    outs, held_ref, in_sem, out_sem = refs[:-3], refs[-3], refs[-2], refs[-1]
    parts = in_sem.shape[1]
    size = held_ref.shape[1] // parts
    for part in range(parts):
        for k, choice in enumerate(choices):
            to = held_ref.at[k, pl.ds(part * size, size)]
            for number, source in enumerate(sources):
                @pl.when(info_ref[choice] == number)
                def _():
                    first = part * size
                    if number < whole:
                        first = pl.multiple_of(info_ref[FIRST_ROW] + first, size)
                    pltpu.make_async_copy(source.at[pl.ds(first, size)], to, in_sem.at[k, part]).start()
    for part in range(parts):
        for k, out_ref in enumerate(outs):
            rows = pl.ds(part * size, size)
            pltpu.make_async_copy(held_ref.at[k, rows], held_ref.at[k, rows], in_sem.at[k, part]).wait()
            pltpu.make_async_copy(held_ref.at[k, rows], out_ref.at[rows], out_sem.at[k, part]).start()
    for part in range(parts):
        for k, out_ref in enumerate(outs):
            rows = pl.ds(part * size, size)
            pltpu.make_async_copy(held_ref.at[k, rows], out_ref.at[rows], out_sem.at[k, part]).wait()


def pick(info, choices, sources, whole, shape):
    dtype = sources[0].dtype
    parts = 4
    return pl.pallas_call(
        functools.partial(pick_kernel, choices, whole, len(sources)),
        out_shape=[jax.ShapeDtypeStruct(shape, dtype)] * len(choices),
        in_specs=[SCALARS] + [HERE] * len(sources),
        out_specs=[HERE] * len(choices),
        scratch_shapes=[
            pltpu.VMEM((len(choices),) + shape, dtype),
            pltpu.SemaphoreType.DMA((len(choices), parts)),
            pltpu.SemaphoreType.DMA((len(choices), parts)),
        ],
        compiler_params=pltpu.CompilerParams(vmem_limit_bytes=8 * 2**20),
        name="pick",
    )(info, *in_hbm(sources))


def pairs_kernel(spots_ref, points_ref, out_ref, weight_ref, wide_ref):
    count, width = points_ref.shape[0], spots_ref.shape[1]
    tiles = width // 128

    @pl.when(pl.program_id(0) == 0)
    def _():
        for k in range(4):
            wide_ref[k] = jnp.broadcast_to(points_ref[:, k : k + 1], (count, 128))

    lanes = [slice(m * 128, (m + 1) * 128) for m in range(tiles)]
    spots = [[jnp.broadcast_to(spots_ref[k : k + 1, at], (16, 128)) for k in range(3)] for at in lanes]

    def step(group, sums):
        rows = pl.ds(pl.multiple_of(group * 16, 16), 16)
        px, py, pz, charge = (wide_ref[k, rows, :] for k in range(4))
        sums = list(sums)
        for m, at in enumerate(lanes):
            dx, dy, dz = spots[m][0] - px, spots[m][1] - py, spots[m][2] - pz
            inv = lax.rsqrt(dx * dx + dy * dy + dz * dz + 1.0)
            sums[m] = sums[m] + charge * inv
            weight_ref[rows, at] = (inv * (inv * inv)).astype(jnp.bfloat16)
        return tuple(sums)

    zeros = tuple(jnp.zeros((16, 128), jnp.float32) for _ in range(tiles))
    sums = lax.fori_loop(0, count // 16, step, zeros, unroll=2)
    for m, at in enumerate(lanes):
        out_ref[:, at] = jnp.sum(sums[m], 0, keepdims=True)


def pair_terms(centers, points):
    total, count = centers.shape[1], points.shape[0]
    width = 512
    part = jax.ShapeDtypeStruct((count, total), jnp.bfloat16)
    return pl.pallas_call(
        pairs_kernel,
        grid=(total // width,),
        out_shape=(jax.ShapeDtypeStruct((1, total), jnp.float32), part),
        in_specs=[pl.BlockSpec((3, width), lambda i: (0, i)), pl.BlockSpec((count, 4), lambda i: (0, 0))],
        out_specs=[pl.BlockSpec((1, width), lambda i: (0, i))] + [pl.BlockSpec((count, width), lambda i: (0, i))],
        scratch_shapes=[pltpu.VMEM((4, count, 128), jnp.float32)],
        compiler_params=pltpu.CompilerParams(vmem_limit_bytes=VMEM_BYTES),
        name="pairs",
    )(centers, points)


def levels_kernel(info_ref, own_ref, first_ref, second_ref, third_ref, gain_ref, level_ref, above_ref, rows_ref):
    lines = level_ref.shape[0]
    sums = own_ref[...] + first_ref[...] + second_ref[...] + third_ref[...]
    potential, diag = sums[0:lines], sums[lines : 2 * lines] + sums[0:lines]
    total = float(lines * 128)
    mean = jnp.sum(diag) / total
    above = diag - mean
    squares = (jnp.sum(sums[2 * lines : 2 * lines + 1]) / 128.0 + jnp.sum(above * above)) / total
    spread = jnp.sqrt(jnp.full((8, 128), squares + 1e-05, jnp.float32))
    gain_ref[0] = jnp.max(1.0 / (3.0 * spread))
    level_ref[...] = potential - mean
    above_ref[...] = above
    half = rows_ref.shape[0]
    first = (2 * info_ref[ROW] + info_ref[CORE]) * (half // 128)
    for k in range(half // 128):
        line = level_ref[pl.ds(first + k, 1), :]
        rows_ref[pl.ds(k * 128, 128), :] = jnp.broadcast_to(line, (128, 128)).T


def level_terms(info, parts, lines, half):
    line = jax.ShapeDtypeStruct((lines, 128), jnp.float32)
    return pl.pallas_call(
        levels_kernel,
        out_shape=(jax.ShapeDtypeStruct((1,), jnp.float32), line, line, jax.ShapeDtypeStruct((half, 128), jnp.float32)),
        in_specs=[SCALARS] + [VMEM] * 4,
        out_specs=(SCALARS, VMEM, VMEM, VMEM),
        compiler_params=pltpu.CompilerParams(vmem_limit_bytes=4 * 2**20),
        name="levels",
    )(info, *parts)


MIDDLE = 10.0


def pull_kernel(gain_ref, spots_ref, above_ref, near_ref, far_ref, weight_ref, coords_ref, charge_ref, out_ref, total_ref):
    index = pl.program_id(0)
    gain = gain_ref[0]
    width = spots_ref.shape[1]
    pieces = []
    for m in range(width // 128):
        line = pl.ds(index * (width // 128) + m, 1)
        cube = near_ref[line, :] + far_ref[line, :]
        pieces.append(0.5 - 1.5 * gain * above_ref[line, :] + 2.0 * (gain * gain * gain) * cube)
    occ = jnp.concatenate(pieces, 1)
    weights = [occ] + [occ * (spots_ref[k : k + 1, :] - MIDDLE) for k in range(3)]
    stacked = jnp.concatenate(weights + [jnp.zeros((4, width), jnp.float32)], 0)
    high = stacked.astype(jnp.bfloat16)
    low = (stacked - high.astype(jnp.float32)).astype(jnp.bfloat16)
    blank = jnp.zeros((128 - 16, width), jnp.bfloat16)
    both = jnp.concatenate([high, low, blank], 0)
    dims = (((1,), (1,)), ((), ()))
    part = lax.dot_general(weight_ref[...], both, dims, preferred_element_type=jnp.float32)

    @pl.when(index == 0)
    def _():
        total_ref[...] = part

    @pl.when(index > 0)
    def _():
        total_ref[...] += part

    @pl.when(index == pl.num_programs(0) - 1)
    def _():
        sums = total_ref[...].T
        sums = sums[0:8] + sums[8:16]
        for k in range(3):
            pull = (coords_ref[k : k + 1, :] - MIDDLE) * sums[0:1] - sums[k + 1 : k + 2]
            out_ref[k : k + 1, :] = -charge_ref[...] * pull


def pull_terms(gain, centers, above, near, far, weights, mm_coords, mm_charges):
    total, count = centers.shape[1], mm_coords.shape[1]
    width = 1280
    return pl.pallas_call(
        pull_kernel,
        grid=(total // width,),
        out_shape=jax.ShapeDtypeStruct((3, count), jnp.float32),
        in_specs=[
            SCALARS,
            pl.BlockSpec((3, width), lambda i: (0, i)),
            pl.BlockSpec(above.shape, lambda i: (0, 0)),
            pl.BlockSpec(above.shape, lambda i: (0, 0)),
            pl.BlockSpec(above.shape, lambda i: (0, 0)),
            pl.BlockSpec((count, width), lambda i: (0, i)),
            pl.BlockSpec((3, count), lambda i: (0, 0)),
            pl.BlockSpec((1, count), lambda i: (0, 0)),
        ],
        out_specs=pl.BlockSpec((3, count), lambda i: (0, 0)),
        scratch_shapes=[pltpu.VMEM((count, 128), jnp.float32)],
        name="pull",
    )(gain, centers, above, near, far, weights, mm_coords, mm_charges[None])


def density_kernel(steps, info_ref, gain_ref, ham_ref, far_ref, level_ref, _, out_ref):
    index = pl.program_id(0)
    core, row, col = info_ref[CORE], info_ref[ROW], info_ref[COL]
    gain = gain_ref[0]
    height, width = out_ref.shape
    linear, cubic = -1.5 * gain, 2.0 * (gain * gain * gain)
    first = ((1 - core) * steps + index) * height

    def one(k, carry):
        rows = pl.ds(pl.multiple_of(k * 16, 16), 16)
        for m in range(width // 128):
            at = slice(m * 128, (m + 1) * 128)
            cube = far_ref[rows, at].astype(jnp.float32)
            out_ref[rows, at] = linear * ham_ref[rows, at].astype(jnp.float32) + cubic * cube
        return carry

    lax.fori_loop(0, height // 16, one, 0, unroll=2)

    @pl.when(row == 2 * col + core)
    def _():
        eye = lax.broadcasted_iota(jnp.int32, (128, 128), 0) == lax.broadcasted_iota(jnp.int32, (128, 128), 1)

        def fix(k, carry):
            rows = pl.ds(pl.multiple_of(k * 128, 128), 128)
            at = pl.ds(pl.multiple_of(first + k * 128, 128), 128)
            line = pl.ds((2 * col + core) * (width // 128) + first // 128 + k, 1)
            out_ref[rows, at] += jnp.where(eye, 0.5 + linear * level_ref[line, :], 0.0)
            return carry

        lax.fori_loop(0, height // 128, fix, 0)


def density_rest(info, gain, ham, far, level, density):
    height, width = ham.shape
    steps = 1
    chunk = far.shape[0] // steps
    return pl.pallas_call(
        functools.partial(density_kernel, steps),
        grid_spec=pltpu.PrefetchScalarGridSpec(
            num_scalar_prefetch=1,
            grid=(steps,),
            in_specs=[
                SCALARS,
                pl.BlockSpec((chunk, width), lambda i, info: ((1 - info[CORE]) * steps + i, 0)),
                pl.BlockSpec((chunk, width), lambda i, info: (i, 0)),
                pl.BlockSpec(level.shape, lambda i, info: (0, 0)),
                HERE,
            ],
            out_specs=pl.BlockSpec((chunk, width), lambda i, info: ((1 - info[CORE]) * steps + i, 0)),
        ),
        out_shape=jax.ShapeDtypeStruct((height, width), jnp.float32),
        input_output_aliases={5: 0},
        compiler_params=pltpu.CompilerParams(vmem_limit_bytes=VMEM_BYTES),
        name="density",
    )(info, gain, ham, far, level, density)


def gossip_shards(sizes, h_core, centers, mm_coords, mm_charges):
    height, width = h_core.shape
    half = height // 2
    total, count = centers.shape[1], mm_coords.shape[1]
    row, col, core = (lax.axis_index(name) for name in ("sec", "col", "rep"))
    row_start = row * height
    col_start = (2 * col + core) * width
    infos, rows, steps, slots_at = device_tables(half)
    device = 4 * row + 2 * col + core
    info, table = (
        lax.dynamic_index_in_dim(jnp.asarray(values, jnp.int32), device, 0, keepdims=False) for values in (infos, rows)
    )

    def over_rep(value):
        return lax.ppermute(value, "rep", [(0, 1), (1, 0)])

    def over_col(value):
        return lax.ppermute(value, "col", [(0, 1), (1, 0)])

    def over_sec(value, step):
        moves = [(2 * start + x, 2 * to + x) for x in range(2) for start, to in Z_MOVES[step][x]]
        return lax.ppermute(value, ("sec", "col"), moves)

    def over_both(value, own):
        moves = []
        for z, x, c in ((z, x, c) for z in range(4) for x in range(2) for c in range(2)):
            if (c if own else 1 - c) == X_SENDS[0][z]:
                to = (z, 1 - x, c)
            else:
                to = (dict(Z_MOVES[0][x])[z], x, 1 - c)
            moves.append((4 * z + 2 * x + c, 4 * to[0] + 2 * to[1] + to[2]))
        return lax.ppermute(value, ("sec", "col", "rep"), moves)

    def swap_all(values):
        return [(value, over_rep(value)) for value in values]

    def flat(groups):
        return [value for group in groups for value in group]

    def after(arrived, work):
        return lax.optimization_barrier((arrived, work))

    shape = (half, width)
    near = lax.dynamic_slice_in_dim(h_core, core * half, half, 0)
    far = lax.dynamic_slice_in_dim(h_core, (1 - core) * half, half, 0)
    got = over_rep(far)
    firsts = (over_both(near, True), over_both(got, False))
    other = over_rep(near)
    points = jnp.concatenate([mm_coords, mm_charges[None]], 0).T
    terms, weights = pair_terms(centers, points)
    rows_glob = row_start + lax.broadcasted_iota(jnp.int32, (height, width), 0)
    cols_glob = col_start + lax.broadcasted_iota(jnp.int32, (height, width), 1)
    on_diag = rows_glob == cols_glob
    wide = h_core.astype(jnp.float32)
    own_diag = jnp.sum(jnp.where(on_diag, wide, 0.0), 0)
    own_off = jnp.sum(jnp.where(on_diag, 0.0, wide * wide))
    diag = lax.dynamic_update_slice_in_dim(jnp.zeros((total,), jnp.float32), own_diag, col_start, 0)
    packed = jnp.concatenate([terms[0], diag, jnp.full((8 * 128,), own_off)]).reshape(-1, 128)
    packed = packed + over_rep(packed)
    firsts, (packed, weights, table, other) = after(firsts, (packed, weights, table, other))
    own_parts = [h_core, got, other]
    sends = pick(info, (SEND_X2, SEND_Z2), (h_core, got) + tuple(firsts), 1, shape)
    firsts, sends = lax.optimization_barrier((list(firsts), sends))
    x2 = over_col(sends[0])
    z2 = over_sec(sends[1], 1)
    operands = own_parts + firsts + [over_rep(first) for first in firsts]

    def grow_square(stage, left_count, slots, totals, token):
        kernel = functools.partial(square_kernel, totals is None, steps[stage], left_count, slots)
        return call_kernel(
            f"square_{stage}", kernel, shape, (table, info), operands + ([] if token is None else [token]), totals, (),
            (jax.ShapeDtypeStruct((8, 128), jnp.float32),), (VMEM,), work_scratch(half, width, len(slots), 4),
        )

    totals, token = grow_square(0, 3, (OWN0, OWN1, X1, Z1), None, None)
    col_packed = over_col(packed)
    (x2, z2, col_packed), (token, packed) = after((x2, z2, col_packed), (token, packed))
    x3 = over_col(z2)
    z3 = over_sec(x2, 2)
    operands = operands + flat(swap_all((x2, z2)))
    totals, token = grow_square(1, 4, (OWN0, OWN1, X1, Z1, X2, Z2), totals, token)
    packed = packed + col_packed
    others = [lax.ppermute(packed, "sec", [(i, (i + hop) % 4) for i in range(4)]) for hop in (1, 2, 3)]
    (x3, z3, others), (token, packed) = after((x3, z3, others), (token, packed))
    last_send = pick(info, (SEND_LAST,), [z3] + operands[5:7], 0, shape)[0]
    x4 = over_col(last_send)
    z4 = over_sec(last_send, 3)
    operands = operands + flat(swap_all((x3, z3)))
    gain, level, above, level_rows = level_terms(info, [packed] + list(others), total // 128, half)
    lines = jax.ShapeDtypeStruct((total // 128, 128), jnp.float32)
    share = jax.ShapeDtypeStruct((half, 128), jnp.float32)
    totals, cube_diag = call_kernel(
        "early_cube", functools.partial(early_kernel, steps[2], slots_at[0]), shape, (table, info),
        operands + [token], totals, (level_rows, level),
        (share,), (VMEM,), work_scratch(half, width, 6, 6),
    )
    (x4, z4), (cube_diag, above, level_rows, level, gain) = after(
        (x4, z4), (cube_diag, above, level_rows, level, gain)
    )
    operands = operands + flat(swap_all((x4, z4)))
    _, sibling, density, cube_diag = call_kernel(
        "late_cube", functools.partial(late_kernel, steps[3], slots_at[1]), shape, (table, info, gain),
        operands, totals, (cube_diag, level_rows, level),
        (jax.ShapeDtypeStruct(shape, jnp.bfloat16), jax.ShapeDtypeStruct((height, width), jnp.float32), lines),
        (HERE, HERE, VMEM),
        work_scratch(half, width, 6, 4)
        + [
            pltpu.SemaphoreType.DMA((2,)),
            pltpu.VMEM(shape, jnp.bfloat16),
            pltpu.VMEM(shape, jnp.bfloat16),
            pltpu.SemaphoreType.DMA,
            pltpu.VMEM((half, 128), jnp.float32),
        ],
    )
    sibling = over_rep(sibling)
    cube_diag = cube_diag + over_rep(cube_diag)
    cube_diag = cube_diag + lax.ppermute(cube_diag, "sec", [(i, i ^ 1) for i in range(4)])
    from_far = lax.ppermute(cube_diag, "sec", [(i, i ^ 2) for i in range(4)])
    density = density_rest(info, gain, h_core, sibling, level, density)
    from_far, density = after(from_far, density)
    forces = pull_terms(gain, centers, above, cube_diag, from_far, weights, mm_coords, mm_charges)
    return (density, forces)


def solution(mesh):
    in_specs = (
        P(("groups", "sec"), ("col", "rep")),
        P(None, "groups"),
        P(None, ("groups", "sec", "col", "rep")),
        P(("groups", "sec", "col", "rep")),
    )
    out_specs = (P(("groups", "sec"), ("col", "rep")), P(None, ("groups", "sec", "col", "rep")))
    sizes = dict(mesh.shape)
    small = (sizes["sec"], sizes["col"], sizes["rep"]) == (4, 2, 2)
    body = functools.partial(gossip_shards if small else gather_shards, sizes)
    return jax.shard_map(body, mesh=mesh, in_specs=in_specs, out_specs=out_specs, check_vma=False)
```

```python
import functools

import jax
import jax.numpy as jnp
from jax import lax
from jax.experimental import pallas as pl
from jax.experimental.pallas import tpu as pltpu
from jax.sharding import PartitionSpec as P

PART = ("sec", "col", "rep")


def potential_kernel(spots_ref, points_ref, out_ref):
    count = points_ref.shape[0]
    width = spots_ref.shape[1]
    sx, sy, sz = (spots_ref[k : k + 1, :] for k in range(3))

    def step(index, accum):
        rows = points_ref[pl.ds(pl.multiple_of(index * 8, 8), 8), :]
        dx = sx - rows[:, 0:1]
        dy = sy - rows[:, 1:2]
        dz = sz - rows[:, 2:3]
        dist = dx * dx + dy * dy + dz * dz + 1.0
        return accum + rows[:, 3:4] * lax.rsqrt(dist)

    total = lax.fori_loop(0, count // 8, step, jnp.zeros((8, width), jnp.float32), unroll=4)
    out_ref[...] = jnp.sum(total, 0, keepdims=True)


def potential_terms(centers, mm_coords, mm_charges):
    total = centers.shape[1]
    count = mm_coords.shape[1]
    width = 1024 if total % 1024 == 0 else total
    points = jnp.concatenate([mm_coords, mm_charges[None]], 0).T
    return pl.pallas_call(
        potential_kernel,
        grid=(total // width,),
        out_shape=jax.ShapeDtypeStruct((1, total), jnp.float32),
        in_specs=[
            pl.BlockSpec((3, width), lambda i: (0, i)),
            pl.BlockSpec((count, 4), lambda i: (0, 0)),
        ],
        out_specs=pl.BlockSpec((1, width), lambda i: (0, i)),
        name="potential",
    )(centers, points)


def force_kernel(spots_ref, occ_ref, points_ref, out_ref):
    total = spots_ref.shape[1]
    rows = points_ref[...]
    px, py, pz, charge = (rows[:, k : k + 1] for k in range(4))
    count = rows.shape[0]

    def step(index, accum):
        lanes = pl.ds(pl.multiple_of(index * 128, 128), 128)
        dx = px - spots_ref[0:1, lanes]
        dy = py - spots_ref[1:2, lanes]
        dz = pz - spots_ref[2:3, lanes]
        inv = lax.rsqrt(dx * dx + dy * dy + dz * dz + 1.0)
        weight = occ_ref[:, lanes] * inv * (inv * inv)
        return (accum[0] + dx * weight, accum[1] + dy * weight, accum[2] + dz * weight)

    zero = jnp.zeros((count, 128), jnp.float32)
    sums = lax.fori_loop(0, total // 128, step, (zero, zero, zero), unroll=4)
    for k in range(3):
        out_ref[:, k : k + 1] = -charge * jnp.sum(sums[k], 1, keepdims=True)


def force_terms(centers, occupation, mm_coords, mm_charges):
    total = centers.shape[1]
    count = mm_coords.shape[1]
    width = 32
    points = jnp.concatenate([mm_coords, mm_charges[None]], 0).T
    summed = pl.pallas_call(
        force_kernel,
        grid=(count // width,),
        out_shape=jax.ShapeDtypeStruct((count, 4), jnp.float32),
        in_specs=[
            pl.BlockSpec((3, total), lambda i: (0, 0)),
            pl.BlockSpec((1, total), lambda i: (0, 0)),
            pl.BlockSpec((width, 4), lambda i: (i, 0)),
        ],
        out_specs=pl.BlockSpec((width, 4), lambda i: (i, 0)),
        name="forces",
    )(centers, occupation, points)
    return summed[:, :3].T


def butterfly_sum(value, sizes, axes=("rep", "col", "sec")):
    for axis in axes:
        size = sizes[axis]
        if size & (size - 1):
            value = lax.psum(value, axis)
            continue
        hop = 1
        while hop < size:
            value = value + lax.ppermute(value, axis, [(i, i ^ hop) for i in range(size)])
            hop *= 2
    return value


def fold_with(left, piece):
    return jnp.dot(left, piece, preferred_element_type=jnp.float32)


def gather_shards(sizes, h_core, centers, mm_coords, mm_charges):
    row_count, col_count = h_core.shape
    total = centers.shape[1]
    row_start = lax.axis_index("sec") * row_count
    col_start = lax.axis_index(("col", "rep")) * col_count
    rows_glob = row_start + lax.broadcasted_iota(jnp.int32, (row_count, col_count), 0)
    cols_glob = col_start + lax.broadcasted_iota(jnp.int32, (row_count, col_count), 1)
    on_diag = rows_glob == cols_glob
    off = jnp.where(on_diag, jnp.zeros((), h_core.dtype), h_core)
    row_panel = lax.all_gather(off, ("col", "rep"), axis=1, tiled=True)
    col_panel = lax.all_gather(off, "sec", axis=0, tiled=True)

    wide = h_core.astype(jnp.float32)
    own_diag = jnp.sum(jnp.where(on_diag, wide, 0.0), 0)
    own_off = jnp.sum(jnp.where(on_diag, 0.0, wide * wide))
    terms = potential_terms(centers, mm_coords, mm_charges)[0]
    own_cols = lax.dynamic_slice_in_dim(terms, col_start, col_count, 0) + own_diag
    terms = lax.dynamic_update_slice_in_dim(terms, own_cols, col_start, 0)
    sums = butterfly_sum(jnp.concatenate([terms, jnp.full((128,), own_off)]), sizes)
    diag_vals, off_total = sums[:total], sums[total]
    mean_level = jnp.sum(diag_vals) / total
    level = diag_vals - mean_level
    spread = jnp.sqrt((off_total + jnp.sum(level * level)) / total + 1e-05)
    gain = 1.0 / (3.0 * spread)

    level_rows = lax.dynamic_slice_in_dim(level, row_start, row_count, 0)[:, None]
    level_cols = lax.dynamic_slice_in_dim(level, col_start, col_count, 0)[None, :]
    off_wide = off.astype(jnp.float32)
    square = fold_with(row_panel, col_panel)
    square = square + off_wide * (level_rows + level_cols) + jnp.where(on_diag, level_rows * level_rows, 0.0)
    shifted = off_wide + jnp.where(on_diag, level_rows, 0.0)
    square_b = square.astype(jnp.bfloat16)
    square_panel = lax.all_gather(square_b, ("col", "rep"), axis=1, tiled=True)
    own_cube = jnp.sum(square * shifted, 0)
    cube_diag = lax.dynamic_update_slice_in_dim(jnp.zeros((total,), jnp.float32), own_cube, col_start, 0)
    cube_diag = butterfly_sum(cube_diag, sizes)
    occupation = 0.5 - 1.5 * gain * level + 2.0 * gain**3 * cube_diag
    forces = force_terms(centers, occupation[None], mm_coords, mm_charges)

    cube = fold_with(square_panel, col_panel) + square_b.astype(jnp.float32) * level_cols
    density = jnp.where(on_diag, 0.5, 0.0) - 1.5 * gain * shifted + 2.0 * gain**3 * cube
    return (density, forces)


ROUND = ((0, 1), (1, 2), (2, 3), (3, 0))
BACK = ((0, 3), (3, 2), (2, 1), (1, 0))
Z_MOVES = ((ROUND, BACK), (BACK, ROUND), (ROUND, BACK), (ROUND, BACK))
OWN0, OWN1, X1, Z1, X2, Z2, X3, Z3, X4, Z4 = range(10)
X_SENDS = ((OWN1, OWN0, OWN1, OWN0), (OWN0, OWN1, OWN0, OWN1), (Z2,) * 4, (Z3, Z1, Z1, Z3))
Z_SENDS = ((OWN0, OWN1, OWN0, OWN1), (OWN1, X1, X1, OWN0), (X2,) * 4, (Z3, Z1, Z1, Z3))
SLOT_STAGE = (0, 0, 0, 0, 1, 1, 2, 2, 3, 3)
LEFT_SLOTS = (OWN0, OWN1, X1, X2)
LEFT_STAGE = (0, 0, 0, 1)
FIELDS = 10
NOTHING, MULTIPLY, FINISH, LEVEL, SEND, ZERO = range(6)
BLOCK_BIT, LEFT_BIT = 0, 8


def block_places():
    chips = [(z, x) for z in range(4) for x in range(2)]
    held = {(z, x): [(z, 2 * x), (z, 2 * x + 1)] for z, x in chips}
    for step in range(4):
        arrived = {}
        for z, x in chips:
            before = next(start for start, to in Z_MOVES[step][x] if to == z)
            arrived[(z, x)] = [held[(z, 1 - x)][X_SENDS[step][z]], held[(before, x)][Z_SENDS[step][before]]]
        for chip in chips:
            held[chip] = held[chip] + arrived[chip]
    return [held[chip] for chip in chips]


def rows_of(products, length, lefts, ahead):
    seen, firsts = set(), []
    for kind, left, block, flip, total, column in products:
        bits = []
        if kind in (MULTIPLY, FINISH, LEVEL):
            loaded_left = block if kind == FINISH else left
            if loaded_left in lefts:
                bits.append(LEFT_BIT + loaded_left)
        if kind == MULTIPLY:
            bits.append(BLOCK_BIT + block)
        firsts.append([bit for bit in dict.fromkeys(bits) if bit not in seen])
        seen.update(bits)
    mask = lambda bits: sum(1 << bit for bit in bits)
    waves = [k for k, first in enumerate(firsts) if first]
    starts = [[] for _ in products]
    for number, k in enumerate(waves):
        at = 0 if number <= ahead else waves[number - ahead]
        starts[at] += firsts[k]
    rows = []
    for k, (kind, left, block, flip, total, column) in enumerate(products):
        rows.append([kind, left, block, flip, total, mask(firsts[k]), column, mask(starts[k]), 0, 0])
    return rows + [[NOTHING] + [0] * (FIELDS - 1)] * (length - len(rows))


def device_lists():
    devices = []
    for chip, slots in enumerate(block_places()):
        assert len({tuple(sorted(place)) for place in slots}) == 10
        row, col = divmod(chip, 2)
        assert all(slots[s][0] == row for s in LEFT_SLOTS)
        lefts = [slots[s][1] for s in LEFT_SLOTS]
        stages = [[], [], [], []]
        for slot, (first, second) in enumerate(slots):
            for inner, outer, flip in [(first, second, 0), (second, first, 1)][: 1 if first == second else 2]:
                left = lefts.index(inner)
                stage = max(LEFT_STAGE[left], SLOT_STAGE[slot])
                base = (0, 0, X3, X4)[stage]
                key = max(slot, LEFT_SLOTS[left])
                stages[stage].append((key, (MULTIPLY, left, slot - base, flip, outer, 0)))
        stages = [[product for _, product in sorted(stage)] for stage in stages]
        first, touched = [], set()
        for product in stages[0]:
            if product[4] not in touched:
                first.append((ZERO, 0, 0, 0, product[4], 0))
            touched.add(product[4])
            first.append(product)
        first += [(ZERO, 0, 0, 0, total, 0) for total in range(4) if total not in touched]
        open_columns = sorted({product[4] for product in stages[3]})
        done_columns = [column for column in range(4) if column not in open_columns]
        assert len(open_columns) == 2

        def find(inner, outer):
            if (inner, outer) in slots:
                return slots.index((inner, outer)), 0
            return slots.index((outer, inner)), 1

        for core in range(2):
            early, early_slots = list(stages[2]), []
            early += [(ZERO, 0, 0, 0, 4 + which, 0) for which in range(2)]
            for k, column in enumerate(done_columns):
                early.append((FINISH, 4 + k, lefts.index(column), int(column == row), column, column))
            for which in range(2):
                for k, column in enumerate(done_columns):
                    slot, flip = find(column, 2 * col + which)
                    early.append((MULTIPLY, 4 + k, 2 + len(early_slots), flip, 4 + which, 0))
                    early_slots.append(slot)
                    if column == 2 * col + which:
                        early.append((LEVEL, 4 + k, 0, 0, 4 + which, column))
            late, late_slots = [], []
            for product in stages[3]:
                left = open_columns.index(lefts[product[1]])
                late.append((MULTIPLY, left) + product[2:])
            for k, column in enumerate(open_columns):
                late.append((FINISH, 2 + k, k, int(column == row), column, column))
            for k, which in enumerate((1 - core, core)):
                for m, column in enumerate(open_columns):
                    slot, flip = find(column, 2 * col + which)
                    late.append((MULTIPLY, 2 + m, 2 + len(late_slots), flip, 4 + which, 0))
                    late_slots.append(slot)
                    if column == 2 * col + which:
                        late.append((LEVEL, 2 + m, 0, 0, 4 + which, column))
                if k == 0:
                    late.append((SEND, 0, 0, 0, 4 + which, 0))
            own_rows = lambda slot: int(slot != core)
            straight = core == X_SENDS[0][row]
            second, last = Z_SENDS[1][row], X_SENDS[3][row]
            info = [
                core, row, col, core * 640,
                own_rows(X_SENDS[1][row]), (2 if straight else 3) if second == X1 else own_rows(second),
                0 if last == Z3 else (1 if straight else 2), int(straight),
            ] + [lefts.index(column) for column in open_columns] + open_columns
            devices.append(
                dict(
                    kernels=[first, stages[1], early, late],
                    slots=[early_slots, late_slots],
                    info=info,
                )
            )
    return devices


CORE, ROW, COL, FIRST_ROW, SEND_X2, SEND_Z2, SEND_LAST, STRAIGHT, OPEN_LEFT, OPEN = (*range(9), 10)


def device_tables(half):
    devices = device_lists()
    steps, rows = [], [[] for _ in devices]
    for kernel, (lefts, ahead) in enumerate((((0, 1, 2), 2), (range(4), 2), (range(4), 2), ((0, 1), 1))):
        length = max(len(device["kernels"][kernel]) for device in devices)
        steps.append((len(rows[0]), length))
        for row, device in zip(rows, devices):
            for fields in rows_of(device["kernels"][kernel], length, lefts, ahead):
                row += fields
    slots = []
    for kernel in range(2):
        slots.append(len(rows[0]))
        for row, device in zip(rows, devices):
            row += device["slots"][kernel]
    for device in devices:
        device["info"][FIRST_ROW] = device["info"][CORE] * half
    return [device["info"] for device in devices], rows, steps, slots


def bit_set(mask, bit):
    return jnp.bitwise_and(mask, jnp.int32(1 << bit)) != 0


class Worker:
    def __init__(self, table_ref, core, half, block_ref, block_sem, left_ref, left_sem, total_ref):
        self.table_ref, self.core, self.half = table_ref, core, half
        self.block_ref, self.block_sem = block_ref, block_sem
        self.left_ref, self.left_sem = left_ref, left_sem
        self.total_ref = total_ref
        self.near = pl.ds(pl.multiple_of(core * half, half), half)
        self.far = pl.ds(pl.multiple_of((1 - core) * half, half), half)
        self.blocks, self.lefts, self.send = {}, {}, None
        self.levels = None

    def load_halves(self, position, near_ref, far_ref):
        pltpu.make_async_copy(near_ref, self.block_ref.at[position, self.near], self.block_sem.at[position, 0]).start()
        pltpu.make_async_copy(far_ref, self.block_ref.at[position, self.far], self.block_sem.at[position, 1]).start()

    def load_block(self, position, slot, sources):
        self.blocks[position] = functools.partial(self.start_block, position, slot, sources)

    def start_block(self, position, slot, sources):
        for number, choices in sources.items():
            if isinstance(slot, int) and slot != number:
                continue
            for condition, near_ref, far_ref in choices:
                condition = slot == number if condition is None else jnp.logical_and(slot == number, condition)
                load = functools.partial(self.load_halves, position, near_ref, far_ref)
                if isinstance(condition, bool):
                    load()
                else:
                    pl.when(condition)(load)

    def own_sources(self, whole_ref, got_ref, other_ref):
        own = (whole_ref.at[self.near], whole_ref.at[self.far])
        return {
            slot: [(self.core == slot, *own), (self.core != slot, got_ref, other_ref)] for slot in (OWN0, OWN1)
        }

    def first_sources(self, straight, first, second, sibling_first, sibling_second):
        crossed = jnp.logical_not(straight)
        return {
            X1: [(straight, first, sibling_second), (crossed, second, sibling_first)],
            Z1: [(straight, sibling_first, second), (crossed, sibling_second, first)],
        }

    def load_left(self, index, number, refs):
        self.lefts[index] = functools.partial(self.start_left, index, number, refs)

    def left_places(self, refs):
        whole_ref, got_ref, straight, first, second = refs[:5]
        places = [(self.core, None, whole_ref.at[self.near]), (1 - self.core, None, got_ref)]
        places += [(2, straight, first), (2, jnp.logical_not(straight), second)]
        return places + [(3, None, ref) for ref in refs[5:]]

    def start_left(self, index, number, refs):
        for at, condition, ref in self.left_places(refs):
            if isinstance(at, int) and isinstance(number, int) and at != number:
                continue
            here = at == number
            if condition is not None:
                here = jnp.logical_and(here, condition)
            copy = functools.partial(self.copy_left, index, ref)
            if isinstance(here, bool):
                copy()
            else:
                pl.when(here)(copy)

    def copy_left(self, index, ref):
        pltpu.make_async_copy(ref, self.left_ref.at[index], self.left_sem.at[index]).start()

    def load_rows(self, refs):
        for k in range(len(refs) - 2):
            self.load_left(k, k, refs)

    def start(self, mask):
        for base, loads in ((LEFT_BIT, self.lefts), (BLOCK_BIT, self.blocks)):
            for index, load in loads.items():
                pl.when(bit_set(mask, base + index))(load)

    def wait(self, mask):
        half_block = self.block_ref.at[0, pl.ds(0, self.half)]
        for position in self.blocks:
            @pl.when(bit_set(mask, BLOCK_BIT + position))
            def _():
                for part in range(2):
                    pltpu.make_async_copy(half_block, half_block, self.block_sem.at[position, part]).wait()
        for index in self.lefts:
            @pl.when(bit_set(mask, LEFT_BIT + index))
            def _():
                pltpu.make_async_copy(self.left_ref.at[0], self.left_ref.at[0], self.left_sem.at[index]).wait()

    def multiply(self, field):
        total, left, block = self.total_ref.at[field[4]], self.left_ref.at[field[1]], self.block_ref.at[field[2]]

        @pl.when(field[3] == 0)
        def _():
            total[...] += jnp.dot(left[...], block[...], preferred_element_type=jnp.float32)

        @pl.when(field[3] == 1)
        def _():
            total[...] += lax.dot_general(
                left[...], block[...], (((1,), (1,)), ((), ())), preferred_element_type=jnp.float32
            )

    def tiles(self, cols_ref, column):
        lines = self.block_ref.shape[2] // 128
        return [jnp.broadcast_to(cols_ref[pl.ds(column * lines + m, 1), :], (16, 128)) for m in range(lines)]

    def finish(self, field):
        rows_ref, cols_ref, diag_ref = self.levels
        half = self.half
        total, left, made = self.total_ref.at[field[4]], self.left_ref.at[field[2]], self.left_ref.at[field[1]]
        cols = self.tiles(cols_ref, field[6])

        def one(index, carry):
            rows = pl.ds(pl.multiple_of(index * 16, 16), 16)
            level = rows_ref[rows, :]
            share = jnp.zeros((16, 128), jnp.float32)
            for m, col in enumerate(cols):
                at = slice(m * 128, (m + 1) * 128)
                ham = left[rows, at].astype(jnp.float32)
                square = total[rows, at] + ham * (level + col)
                made[rows, at] = square.astype(jnp.bfloat16)
                share = share + square * ham
            diag_ref[rows, :] += share
            return carry

        lax.fori_loop(0, half // 16, one, 0, unroll=2)

        @pl.when(field[3] == 1)
        def _():
            eye = lax.broadcasted_iota(jnp.int32, (128, 128), 0) == lax.broadcasted_iota(jnp.int32, (128, 128), 1)

            def fix(index, carry):
                rows = pl.ds(pl.multiple_of(index * 128, 128), 128)
                at = pl.ds(pl.multiple_of(self.core * half + index * 128, 128), 128)
                col = cols_ref[pl.ds((2 * field[6] + self.core) * (half // 128) + index, 1), :]
                level = rows_ref[rows, :]
                ham = left[rows, at].astype(jnp.float32)
                square = total[rows, at] + ham * (level + col)
                full = square + jnp.where(eye, level * level, 0.0)
                made[rows, at] = full.astype(jnp.bfloat16)
                diag_ref[rows, :] += jnp.where(eye, full * (ham + level) - square * ham, 0.0)
                return carry

            lax.fori_loop(0, half // 128, fix, 0)

    def add_level(self, field):
        cols = self.tiles(self.levels[1], field[6])
        total, left = self.total_ref.at[field[4]], self.left_ref.at[field[1]]

        def one(index, carry):
            rows = pl.ds(pl.multiple_of(index * 16, 16), 16)
            for m, col in enumerate(cols):
                at = slice(m * 128, (m + 1) * 128)
                total[rows, at] += left[rows, at].astype(jnp.float32) * col
            return carry

        lax.fori_loop(0, self.half // 16, one, 0, unroll=2)

    def clear(self, field):
        self.total_ref[field[4]] = jnp.zeros_like(self.total_ref[0])

    def run(self, start_count):
        start, count = start_count
        works = [(MULTIPLY, self.multiply), (ZERO, self.clear)]
        if self.levels is not None:
            works += [(FINISH, self.finish), (LEVEL, self.add_level)]
        if self.send is not None:
            works.append((SEND, self.send))

        def step(index, carry):
            field = [self.table_ref[start + index * FIELDS + k] for k in range(8)]
            pl.when(field[7] != 0)(functools.partial(self.start, field[7]))
            pl.when(field[5] != 0)(functools.partial(self.wait, field[5]))
            for kind, work in works:
                pl.when(field[0] == kind)(functools.partial(work, field))
            return carry

        lax.fori_loop(0, count, step, 0)


def take_inputs(refs, last):
    count = 7 + 2 * max(last - Z1, 0)
    return list(refs[:count]), list(refs[count:])


def use_inputs(worker, info_ref, inputs):
    own, first, rest = inputs[:3], inputs[3:7], inputs[7:]
    straight = info_ref[STRAIGHT] == 1
    sources = {**worker.own_sources(*own), **worker.first_sources(straight, *first)}
    for k in range(len(rest) // 2):
        sources[X2 + k] = [(None, rest[2 * k], rest[2 * k + 1])]
    return [own[0], own[1], straight, first[0], first[1]] + rest[:1], sources


def square_kernel(first, steps, left_count, slots, table_ref, info_ref, *refs):
    inputs, refs = take_inputs(refs, slots[-1])
    refs = refs[0 if first else 2 :]
    total_ref, token_ref, block_ref, block_sem, left_ref, left_sem = refs
    half = left_ref.shape[1]
    worker = Worker(table_ref, info_ref[CORE], half, block_ref, block_sem, left_ref, left_sem, total_ref)
    row_refs, sources = use_inputs(worker, info_ref, inputs)
    worker.load_rows(row_refs[: left_count + 2])
    for position, slot in enumerate(slots):
        worker.load_block(position, slot, sources)
    worker.run(steps)
    token_ref[...] = jnp.zeros_like(token_ref)


def early_kernel(steps, slots_at, table_ref, info_ref, *refs):
    inputs, refs = take_inputs(refs, Z3)
    _, _, level_rows_ref, level_ref, total_ref, diag_ref = (refs.pop(0) for _ in range(6))
    block_ref, block_sem, left_ref, left_sem = refs
    half = left_ref.shape[1]
    worker = Worker(table_ref, info_ref[CORE], half, block_ref, block_sem, left_ref, left_sem, total_ref)
    worker.levels = (level_rows_ref, level_ref, diag_ref)
    row_refs, sources = use_inputs(worker, info_ref, inputs)
    worker.load_rows(row_refs)
    worker.load_block(0, X3, sources)
    worker.load_block(1, Z3, sources)
    for k in range(4):
        worker.load_block(2 + k, table_ref[slots_at + k], sources)
    diag_ref[...] = jnp.zeros_like(diag_ref)
    worker.run(steps)


def late_kernel(steps, slots_at, table_ref, info_ref, gain_ref, *refs):
    inputs, refs = take_inputs(refs, Z4)
    _, old_diag_ref, level_rows_ref, level_ref, total_ref, cube_ref, density_ref, cube_diag_ref = (
        refs.pop(0) for _ in range(8)
    )
    block_ref, block_sem, left_ref, left_sem, out_sem, sent_ref, ham_ref, ham_sem, diag_ref = refs
    half, width = left_ref.shape[1:]
    core, row, col = info_ref[CORE], info_ref[ROW], info_ref[COL]
    worker = Worker(table_ref, core, half, block_ref, block_sem, left_ref, left_sem, total_ref)
    worker.levels = (level_rows_ref, level_ref, diag_ref)
    row_refs, sources = use_inputs(worker, info_ref, inputs)
    worker.load_block(0, X4, sources)
    worker.load_block(1, Z4, sources)
    for k in range(2):
        worker.load_left(k, info_ref[OPEN_LEFT + k], row_refs)
    for k in range(4):
        worker.load_block(2 + k, table_ref[slots_at + k], sources)
    ham_copy = pltpu.make_async_copy(row_refs[0].at[worker.near], ham_ref, ham_sem)
    sent_copy = pltpu.make_async_copy(sent_ref, cube_ref, out_sem.at[0])
    parts = 5
    rows_each = half // parts

    def density_copy(part):
        rows = pl.ds(pl.multiple_of(part * rows_each, rows_each), rows_each)
        to = pl.ds(pl.multiple_of(core * half + part * rows_each, rows_each), rows_each)
        return pltpu.make_async_copy(total_ref.at[4 + core, rows], density_ref.at[to], out_sem.at[1])

    def send(field):
        sent_ref[...] = total_ref[field[4]].astype(sent_ref.dtype)
        sent_copy.start()
        ham_copy.start()

    worker.send = send
    diag_ref[...] = old_diag_ref[...]
    worker.run(steps)
    ham_copy.wait()
    gain = gain_ref[0]
    linear, cubic = -1.5 * gain, 2.0 * (gain * gain * gain)

    eye = lax.broadcasted_iota(jnp.int32, (128, 128), 0) == lax.broadcasted_iota(jnp.int32, (128, 128), 1)

    def one_part(part, carry):
        def one(index, carry):
            rows = pl.ds(pl.multiple_of(part * rows_each + index * 16, 16), 16)
            for m in range(width // 128):
                at = slice(m * 128, (m + 1) * 128)
                cube = total_ref[4 + core, rows, at]
                total_ref[4 + core, rows, at] = linear * ham_ref[rows, at].astype(jnp.float32) + cubic * cube
            return carry

        lax.fori_loop(0, rows_each // 16, one, 0, unroll=2)

        @pl.when(row == 2 * col + core)
        def _():
            rows = pl.ds(pl.multiple_of(part * rows_each, rows_each), rows_each)
            at = pl.ds(pl.multiple_of(core * half + part * rows_each, rows_each), rows_each)
            total_ref[4 + core, rows, at] += jnp.where(eye, 0.5 + linear * level_rows_ref[rows, :], 0.0)

        density_copy(part).start()
        return carry

    lax.fori_loop(0, parts, one_part, 0)
    lines = half // 128
    cube_diag_ref[...] = jnp.zeros_like(cube_diag_ref)
    for k in range(lines):
        share = jnp.sum(diag_ref[pl.ds(k * 128, 128), :].T, 0, keepdims=True)
        cube_diag_ref[pl.ds((2 * row + core) * lines + k, 1), :] = share
    sent_copy.wait()
    for part in range(parts):
        density_copy(part).wait()


HERE = pl.BlockSpec(memory_space=pltpu.HBM)
SCALARS = pl.BlockSpec(memory_space=pltpu.SMEM)
VMEM = pl.BlockSpec(memory_space=pltpu.VMEM)
VMEM_BYTES = 38 * 2**20


def in_hbm(values):
    return [pltpu.with_memory_space_constraint(value, pltpu.HBM) for value in values]


def work_scratch(half, width, blocks, lefts):
    return [
        pltpu.VMEM((blocks, 2 * half, width), jnp.bfloat16),
        pltpu.SemaphoreType.DMA((blocks, 2)),
        pltpu.VMEM((lefts, half, width), jnp.bfloat16),
        pltpu.SemaphoreType.DMA((lefts,)),
    ]


def call_kernel(name, kernel, shape, scalars, operands, totals, in_vmem, out_shape, out_specs, scratch):
    first = len(scalars) + len(operands)
    held = [] if totals is None else [pltpu.with_memory_space_constraint(totals, pltpu.VMEM)]
    return pl.pallas_call(
        kernel,
        out_shape=(pltpu.VMEM((6,) + shape, jnp.float32),) + tuple(out_shape),
        in_specs=[SCALARS] * len(scalars) + [HERE] * len(operands) + [VMEM] * (len(held) + len(in_vmem)),
        out_specs=(VMEM,) + tuple(out_specs),
        scratch_shapes=scratch,
        input_output_aliases={first: 0} if held else {},
        compiler_params=pltpu.CompilerParams(vmem_limit_bytes=VMEM_BYTES),
        name=name,
    )(*scalars, *in_hbm(operands), *held, *in_vmem)


def pick_kernel(choices, whole, count, info_ref, *refs):
    sources, outs, in_sem = refs[:count], refs[count:-1], refs[-1]
    parts = in_sem.shape[1]
    size = outs[0].shape[0] // parts
    for part in range(parts):
        for k, choice in enumerate(choices):
            to = outs[k].at[pl.ds(part * size, size)]
            for number, source in enumerate(sources):
                @pl.when(info_ref[choice] == number)
                def _():
                    first = part * size
                    if number < whole:
                        first = pl.multiple_of(info_ref[FIRST_ROW] + first, size)
                    pltpu.make_async_copy(source.at[pl.ds(first, size)], to, in_sem.at[k, part]).start()
    for part in range(parts):
        for k, out_ref in enumerate(outs):
            to = out_ref.at[pl.ds(part * size, size)]
            pltpu.make_async_copy(to, to, in_sem.at[k, part]).wait()


def pick(info, choices, sources, whole, shape):
    parts = 4
    return pl.pallas_call(
        functools.partial(pick_kernel, choices, whole, len(sources)),
        out_shape=[pltpu.VMEM(shape, sources[0].dtype)] * len(choices),
        in_specs=[SCALARS] + [HERE] * len(sources),
        out_specs=[VMEM] * len(choices),
        scratch_shapes=[pltpu.SemaphoreType.DMA((len(choices), parts))],
        compiler_params=pltpu.CompilerParams(vmem_limit_bytes=8 * 2**20),
        name="pick",
    )(info, *in_hbm(sources))


def pairs_kernel(spots_ref, points_ref, out_ref, weight_ref, wide_ref):
    count, width = points_ref.shape[0], spots_ref.shape[1]
    tiles = width // 128

    @pl.when(pl.program_id(0) == 0)
    def _():
        for k in range(4):
            wide_ref[k] = jnp.broadcast_to(points_ref[:, k : k + 1], (count, 128))

    lanes = [slice(m * 128, (m + 1) * 128) for m in range(tiles)]
    spots = [[jnp.broadcast_to(spots_ref[k : k + 1, at], (16, 128)) for k in range(3)] for at in lanes]

    def step(group, sums):
        rows = pl.ds(pl.multiple_of(group * 16, 16), 16)
        px, py, pz, charge = (wide_ref[k, rows, :] for k in range(4))
        sums = list(sums)
        for m, at in enumerate(lanes):
            dx, dy, dz = spots[m][0] - px, spots[m][1] - py, spots[m][2] - pz
            inv = lax.rsqrt(dx * dx + dy * dy + dz * dz + 1.0)
            sums[m] = sums[m] + charge * inv
            weight_ref[rows, at] = (inv * (inv * inv)).astype(jnp.bfloat16)
        return tuple(sums)

    zeros = tuple(jnp.zeros((16, 128), jnp.float32) for _ in range(tiles))
    sums = lax.fori_loop(0, count // 16, step, zeros, unroll=2)
    for m, at in enumerate(lanes):
        out_ref[:, at] = jnp.sum(sums[m], 0, keepdims=True)


def pair_terms(centers, points):
    total, count = centers.shape[1], points.shape[0]
    width = 512
    part = jax.ShapeDtypeStruct((count, total), jnp.bfloat16)
    return pl.pallas_call(
        pairs_kernel,
        grid=(total // width,),
        out_shape=(jax.ShapeDtypeStruct((1, total), jnp.float32), part),
        in_specs=[pl.BlockSpec((3, width), lambda i: (0, i)), pl.BlockSpec((count, 4), lambda i: (0, 0))],
        out_specs=[pl.BlockSpec((1, width), lambda i: (0, i))] + [pl.BlockSpec((count, width), lambda i: (0, i))],
        scratch_shapes=[pltpu.VMEM((4, count, 128), jnp.float32)],
        compiler_params=pltpu.CompilerParams(vmem_limit_bytes=VMEM_BYTES),
        name="pairs",
    )(centers, points)


def levels_kernel(info_ref, near_ref, far_ref, gain_ref, level_ref, above_ref, rows_ref):
    lines = level_ref.shape[0]
    sums = near_ref[...] + far_ref[...]
    potential, diag = sums[0:lines], sums[lines : 2 * lines] + sums[0:lines]
    total = float(lines * 128)
    mean = jnp.sum(diag) / total
    above = diag - mean
    squares = (jnp.sum(sums[2 * lines : 2 * lines + 1]) / 128.0 + jnp.sum(above * above)) / total
    spread = jnp.sqrt(jnp.full((8, 128), squares + 1e-05, jnp.float32))
    gain_ref[0] = jnp.max(1.0 / (3.0 * spread))
    level_ref[...] = potential - mean
    above_ref[...] = above
    half = rows_ref.shape[0]
    first = (2 * info_ref[ROW] + info_ref[CORE]) * (half // 128)
    for k in range(half // 128):
        line = level_ref[pl.ds(first + k, 1), :]
        rows_ref[pl.ds(k * 128, 128), :] = jnp.broadcast_to(line, (128, 128)).T


def level_terms(info, parts, lines, half):
    line = jax.ShapeDtypeStruct((lines, 128), jnp.float32)
    return pl.pallas_call(
        levels_kernel,
        out_shape=(jax.ShapeDtypeStruct((1,), jnp.float32), line, line, jax.ShapeDtypeStruct((half, 128), jnp.float32)),
        in_specs=[SCALARS] + [VMEM] * 2,
        out_specs=(SCALARS, VMEM, VMEM, VMEM),
        compiler_params=pltpu.CompilerParams(vmem_limit_bytes=4 * 2**20),
        name="levels",
    )(info, *parts)


MIDDLE = 10.0


def pull_kernel(gain_ref, spots_ref, above_ref, near_ref, far_ref, weight_ref, coords_ref, charge_ref, out_ref, total_ref):
    gain = gain_ref[0]
    lines = 10
    width = lines * 128

    def one(index, carry):
        lanes = pl.ds(pl.multiple_of(index * width, width), width)
        pieces = []
        for m in range(lines):
            line = pl.ds(index * lines + m, 1)
            cube = near_ref[line, :] + far_ref[line, :]
            pieces.append(0.5 - 1.5 * gain * above_ref[line, :] + 2.0 * (gain * gain * gain) * cube)
        occ = jnp.concatenate(pieces, 1)
        weights = [occ] + [occ * (spots_ref[k : k + 1, lanes] - MIDDLE) for k in range(3)]
        stacked = jnp.concatenate(weights + [jnp.zeros((4, width), jnp.float32)], 0)
        high = stacked.astype(jnp.bfloat16)
        low = (stacked - high.astype(jnp.float32)).astype(jnp.bfloat16)
        both = jnp.concatenate([high, low, jnp.zeros((128 - 16, width), jnp.bfloat16)], 0)
        total_ref[...] += lax.dot_general(
            weight_ref[:, lanes], both, (((1,), (1,)), ((), ())), preferred_element_type=jnp.float32
        )
        return carry

    total_ref[...] = jnp.zeros_like(total_ref)
    lax.fori_loop(0, spots_ref.shape[1] // width, one, 0)
    sums = total_ref[...].T
    sums = sums[0:8] + sums[8:16]
    for k in range(3):
        pull = (coords_ref[k : k + 1, :] - MIDDLE) * sums[0:1] - sums[k + 1 : k + 2]
        out_ref[k : k + 1, :] = -charge_ref[...] * pull


def pull_terms(gain, centers, above, near, far, weights, mm_coords, mm_charges):
    count = mm_coords.shape[1]
    return pl.pallas_call(
        pull_kernel,
        out_shape=jax.ShapeDtypeStruct((3, count), jnp.float32),
        in_specs=[SCALARS] + [VMEM] * 7,
        out_specs=VMEM,
        scratch_shapes=[pltpu.VMEM((count, 128), jnp.float32)],
        compiler_params=pltpu.CompilerParams(vmem_limit_bytes=16 * 2**20),
        name="pull",
    )(
        gain, centers, above, near, far, pltpu.with_memory_space_constraint(weights, pltpu.VMEM), mm_coords,
        mm_charges[None],
    )


def density_kernel(steps, info_ref, gain_ref, ham_ref, far_ref, level_ref, _, out_ref):
    index = pl.program_id(0)
    core, row, col = info_ref[CORE], info_ref[ROW], info_ref[COL]
    gain = gain_ref[0]
    height, width = out_ref.shape
    linear, cubic = -1.5 * gain, 2.0 * (gain * gain * gain)
    first = ((1 - core) * steps + index) * height

    def one(k, carry):
        rows = pl.ds(pl.multiple_of(k * 16, 16), 16)
        for m in range(width // 128):
            at = slice(m * 128, (m + 1) * 128)
            cube = far_ref[rows, at].astype(jnp.float32)
            out_ref[rows, at] = linear * ham_ref[rows, at].astype(jnp.float32) + cubic * cube
        return carry

    lax.fori_loop(0, height // 16, one, 0, unroll=2)

    @pl.when(row == 2 * col + core)
    def _():
        eye = lax.broadcasted_iota(jnp.int32, (128, 128), 0) == lax.broadcasted_iota(jnp.int32, (128, 128), 1)

        def fix(k, carry):
            rows = pl.ds(pl.multiple_of(k * 128, 128), 128)
            at = pl.ds(pl.multiple_of(first + k * 128, 128), 128)
            line = pl.ds((2 * col + core) * (width // 128) + first // 128 + k, 1)
            out_ref[rows, at] += jnp.where(eye, 0.5 + linear * level_ref[line, :], 0.0)
            return carry

        lax.fori_loop(0, height // 128, fix, 0)


def density_rest(info, gain, ham, far, level, density):
    height, width = ham.shape
    steps = 1
    chunk = far.shape[0] // steps
    return pl.pallas_call(
        functools.partial(density_kernel, steps),
        grid_spec=pltpu.PrefetchScalarGridSpec(
            num_scalar_prefetch=1,
            grid=(steps,),
            in_specs=[
                SCALARS,
                pl.BlockSpec((chunk, width), lambda i, info: ((1 - info[CORE]) * steps + i, 0)),
                pl.BlockSpec((chunk, width), lambda i, info: (i, 0)),
                pl.BlockSpec(level.shape, lambda i, info: (0, 0)),
                HERE,
            ],
            out_specs=pl.BlockSpec((chunk, width), lambda i, info: ((1 - info[CORE]) * steps + i, 0)),
        ),
        out_shape=jax.ShapeDtypeStruct((height, width), jnp.float32),
        input_output_aliases={5: 0},
        compiler_params=pltpu.CompilerParams(vmem_limit_bytes=VMEM_BYTES),
        name="density",
    )(info, gain, ham, far, level, density)


def gossip_shards(sizes, h_core, centers, mm_coords, mm_charges):
    height, width = h_core.shape
    half = height // 2
    total, count = centers.shape[1], mm_coords.shape[1]
    row, col, core = (lax.axis_index(name) for name in ("sec", "col", "rep"))
    row_start = row * height
    col_start = (2 * col + core) * width
    infos, rows, steps, slots_at = device_tables(half)
    device = 4 * row + 2 * col + core
    info, table = (
        lax.dynamic_index_in_dim(jnp.asarray(values, jnp.int32), device, 0, keepdims=False) for values in (infos, rows)
    )

    def over_rep(value):
        return lax.ppermute(value, "rep", [(0, 1), (1, 0)])

    def over_col(value):
        return lax.ppermute(value, "col", [(0, 1), (1, 0)])

    def over_sec(value, step):
        moves = [(2 * start + x, 2 * to + x) for x in range(2) for start, to in Z_MOVES[step][x]]
        return lax.ppermute(value, ("sec", "col"), moves)

    def over_both(value, own):
        moves = []
        for z, x, c in ((z, x, c) for z in range(4) for x in range(2) for c in range(2)):
            if (c if own else 1 - c) == X_SENDS[0][z]:
                to = (z, 1 - x, c)
            else:
                to = (dict(Z_MOVES[0][x])[z], x, 1 - c)
            moves.append((4 * z + 2 * x + c, 4 * to[0] + 2 * to[1] + to[2]))
        return lax.ppermute(value, ("sec", "col", "rep"), moves)

    def swap_all(values):
        return [(value, over_rep(value)) for value in values]

    def flat(groups):
        return [value for group in groups for value in group]

    def after(arrived, work):
        return lax.optimization_barrier((arrived, work))

    shape = (half, width)
    near = lax.dynamic_slice_in_dim(h_core, core * half, half, 0)
    far = lax.dynamic_slice_in_dim(h_core, (1 - core) * half, half, 0)
    got = over_rep(far)
    firsts = (over_both(near, True), over_both(got, False))
    other = over_rep(near)
    points = jnp.concatenate([mm_coords, mm_charges[None]], 0).T
    terms, weights = pair_terms(centers, points)
    rows_glob = row_start + lax.broadcasted_iota(jnp.int32, (height, width), 0)
    cols_glob = col_start + lax.broadcasted_iota(jnp.int32, (height, width), 1)
    on_diag = rows_glob == cols_glob
    wide = h_core.astype(jnp.float32)
    own_diag = jnp.sum(jnp.where(on_diag, wide, 0.0), 0)
    own_off = jnp.sum(jnp.where(on_diag, 0.0, wide * wide))
    diag = lax.dynamic_update_slice_in_dim(jnp.zeros((total,), jnp.float32), own_diag, col_start, 0)
    packed = jnp.concatenate([terms[0], diag, jnp.full((8 * 128,), own_off)]).reshape(-1, 128)
    packed = packed + over_rep(packed)
    from_col = over_col(packed)
    (firsts, from_col), (packed, weights, table, other) = after((firsts, from_col), (packed, weights, table, other))
    own_parts = [h_core, got, other]
    sends = pick(info, (SEND_X2, SEND_Z2), (h_core, got) + tuple(firsts), 1, shape)
    firsts, sends = lax.optimization_barrier((list(firsts), sends))
    x2 = over_col(sends[0])
    z2 = over_sec(sends[1], 1)
    packed = packed + from_col
    from_near = lax.ppermute(packed, "sec", [(i, i ^ 1) for i in range(4)])
    operands = own_parts + firsts + [over_rep(first) for first in firsts]

    def grow_square(stage, left_count, slots, totals, token):
        kernel = functools.partial(square_kernel, totals is None, steps[stage], left_count, slots)
        return call_kernel(
            f"square_{stage}", kernel, shape, (table, info), operands + ([] if token is None else [token]), totals, (),
            (jax.ShapeDtypeStruct((8, 128), jnp.float32),), (VMEM,), work_scratch(half, width, len(slots), 4),
        )

    totals, token = grow_square(0, 3, (OWN0, OWN1, X1, Z1), None, None)
    (x2, z2, from_near), (token, packed) = after((x2, z2, from_near), (token, packed))
    x3 = over_col(z2)
    z3 = over_sec(x2, 2)
    operands = operands + flat(swap_all((x2, z2)))
    totals, token = grow_square(1, 4, (OWN0, OWN1, X1, Z1, X2, Z2), totals, token)
    packed = packed + from_near
    from_far = lax.ppermute(packed, "sec", [(i, i ^ 2) for i in range(4)])
    (x3, z3, from_far), (token, packed) = after((x3, z3, from_far), (token, packed))
    last_send = pick(info, (SEND_LAST,), [z3] + operands[5:7], 0, shape)[0]
    (x3, z3), last_send = after((x3, z3), last_send)
    x4 = over_col(last_send)
    z4 = over_sec(last_send, 3)
    operands = operands + flat(swap_all((x3, z3)))
    gain, level, above, level_rows = level_terms(info, [packed, from_far], total // 128, half)
    lines = jax.ShapeDtypeStruct((total // 128, 128), jnp.float32)
    share = jax.ShapeDtypeStruct((half, 128), jnp.float32)
    totals, cube_diag = call_kernel(
        "early_cube", functools.partial(early_kernel, steps[2], slots_at[0]), shape, (table, info),
        operands + [token], totals, (level_rows, level),
        (share,), (VMEM,), work_scratch(half, width, 6, 6),
    )
    (x4, z4), (cube_diag, above, level_rows, level, gain) = after(
        (x4, z4), (cube_diag, above, level_rows, level, gain)
    )
    operands = operands + flat(swap_all((x4, z4)))
    _, sibling, density, cube_diag = call_kernel(
        "late_cube", functools.partial(late_kernel, steps[3], slots_at[1]), shape, (table, info, gain),
        operands, totals, (cube_diag, level_rows, level),
        (jax.ShapeDtypeStruct(shape, jnp.bfloat16), jax.ShapeDtypeStruct((height, width), jnp.float32), lines),
        (HERE, HERE, VMEM),
        work_scratch(half, width, 6, 4)
        + [
            pltpu.SemaphoreType.DMA((2,)),
            pltpu.VMEM(shape, jnp.bfloat16),
            pltpu.VMEM(shape, jnp.bfloat16),
            pltpu.SemaphoreType.DMA,
            pltpu.VMEM((half, 128), jnp.float32),
        ],
    )
    sibling = over_rep(sibling)
    cube_diag = cube_diag + over_rep(cube_diag)
    cube_diag = cube_diag + lax.ppermute(cube_diag, "sec", [(i, i ^ 1) for i in range(4)])
    from_far = lax.ppermute(cube_diag, "sec", [(i, i ^ 2) for i in range(4)])
    density = density_rest(info, gain, h_core, sibling, level, density)
    from_far, density = after(from_far, density)
    forces = pull_terms(gain, centers, above, cube_diag, from_far, weights, mm_coords, mm_charges)
    return (density, forces)


def solution(mesh):
    in_specs = (
        P(("groups", "sec"), ("col", "rep")),
        P(None, "groups"),
        P(None, ("groups", "sec", "col", "rep")),
        P(("groups", "sec", "col", "rep")),
    )
    out_specs = (P(("groups", "sec"), ("col", "rep")), P(None, ("groups", "sec", "col", "rep")))
    sizes = dict(mesh.shape)
    small = (sizes["sec"], sizes["col"], sizes["rep"]) == (4, 2, 2)
    body = functools.partial(gossip_shards if small else gather_shards, sizes)
    return jax.shard_map(body, mesh=mesh, in_specs=in_specs, out_specs=out_specs, check_vma=False)
```

```python
import functools

import jax
import jax.numpy as jnp
from jax import lax
from jax.experimental import pallas as pl
from jax.experimental.pallas import tpu as pltpu
from jax.sharding import PartitionSpec as P

PART = ("sec", "col", "rep")


def potential_kernel(spots_ref, points_ref, out_ref):
    count = points_ref.shape[0]
    width = spots_ref.shape[1]
    sx, sy, sz = (spots_ref[k : k + 1, :] for k in range(3))

    def step(index, accum):
        rows = points_ref[pl.ds(pl.multiple_of(index * 8, 8), 8), :]
        dx = sx - rows[:, 0:1]
        dy = sy - rows[:, 1:2]
        dz = sz - rows[:, 2:3]
        dist = dx * dx + dy * dy + dz * dz + 1.0
        return accum + rows[:, 3:4] * lax.rsqrt(dist)

    total = lax.fori_loop(0, count // 8, step, jnp.zeros((8, width), jnp.float32), unroll=4)
    out_ref[...] = jnp.sum(total, 0, keepdims=True)


def potential_terms(centers, mm_coords, mm_charges):
    total = centers.shape[1]
    count = mm_coords.shape[1]
    width = 1024 if total % 1024 == 0 else total
    points = jnp.concatenate([mm_coords, mm_charges[None]], 0).T
    return pl.pallas_call(
        potential_kernel,
        grid=(total // width,),
        out_shape=jax.ShapeDtypeStruct((1, total), jnp.float32),
        in_specs=[
            pl.BlockSpec((3, width), lambda i: (0, i)),
            pl.BlockSpec((count, 4), lambda i: (0, 0)),
        ],
        out_specs=pl.BlockSpec((1, width), lambda i: (0, i)),
        name="potential",
    )(centers, points)


def force_kernel(spots_ref, occ_ref, points_ref, out_ref):
    total = spots_ref.shape[1]
    rows = points_ref[...]
    px, py, pz, charge = (rows[:, k : k + 1] for k in range(4))
    count = rows.shape[0]

    def step(index, accum):
        lanes = pl.ds(pl.multiple_of(index * 128, 128), 128)
        dx = px - spots_ref[0:1, lanes]
        dy = py - spots_ref[1:2, lanes]
        dz = pz - spots_ref[2:3, lanes]
        inv = lax.rsqrt(dx * dx + dy * dy + dz * dz + 1.0)
        weight = occ_ref[:, lanes] * inv * (inv * inv)
        return (accum[0] + dx * weight, accum[1] + dy * weight, accum[2] + dz * weight)

    zero = jnp.zeros((count, 128), jnp.float32)
    sums = lax.fori_loop(0, total // 128, step, (zero, zero, zero), unroll=4)
    for k in range(3):
        out_ref[:, k : k + 1] = -charge * jnp.sum(sums[k], 1, keepdims=True)


def force_terms(centers, occupation, mm_coords, mm_charges):
    total = centers.shape[1]
    count = mm_coords.shape[1]
    width = 32
    points = jnp.concatenate([mm_coords, mm_charges[None]], 0).T
    summed = pl.pallas_call(
        force_kernel,
        grid=(count // width,),
        out_shape=jax.ShapeDtypeStruct((count, 4), jnp.float32),
        in_specs=[
            pl.BlockSpec((3, total), lambda i: (0, 0)),
            pl.BlockSpec((1, total), lambda i: (0, 0)),
            pl.BlockSpec((width, 4), lambda i: (i, 0)),
        ],
        out_specs=pl.BlockSpec((width, 4), lambda i: (i, 0)),
        name="forces",
    )(centers, occupation, points)
    return summed[:, :3].T


def butterfly_sum(value, sizes, axes=("rep", "col", "sec")):
    for axis in axes:
        size = sizes[axis]
        if size & (size - 1):
            value = lax.psum(value, axis)
            continue
        hop = 1
        while hop < size:
            value = value + lax.ppermute(value, axis, [(i, i ^ hop) for i in range(size)])
            hop *= 2
    return value


def fold_with(left, piece):
    return jnp.dot(left, piece, preferred_element_type=jnp.float32)


def gather_shards(sizes, h_core, centers, mm_coords, mm_charges):
    row_count, col_count = h_core.shape
    total = centers.shape[1]
    row_start = lax.axis_index("sec") * row_count
    col_start = lax.axis_index(("col", "rep")) * col_count
    rows_glob = row_start + lax.broadcasted_iota(jnp.int32, (row_count, col_count), 0)
    cols_glob = col_start + lax.broadcasted_iota(jnp.int32, (row_count, col_count), 1)
    on_diag = rows_glob == cols_glob
    off = jnp.where(on_diag, jnp.zeros((), h_core.dtype), h_core)
    row_panel = lax.all_gather(off, ("col", "rep"), axis=1, tiled=True)
    col_panel = lax.all_gather(off, "sec", axis=0, tiled=True)

    wide = h_core.astype(jnp.float32)
    own_diag = jnp.sum(jnp.where(on_diag, wide, 0.0), 0)
    own_off = jnp.sum(jnp.where(on_diag, 0.0, wide * wide))
    terms = potential_terms(centers, mm_coords, mm_charges)[0]
    own_cols = lax.dynamic_slice_in_dim(terms, col_start, col_count, 0) + own_diag
    terms = lax.dynamic_update_slice_in_dim(terms, own_cols, col_start, 0)
    sums = butterfly_sum(jnp.concatenate([terms, jnp.full((128,), own_off)]), sizes)
    diag_vals, off_total = sums[:total], sums[total]
    mean_level = jnp.sum(diag_vals) / total
    level = diag_vals - mean_level
    spread = jnp.sqrt((off_total + jnp.sum(level * level)) / total + 1e-05)
    gain = 1.0 / (3.0 * spread)

    level_rows = lax.dynamic_slice_in_dim(level, row_start, row_count, 0)[:, None]
    level_cols = lax.dynamic_slice_in_dim(level, col_start, col_count, 0)[None, :]
    off_wide = off.astype(jnp.float32)
    square = fold_with(row_panel, col_panel)
    square = square + off_wide * (level_rows + level_cols) + jnp.where(on_diag, level_rows * level_rows, 0.0)
    shifted = off_wide + jnp.where(on_diag, level_rows, 0.0)
    square_b = square.astype(jnp.bfloat16)
    square_panel = lax.all_gather(square_b, ("col", "rep"), axis=1, tiled=True)
    own_cube = jnp.sum(square * shifted, 0)
    cube_diag = lax.dynamic_update_slice_in_dim(jnp.zeros((total,), jnp.float32), own_cube, col_start, 0)
    cube_diag = butterfly_sum(cube_diag, sizes)
    occupation = 0.5 - 1.5 * gain * level + 2.0 * gain**3 * cube_diag
    forces = force_terms(centers, occupation[None], mm_coords, mm_charges)

    cube = fold_with(square_panel, col_panel) + square_b.astype(jnp.float32) * level_cols
    density = jnp.where(on_diag, 0.5, 0.0) - 1.5 * gain * shifted + 2.0 * gain**3 * cube
    return (density, forces)


ROUND = ((0, 1), (1, 2), (2, 3), (3, 0))
BACK = ((0, 3), (3, 2), (2, 1), (1, 0))
Z_MOVES = ((ROUND, BACK), (BACK, ROUND), (ROUND, BACK), (ROUND, BACK))
OWN0, OWN1, X1, Z1, X2, Z2, X3, Z3, X4, Z4 = range(10)
X_SENDS = ((OWN1, OWN0, OWN1, OWN0), (OWN0, OWN1, OWN0, OWN1), (Z2,) * 4, (Z3, Z1, Z1, Z3))
Z_SENDS = ((OWN0, OWN1, OWN0, OWN1), (OWN1, X1, X1, OWN0), (X2,) * 4, (Z3, Z1, Z1, Z3))
SLOT_STAGE = (0, 0, 0, 0, 1, 1, 2, 2, 3, 3)
LEFT_SLOTS = (OWN0, OWN1, X1, X2)
LEFT_STAGE = (0, 0, 0, 1)
FIELDS = 10
NOTHING, MULTIPLY, FINISH, LEVEL, SEND, ZERO = range(6)
BLOCK_BIT, LEFT_BIT = 0, 8


def block_places():
    chips = [(z, x) for z in range(4) for x in range(2)]
    held = {(z, x): [(z, 2 * x), (z, 2 * x + 1)] for z, x in chips}
    for step in range(4):
        arrived = {}
        for z, x in chips:
            before = next(start for start, to in Z_MOVES[step][x] if to == z)
            arrived[(z, x)] = [held[(z, 1 - x)][X_SENDS[step][z]], held[(before, x)][Z_SENDS[step][before]]]
        for chip in chips:
            held[chip] = held[chip] + arrived[chip]
    return [held[chip] for chip in chips]


def rows_of(products, length, lefts, ahead):
    seen, firsts = set(), []
    for kind, left, block, flip, total, column in products:
        bits = []
        if kind in (MULTIPLY, FINISH, LEVEL):
            loaded_left = block if kind == FINISH else left
            if loaded_left in lefts:
                bits.append(LEFT_BIT + loaded_left)
        if kind == MULTIPLY:
            bits.append(BLOCK_BIT + block)
        firsts.append([bit for bit in dict.fromkeys(bits) if bit not in seen])
        seen.update(bits)
    mask = lambda bits: sum(1 << bit for bit in bits)
    waves = [k for k, first in enumerate(firsts) if first]
    starts = [[] for _ in products]
    for number, k in enumerate(waves):
        at = 0 if number <= ahead else waves[number - ahead]
        starts[at] += firsts[k]
    rows = []
    for k, (kind, left, block, flip, total, column) in enumerate(products):
        rows.append([kind, left, block, flip, total, mask(firsts[k]), column, mask(starts[k]), 0, 0])
    return rows + [[NOTHING] + [0] * (FIELDS - 1)] * (length - len(rows))


def device_lists():
    devices = []
    for chip, slots in enumerate(block_places()):
        assert len({tuple(sorted(place)) for place in slots}) == 10
        row, col = divmod(chip, 2)
        assert all(slots[s][0] == row for s in LEFT_SLOTS)
        lefts = [slots[s][1] for s in LEFT_SLOTS]
        stages = [[], [], [], []]
        for slot, (first, second) in enumerate(slots):
            for inner, outer, flip in [(first, second, 0), (second, first, 1)][: 1 if first == second else 2]:
                left = lefts.index(inner)
                stage = max(LEFT_STAGE[left], SLOT_STAGE[slot])
                base = (0, 0, X3, X4)[stage]
                key = max(slot, LEFT_SLOTS[left])
                stages[stage].append((key, (MULTIPLY, left, slot - base, flip, outer, 0)))
        stages = [[product for _, product in sorted(stage)] for stage in stages]
        first, touched = [], set()
        for product in stages[0]:
            if product[4] not in touched:
                first.append((ZERO, 0, 0, 0, product[4], 0))
            touched.add(product[4])
            first.append(product)
        first += [(ZERO, 0, 0, 0, total, 0) for total in range(4) if total not in touched]
        open_columns = sorted({product[4] for product in stages[3]})
        done_columns = [column for column in range(4) if column not in open_columns]
        assert len(open_columns) == 2

        def find(inner, outer):
            if (inner, outer) in slots:
                return slots.index((inner, outer)), 0
            return slots.index((outer, inner)), 1

        for core in range(2):
            early, early_slots = list(stages[2]), []
            early += [(ZERO, 0, 0, 0, 4 + which, 0) for which in range(2)]
            for k, column in enumerate(done_columns):
                early.append((FINISH, 4 + k, lefts.index(column), int(column == row), column, column))
            for which in range(2):
                for k, column in enumerate(done_columns):
                    slot, flip = find(column, 2 * col + which)
                    early.append((MULTIPLY, 4 + k, 2 + len(early_slots), flip, 4 + which, 0))
                    early_slots.append(slot)
                    if column == 2 * col + which:
                        early.append((LEVEL, 4 + k, 0, 0, 4 + which, column))
            late, late_slots = [], []
            for product in stages[3]:
                left = open_columns.index(lefts[product[1]])
                late.append((MULTIPLY, left) + product[2:])
            for k, column in enumerate(open_columns):
                late.append((FINISH, 2 + k, k, int(column == row), column, column))
            for k, which in enumerate((1 - core, core)):
                for m, column in enumerate(open_columns):
                    slot, flip = find(column, 2 * col + which)
                    late.append((MULTIPLY, 2 + m, 2 + len(late_slots), flip, 4 + which, 0))
                    late_slots.append(slot)
                    if column == 2 * col + which:
                        late.append((LEVEL, 2 + m, 0, 0, 4 + which, column))
                if k == 0:
                    late.append((SEND, 0, 0, 0, 4 + which, 0))
            own_rows = lambda slot: int(slot != core)
            straight = core == X_SENDS[0][row]
            second, last = Z_SENDS[1][row], X_SENDS[3][row]
            info = [
                core, row, col, core * 640,
                own_rows(X_SENDS[1][row]), (2 if straight else 3) if second == X1 else own_rows(second),
                0 if last == Z3 else (1 if straight else 2), int(straight),
            ] + [lefts.index(column) for column in open_columns] + open_columns
            devices.append(
                dict(
                    kernels=[first, stages[1], early, late],
                    slots=[early_slots, late_slots],
                    info=info,
                )
            )
    return devices


CORE, ROW, COL, FIRST_ROW, SEND_X2, SEND_Z2, SEND_LAST, STRAIGHT, OPEN_LEFT, OPEN = (*range(9), 10)


def device_tables(half):
    devices = device_lists()
    steps, rows = [], [[] for _ in devices]
    for kernel, (lefts, ahead) in enumerate((((0, 1, 2), 2), (range(4), 2), (range(4), 2), ((0, 1), 1))):
        length = max(len(device["kernels"][kernel]) for device in devices)
        steps.append((len(rows[0]), length))
        for row, device in zip(rows, devices):
            for fields in rows_of(device["kernels"][kernel], length, lefts, ahead):
                row += fields
    slots = []
    for kernel in range(2):
        slots.append(len(rows[0]))
        for row, device in zip(rows, devices):
            row += device["slots"][kernel]
    for device in devices:
        device["info"][FIRST_ROW] = device["info"][CORE] * half
    return [device["info"] for device in devices], rows, steps, slots


def bit_set(mask, bit):
    return jnp.bitwise_and(mask, jnp.int32(1 << bit)) != 0


class Worker:
    def __init__(self, table_ref, core, half, block_ref, block_sem, left_ref, left_sem, total_ref):
        self.table_ref, self.core, self.half = table_ref, core, half
        self.block_ref, self.block_sem = block_ref, block_sem
        self.left_ref, self.left_sem = left_ref, left_sem
        self.total_ref = total_ref
        self.near = pl.ds(pl.multiple_of(core * half, half), half)
        self.far = pl.ds(pl.multiple_of((1 - core) * half, half), half)
        self.blocks, self.lefts, self.send = {}, {}, None
        self.levels = None

    def load_halves(self, position, near_ref, far_ref):
        pltpu.make_async_copy(near_ref, self.block_ref.at[position, self.near], self.block_sem.at[position, 0]).start()
        pltpu.make_async_copy(far_ref, self.block_ref.at[position, self.far], self.block_sem.at[position, 1]).start()

    def load_block(self, position, slot, sources):
        self.blocks[position] = functools.partial(self.start_block, position, slot, sources)

    def start_block(self, position, slot, sources):
        for number, choices in sources.items():
            if isinstance(slot, int) and slot != number:
                continue
            for condition, near_ref, far_ref in choices:
                condition = slot == number if condition is None else jnp.logical_and(slot == number, condition)
                load = functools.partial(self.load_halves, position, near_ref, far_ref)
                if isinstance(condition, bool):
                    load()
                else:
                    pl.when(condition)(load)

    def own_sources(self, whole_ref, got_ref, other_ref):
        own = (whole_ref.at[self.near], whole_ref.at[self.far])
        return {
            slot: [(self.core == slot, *own), (self.core != slot, got_ref, other_ref)] for slot in (OWN0, OWN1)
        }

    def first_sources(self, straight, first, second, sibling_first, sibling_second):
        crossed = jnp.logical_not(straight)
        return {
            X1: [(straight, first, sibling_second), (crossed, second, sibling_first)],
            Z1: [(straight, sibling_first, second), (crossed, sibling_second, first)],
        }

    def load_left(self, index, number, refs):
        self.lefts[index] = functools.partial(self.start_left, index, number, refs)

    def left_places(self, refs):
        whole_ref, got_ref, straight, first, second = refs[:5]
        places = [(self.core, None, whole_ref.at[self.near]), (1 - self.core, None, got_ref)]
        places += [(2, straight, first), (2, jnp.logical_not(straight), second)]
        return places + [(3, None, ref) for ref in refs[5:]]

    def start_left(self, index, number, refs):
        for at, condition, ref in self.left_places(refs):
            if isinstance(at, int) and isinstance(number, int) and at != number:
                continue
            here = at == number
            if condition is not None:
                here = jnp.logical_and(here, condition)
            copy = functools.partial(self.copy_left, index, ref)
            if isinstance(here, bool):
                copy()
            else:
                pl.when(here)(copy)

    def copy_left(self, index, ref):
        pltpu.make_async_copy(ref, self.left_ref.at[index], self.left_sem.at[index]).start()

    def load_rows(self, refs):
        for k in range(len(refs) - 2):
            self.load_left(k, k, refs)

    def start(self, mask):
        for base, loads in ((LEFT_BIT, self.lefts), (BLOCK_BIT, self.blocks)):
            for index, load in loads.items():
                pl.when(bit_set(mask, base + index))(load)

    def wait(self, mask):
        half_block = self.block_ref.at[0, pl.ds(0, self.half)]
        for position in self.blocks:
            @pl.when(bit_set(mask, BLOCK_BIT + position))
            def _():
                for part in range(2):
                    pltpu.make_async_copy(half_block, half_block, self.block_sem.at[position, part]).wait()
        for index in self.lefts:
            @pl.when(bit_set(mask, LEFT_BIT + index))
            def _():
                pltpu.make_async_copy(self.left_ref.at[0], self.left_ref.at[0], self.left_sem.at[index]).wait()

    def multiply(self, field):
        total, left, block = self.total_ref.at[field[4]], self.left_ref.at[field[1]], self.block_ref.at[field[2]]

        @pl.when(field[3] == 0)
        def _():
            total[...] += jnp.dot(left[...], block[...], preferred_element_type=jnp.float32)

        @pl.when(field[3] == 1)
        def _():
            total[...] += lax.dot_general(
                left[...], block[...], (((1,), (1,)), ((), ())), preferred_element_type=jnp.float32
            )

    def tiles(self, cols_ref, column):
        lines = self.block_ref.shape[2] // 128
        return [jnp.broadcast_to(cols_ref[pl.ds(column * lines + m, 1), :], (16, 128)) for m in range(lines)]

    def finish(self, field):
        rows_ref, cols_ref, diag_ref = self.levels
        half = self.half
        total, left, made = self.total_ref.at[field[4]], self.left_ref.at[field[2]], self.left_ref.at[field[1]]
        cols = self.tiles(cols_ref, field[6])

        def one(index, carry):
            rows = pl.ds(pl.multiple_of(index * 16, 16), 16)
            level = rows_ref[rows, :]
            share = jnp.zeros((16, 128), jnp.float32)
            for m, col in enumerate(cols):
                at = slice(m * 128, (m + 1) * 128)
                ham = left[rows, at].astype(jnp.float32)
                square = total[rows, at] + ham * (level + col)
                made[rows, at] = square.astype(jnp.bfloat16)
                share = share + square * ham
            diag_ref[rows, :] += share
            return carry

        lax.fori_loop(0, half // 16, one, 0, unroll=2)

        @pl.when(field[3] == 1)
        def _():
            eye = lax.broadcasted_iota(jnp.int32, (128, 128), 0) == lax.broadcasted_iota(jnp.int32, (128, 128), 1)

            def fix(index, carry):
                rows = pl.ds(pl.multiple_of(index * 128, 128), 128)
                at = pl.ds(pl.multiple_of(self.core * half + index * 128, 128), 128)
                col = cols_ref[pl.ds((2 * field[6] + self.core) * (half // 128) + index, 1), :]
                level = rows_ref[rows, :]
                ham = left[rows, at].astype(jnp.float32)
                square = total[rows, at] + ham * (level + col)
                full = square + jnp.where(eye, level * level, 0.0)
                made[rows, at] = full.astype(jnp.bfloat16)
                diag_ref[rows, :] += jnp.where(eye, full * (ham + level) - square * ham, 0.0)
                return carry

            lax.fori_loop(0, half // 128, fix, 0)

    def add_level(self, field):
        cols = self.tiles(self.levels[1], field[6])
        total, left = self.total_ref.at[field[4]], self.left_ref.at[field[1]]

        def one(index, carry):
            rows = pl.ds(pl.multiple_of(index * 16, 16), 16)
            for m, col in enumerate(cols):
                at = slice(m * 128, (m + 1) * 128)
                total[rows, at] += left[rows, at].astype(jnp.float32) * col
            return carry

        lax.fori_loop(0, self.half // 16, one, 0, unroll=2)

    def clear(self, field):
        self.total_ref[field[4]] = jnp.zeros_like(self.total_ref[0])

    def run(self, start_count):
        start, count = start_count
        works = [(MULTIPLY, self.multiply), (ZERO, self.clear)]
        if self.levels is not None:
            works += [(FINISH, self.finish), (LEVEL, self.add_level)]
        if self.send is not None:
            works.append((SEND, self.send))

        def step(index, carry):
            field = [self.table_ref[start + index * FIELDS + k] for k in range(8)]
            pl.when(field[7] != 0)(functools.partial(self.start, field[7]))
            pl.when(field[5] != 0)(functools.partial(self.wait, field[5]))
            for kind, work in works:
                pl.when(field[0] == kind)(functools.partial(work, field))
            return carry

        lax.fori_loop(0, count, step, 0)


def take_inputs(refs, last):
    count = 7 + 2 * max(last - Z1, 0)
    return list(refs[:count]), list(refs[count:])


def use_inputs(worker, info_ref, inputs):
    own, first, rest = inputs[:3], inputs[3:7], inputs[7:]
    straight = info_ref[STRAIGHT] == 1
    sources = {**worker.own_sources(*own), **worker.first_sources(straight, *first)}
    for k in range(len(rest) // 2):
        sources[X2 + k] = [(None, rest[2 * k], rest[2 * k + 1])]
    return [own[0], own[1], straight, first[0], first[1]] + rest[:1], sources


def square_kernel(first, steps, left_count, slots, table_ref, info_ref, *refs):
    inputs, refs = take_inputs(refs, slots[-1])
    refs = refs[0 if first else 2 :]
    total_ref, token_ref, block_ref, block_sem, left_ref, left_sem = refs
    half = left_ref.shape[1]
    worker = Worker(table_ref, info_ref[CORE], half, block_ref, block_sem, left_ref, left_sem, total_ref)
    row_refs, sources = use_inputs(worker, info_ref, inputs)
    worker.load_rows(row_refs[: left_count + 2])
    for position, slot in enumerate(slots):
        worker.load_block(position, slot, sources)
    worker.run(steps)
    token_ref[...] = jnp.zeros_like(token_ref)


def early_kernel(steps, slots_at, table_ref, info_ref, *refs):
    inputs, refs = take_inputs(refs, Z3)
    _, _, level_rows_ref, level_ref, total_ref, diag_ref = (refs.pop(0) for _ in range(6))
    block_ref, block_sem, left_ref, left_sem = refs
    half = left_ref.shape[1]
    worker = Worker(table_ref, info_ref[CORE], half, block_ref, block_sem, left_ref, left_sem, total_ref)
    worker.levels = (level_rows_ref, level_ref, diag_ref)
    row_refs, sources = use_inputs(worker, info_ref, inputs)
    worker.load_rows(row_refs)
    worker.load_block(0, X3, sources)
    worker.load_block(1, Z3, sources)
    for k in range(4):
        worker.load_block(2 + k, table_ref[slots_at + k], sources)
    diag_ref[...] = jnp.zeros_like(diag_ref)
    worker.run(steps)


def late_kernel(steps, slots_at, table_ref, info_ref, gain_ref, *refs):
    inputs, refs = take_inputs(refs, Z4)
    _, old_diag_ref, level_rows_ref, level_ref, total_ref, cube_ref, density_ref, cube_diag_ref = (
        refs.pop(0) for _ in range(8)
    )
    block_ref, block_sem, left_ref, left_sem, out_sem, sent_ref, ham_ref, ham_sem, diag_ref = refs
    half, width = left_ref.shape[1:]
    core, row, col = info_ref[CORE], info_ref[ROW], info_ref[COL]
    worker = Worker(table_ref, core, half, block_ref, block_sem, left_ref, left_sem, total_ref)
    worker.levels = (level_rows_ref, level_ref, diag_ref)
    row_refs, sources = use_inputs(worker, info_ref, inputs)
    worker.load_block(0, X4, sources)
    worker.load_block(1, Z4, sources)
    for k in range(2):
        worker.load_left(k, info_ref[OPEN_LEFT + k], row_refs)
    for k in range(4):
        worker.load_block(2 + k, table_ref[slots_at + k], sources)
    ham_copy = pltpu.make_async_copy(row_refs[0].at[worker.near], ham_ref, ham_sem)
    sent_copy = pltpu.make_async_copy(sent_ref, cube_ref, out_sem.at[0])
    parts = 5
    rows_each = half // parts

    def density_copy(part):
        rows = pl.ds(pl.multiple_of(part * rows_each, rows_each), rows_each)
        to = pl.ds(pl.multiple_of(core * half + part * rows_each, rows_each), rows_each)
        return pltpu.make_async_copy(total_ref.at[4 + core, rows], density_ref.at[to], out_sem.at[1])

    def send(field):
        sent_ref[...] = total_ref[field[4]].astype(sent_ref.dtype)
        sent_copy.start()
        ham_copy.start()

    worker.send = send
    diag_ref[...] = old_diag_ref[...]
    worker.run(steps)
    ham_copy.wait()
    gain = gain_ref[0]
    linear, cubic = -1.5 * gain, 2.0 * (gain * gain * gain)

    eye = lax.broadcasted_iota(jnp.int32, (128, 128), 0) == lax.broadcasted_iota(jnp.int32, (128, 128), 1)

    def one_part(part, carry):
        def one(index, carry):
            rows = pl.ds(pl.multiple_of(part * rows_each + index * 16, 16), 16)
            for m in range(width // 128):
                at = slice(m * 128, (m + 1) * 128)
                cube = total_ref[4 + core, rows, at]
                total_ref[4 + core, rows, at] = linear * ham_ref[rows, at].astype(jnp.float32) + cubic * cube
            return carry

        lax.fori_loop(0, rows_each // 16, one, 0, unroll=2)

        @pl.when(row == 2 * col + core)
        def _():
            rows = pl.ds(pl.multiple_of(part * rows_each, rows_each), rows_each)
            at = pl.ds(pl.multiple_of(core * half + part * rows_each, rows_each), rows_each)
            total_ref[4 + core, rows, at] += jnp.where(eye, 0.5 + linear * level_rows_ref[rows, :], 0.0)

        density_copy(part).start()
        return carry

    lax.fori_loop(0, parts, one_part, 0)
    lines = half // 128
    cube_diag_ref[...] = jnp.zeros_like(cube_diag_ref)
    for k in range(lines):
        share = jnp.sum(diag_ref[pl.ds(k * 128, 128), :].T, 0, keepdims=True)
        cube_diag_ref[pl.ds((2 * row + core) * lines + k, 1), :] = share
    sent_copy.wait()
    for part in range(parts):
        density_copy(part).wait()


HERE = pl.BlockSpec(memory_space=pltpu.HBM)
SCALARS = pl.BlockSpec(memory_space=pltpu.SMEM)
VMEM = pl.BlockSpec(memory_space=pltpu.VMEM)
VMEM_BYTES = 38 * 2**20


def in_hbm(values):
    return [pltpu.with_memory_space_constraint(value, pltpu.HBM) for value in values]


def work_scratch(half, width, blocks, lefts):
    return [
        pltpu.VMEM((blocks, 2 * half, width), jnp.bfloat16),
        pltpu.SemaphoreType.DMA((blocks, 2)),
        pltpu.VMEM((lefts, half, width), jnp.bfloat16),
        pltpu.SemaphoreType.DMA((lefts,)),
    ]


def call_kernel(name, kernel, shape, scalars, operands, totals, in_vmem, out_shape, out_specs, scratch):
    first = len(scalars) + len(operands)
    held = [] if totals is None else [pltpu.with_memory_space_constraint(totals, pltpu.VMEM)]
    return pl.pallas_call(
        kernel,
        out_shape=(pltpu.VMEM((6,) + shape, jnp.float32),) + tuple(out_shape),
        in_specs=[SCALARS] * len(scalars) + [HERE] * len(operands) + [VMEM] * (len(held) + len(in_vmem)),
        out_specs=(VMEM,) + tuple(out_specs),
        scratch_shapes=scratch,
        input_output_aliases={first: 0} if held else {},
        compiler_params=pltpu.CompilerParams(vmem_limit_bytes=VMEM_BYTES),
        name=name,
    )(*scalars, *in_hbm(operands), *held, *in_vmem)


def pick_kernel(choices, whole, count, info_ref, *refs):
    sources, outs, in_sem = refs[:count], refs[count:-1], refs[-1]
    parts = in_sem.shape[1]
    size = outs[0].shape[0] // parts
    for part in range(parts):
        for k, choice in enumerate(choices):
            to = outs[k].at[pl.ds(part * size, size)]
            for number, source in enumerate(sources):
                @pl.when(info_ref[choice] == number)
                def _():
                    first = part * size
                    if number < whole:
                        first = pl.multiple_of(info_ref[FIRST_ROW] + first, size)
                    pltpu.make_async_copy(source.at[pl.ds(first, size)], to, in_sem.at[k, part]).start()
    for part in range(parts):
        for k, out_ref in enumerate(outs):
            to = out_ref.at[pl.ds(part * size, size)]
            pltpu.make_async_copy(to, to, in_sem.at[k, part]).wait()


def pick(info, choices, sources, whole, shape):
    parts = 4
    return pl.pallas_call(
        functools.partial(pick_kernel, choices, whole, len(sources)),
        out_shape=[pltpu.VMEM(shape, sources[0].dtype)] * len(choices),
        in_specs=[SCALARS] + [HERE] * len(sources),
        out_specs=[VMEM] * len(choices),
        scratch_shapes=[pltpu.SemaphoreType.DMA((len(choices), parts))],
        compiler_params=pltpu.CompilerParams(vmem_limit_bytes=8 * 2**20),
        name="pick",
    )(info, *in_hbm(sources))


def pairs_kernel(spots_ref, points_ref, out_ref, weight_ref, wide_ref):
    count, width = points_ref.shape[0], spots_ref.shape[1]
    tiles = width // 128

    @pl.when(pl.program_id(0) == 0)
    def _():
        for k in range(4):
            wide_ref[k] = jnp.broadcast_to(points_ref[:, k : k + 1], (count, 128))

    lanes = [slice(m * 128, (m + 1) * 128) for m in range(tiles)]
    spots = [[jnp.broadcast_to(spots_ref[k : k + 1, at], (16, 128)) for k in range(3)] for at in lanes]

    def step(group, sums):
        rows = pl.ds(pl.multiple_of(group * 16, 16), 16)
        px, py, pz, charge = (wide_ref[k, rows, :] for k in range(4))
        sums = list(sums)
        for m, at in enumerate(lanes):
            dx, dy, dz = spots[m][0] - px, spots[m][1] - py, spots[m][2] - pz
            inv = lax.rsqrt(dx * dx + dy * dy + dz * dz + 1.0)
            sums[m] = sums[m] + charge * inv
            weight_ref[rows, at] = (inv * (inv * inv)).astype(jnp.bfloat16)
        return tuple(sums)

    zeros = tuple(jnp.zeros((16, 128), jnp.float32) for _ in range(tiles))
    sums = lax.fori_loop(0, count // 16, step, zeros, unroll=2)
    for m, at in enumerate(lanes):
        out_ref[:, at] = jnp.sum(sums[m], 0, keepdims=True)


def pair_terms(centers, points):
    total, count = centers.shape[1], points.shape[0]
    width = 512
    part = jax.ShapeDtypeStruct((count, total), jnp.bfloat16)
    return pl.pallas_call(
        pairs_kernel,
        grid=(total // width,),
        out_shape=(jax.ShapeDtypeStruct((1, total), jnp.float32), part),
        in_specs=[pl.BlockSpec((3, width), lambda i: (0, i)), pl.BlockSpec((count, 4), lambda i: (0, 0))],
        out_specs=[pl.BlockSpec((1, width), lambda i: (0, i))] + [pl.BlockSpec((count, width), lambda i: (0, i))],
        scratch_shapes=[pltpu.VMEM((4, count, 128), jnp.float32)],
        compiler_params=pltpu.CompilerParams(vmem_limit_bytes=VMEM_BYTES),
        name="pairs",
    )(centers, points)


def levels_kernel(info_ref, near_ref, far_ref, gain_ref, level_ref, above_ref, rows_ref):
    lines = level_ref.shape[0]
    sums = near_ref[...] + far_ref[...]
    potential, diag = sums[0:lines], sums[lines : 2 * lines] + sums[0:lines]
    total = float(lines * 128)
    mean = jnp.sum(diag) / total
    above = diag - mean
    squares = (jnp.sum(sums[2 * lines : 2 * lines + 1]) / 128.0 + jnp.sum(above * above)) / total
    spread = jnp.sqrt(jnp.full((8, 128), squares + 1e-05, jnp.float32))
    gain_ref[0] = jnp.max(1.0 / (3.0 * spread))
    level_ref[...] = potential - mean
    above_ref[...] = above
    half = rows_ref.shape[0]
    first = (2 * info_ref[ROW] + info_ref[CORE]) * (half // 128)
    for k in range(half // 128):
        line = level_ref[pl.ds(first + k, 1), :]
        rows_ref[pl.ds(k * 128, 128), :] = jnp.broadcast_to(line, (128, 128)).T


def level_terms(info, parts, lines, half):
    line = jax.ShapeDtypeStruct((lines, 128), jnp.float32)
    return pl.pallas_call(
        levels_kernel,
        out_shape=(jax.ShapeDtypeStruct((1,), jnp.float32), line, line, jax.ShapeDtypeStruct((half, 128), jnp.float32)),
        in_specs=[SCALARS] + [VMEM] * 2,
        out_specs=(SCALARS, VMEM, VMEM, VMEM),
        compiler_params=pltpu.CompilerParams(vmem_limit_bytes=4 * 2**20),
        name="levels",
    )(info, *parts)


MIDDLE = 10.0


def pull_kernel(gain_ref, spots_ref, above_ref, near_ref, far_ref, weight_ref, coords_ref, charge_ref, out_ref, total_ref):
    gain = gain_ref[0]
    lines = 10
    width = lines * 128

    def one(index, carry):
        lanes = pl.ds(pl.multiple_of(index * width, width), width)
        pieces = []
        for m in range(lines):
            line = pl.ds(index * lines + m, 1)
            cube = near_ref[line, :] + far_ref[line, :]
            pieces.append(0.5 - 1.5 * gain * above_ref[line, :] + 2.0 * (gain * gain * gain) * cube)
        occ = jnp.concatenate(pieces, 1)
        weights = [occ] + [occ * (spots_ref[k : k + 1, lanes] - MIDDLE) for k in range(3)]
        stacked = jnp.concatenate(weights + [jnp.zeros((4, width), jnp.float32)], 0)
        high = stacked.astype(jnp.bfloat16)
        low = (stacked - high.astype(jnp.float32)).astype(jnp.bfloat16)
        both = jnp.concatenate([high, low, jnp.zeros((128 - 16, width), jnp.bfloat16)], 0)
        total_ref[...] += lax.dot_general(
            weight_ref[:, lanes], both, (((1,), (1,)), ((), ())), preferred_element_type=jnp.float32
        )
        return carry

    total_ref[...] = jnp.zeros_like(total_ref)
    lax.fori_loop(0, spots_ref.shape[1] // width, one, 0)
    sums = total_ref[...].T
    sums = sums[0:8] + sums[8:16]
    for k in range(3):
        pull = (coords_ref[k : k + 1, :] - MIDDLE) * sums[0:1] - sums[k + 1 : k + 2]
        out_ref[k : k + 1, :] = -charge_ref[...] * pull


def pull_terms(gain, centers, above, near, far, weights, mm_coords, mm_charges):
    count = mm_coords.shape[1]
    return pl.pallas_call(
        pull_kernel,
        out_shape=jax.ShapeDtypeStruct((3, count), jnp.float32),
        in_specs=[SCALARS] + [VMEM] * 7,
        out_specs=VMEM,
        scratch_shapes=[pltpu.VMEM((count, 128), jnp.float32)],
        compiler_params=pltpu.CompilerParams(vmem_limit_bytes=16 * 2**20),
        name="pull",
    )(
        gain, centers, above, near, far, pltpu.with_memory_space_constraint(weights, pltpu.VMEM), mm_coords,
        mm_charges[None],
    )


def density_kernel(start, steps, info_ref, gain_ref, ham_ref, far_ref, level_ref, _, out_ref):
    index = pl.program_id(0)
    core, row, col = info_ref[CORE], info_ref[ROW], info_ref[COL]
    gain = gain_ref[0]
    height, width = out_ref.shape
    linear, cubic = -1.5 * gain, 2.0 * (gain * gain * gain)
    first = ((1 - core) * steps + start + index) * height

    def one(k, carry):
        rows = pl.ds(pl.multiple_of(k * 16, 16), 16)
        for m in range(width // 128):
            at = slice(m * 128, (m + 1) * 128)
            cube = far_ref[rows, at].astype(jnp.float32)
            out_ref[rows, at] = linear * ham_ref[rows, at].astype(jnp.float32) + cubic * cube
        return carry

    lax.fori_loop(0, height // 16, one, 0, unroll=2)

    @pl.when(row == 2 * col + core)
    def _():
        eye = lax.broadcasted_iota(jnp.int32, (128, 128), 0) == lax.broadcasted_iota(jnp.int32, (128, 128), 1)

        def fix(k, carry):
            rows = pl.ds(pl.multiple_of(k * 128, 128), 128)
            at = pl.ds(pl.multiple_of(first + k * 128, 128), 128)
            line = pl.ds((2 * col + core) * (width // 128) + first // 128 + k, 1)
            out_ref[rows, at] += jnp.where(eye, 0.5 + linear * level_ref[line, :], 0.0)
            return carry

        lax.fori_loop(0, height // 128, fix, 0)


def density_rest(info, gain, ham, far, level, density, start, stop):
    height, width = ham.shape
    chunk = 128
    steps = far.shape[0] // chunk
    return pl.pallas_call(
        functools.partial(density_kernel, start, steps),
        grid_spec=pltpu.PrefetchScalarGridSpec(
            num_scalar_prefetch=1,
            grid=(stop - start,),
            in_specs=[
                SCALARS,
                pl.BlockSpec((chunk, width), lambda i, info: ((1 - info[CORE]) * steps + start + i, 0)),
                pl.BlockSpec((chunk, width), lambda i, info: (start + i, 0)),
                pl.BlockSpec(level.shape, lambda i, info: (0, 0)),
                HERE,
            ],
            out_specs=pl.BlockSpec((chunk, width), lambda i, info: ((1 - info[CORE]) * steps + start + i, 0)),
        ),
        out_shape=jax.ShapeDtypeStruct((height, width), jnp.float32),
        input_output_aliases={5: 0},
        compiler_params=pltpu.CompilerParams(vmem_limit_bytes=VMEM_BYTES),
        name="density",
    )(info, gain, ham, far, level, density)


def gossip_shards(sizes, h_core, centers, mm_coords, mm_charges):
    height, width = h_core.shape
    half = height // 2
    total, count = centers.shape[1], mm_coords.shape[1]
    row, col, core = (lax.axis_index(name) for name in ("sec", "col", "rep"))
    row_start = row * height
    col_start = (2 * col + core) * width
    infos, rows, steps, slots_at = device_tables(half)
    device = 4 * row + 2 * col + core
    info, table = (
        lax.dynamic_index_in_dim(jnp.asarray(values, jnp.int32), device, 0, keepdims=False) for values in (infos, rows)
    )

    def over_rep(value):
        return lax.ppermute(value, "rep", [(0, 1), (1, 0)])

    def over_col(value):
        return lax.ppermute(value, "col", [(0, 1), (1, 0)])

    def over_sec(value, step):
        moves = [(2 * start + x, 2 * to + x) for x in range(2) for start, to in Z_MOVES[step][x]]
        return lax.ppermute(value, ("sec", "col"), moves)

    def over_both(value, own):
        moves = []
        for z, x, c in ((z, x, c) for z in range(4) for x in range(2) for c in range(2)):
            if (c if own else 1 - c) == X_SENDS[0][z]:
                to = (z, 1 - x, c)
            else:
                to = (dict(Z_MOVES[0][x])[z], x, 1 - c)
            moves.append((4 * z + 2 * x + c, 4 * to[0] + 2 * to[1] + to[2]))
        return lax.ppermute(value, ("sec", "col", "rep"), moves)

    def swap_all(values):
        return [(value, over_rep(value)) for value in values]

    def flat(groups):
        return [value for group in groups for value in group]

    def after(arrived, work):
        return lax.optimization_barrier((arrived, work))

    shape = (half, width)
    near = lax.dynamic_slice_in_dim(h_core, core * half, half, 0)
    far = lax.dynamic_slice_in_dim(h_core, (1 - core) * half, half, 0)
    got = over_rep(far)
    firsts = (over_both(near, True), over_both(got, False))
    other = over_rep(near)
    points = jnp.concatenate([mm_coords, mm_charges[None]], 0).T
    terms, weights = pair_terms(centers, points)
    rows_glob = row_start + lax.broadcasted_iota(jnp.int32, (height, width), 0)
    cols_glob = col_start + lax.broadcasted_iota(jnp.int32, (height, width), 1)
    on_diag = rows_glob == cols_glob
    wide = h_core.astype(jnp.float32)
    own_diag = jnp.sum(jnp.where(on_diag, wide, 0.0), 0)
    own_off = jnp.sum(jnp.where(on_diag, 0.0, wide * wide))
    diag = lax.dynamic_update_slice_in_dim(jnp.zeros((total,), jnp.float32), own_diag, col_start, 0)
    packed = jnp.concatenate([terms[0], diag, jnp.full((8 * 128,), own_off)]).reshape(-1, 128)
    packed = packed + over_rep(packed)
    from_col = over_col(packed)
    (firsts, from_col), (packed, weights, table, other) = after((firsts, from_col), (packed, weights, table, other))
    own_parts = [h_core, got, other]
    sends = pick(info, (SEND_X2, SEND_Z2), (h_core, got) + tuple(firsts), 1, shape)
    firsts, sends = lax.optimization_barrier((list(firsts), sends))
    z2 = over_sec(sends[1], 1)
    x2 = over_col(sends[0])
    packed = packed + from_col
    from_near = lax.ppermute(packed, "sec", [(i, i ^ 1) for i in range(4)])
    operands = own_parts + firsts + [over_rep(first) for first in firsts]

    def grow_square(stage, left_count, slots, totals, token):
        kernel = functools.partial(square_kernel, totals is None, steps[stage], left_count, slots)
        return call_kernel(
            f"square_{stage}", kernel, shape, (table, info), operands + ([] if token is None else [token]), totals, (),
            (jax.ShapeDtypeStruct((8, 128), jnp.float32),), (VMEM,), work_scratch(half, width, len(slots), 4),
        )

    totals, token = grow_square(0, 3, (OWN0, OWN1, X1, Z1), None, None)
    (x2, z2, from_near), (token, packed) = after((x2, z2, from_near), (token, packed))
    z3 = over_sec(x2, 2)
    x3 = over_col(z2)
    operands = operands + flat(swap_all((x2, z2)))
    totals, token = grow_square(1, 4, (OWN0, OWN1, X1, Z1, X2, Z2), totals, token)
    packed = packed + from_near
    from_far = lax.ppermute(packed, "sec", [(i, i ^ 2) for i in range(4)])
    (x3, z3, from_far), (token, packed) = after((x3, z3, from_far), (token, packed))
    last_send = pick(info, (SEND_LAST,), [z3] + operands[5:7], 0, shape)[0]
    (x3, z3), last_send = after((x3, z3), last_send)
    z4 = over_sec(last_send, 3)
    x4 = over_col(last_send)
    operands = operands + flat(swap_all((x3, z3)))
    gain, level, above, level_rows = level_terms(info, [packed, from_far], total // 128, half)
    lines = jax.ShapeDtypeStruct((total // 128, 128), jnp.float32)
    share = jax.ShapeDtypeStruct((half, 128), jnp.float32)
    totals, cube_diag = call_kernel(
        "early_cube", functools.partial(early_kernel, steps[2], slots_at[0]), shape, (table, info),
        operands + [token], totals, (level_rows, level),
        (share,), (VMEM,), work_scratch(half, width, 6, 6),
    )
    (x4, z4), (cube_diag, above, level_rows, level, gain) = after(
        (x4, z4), (cube_diag, above, level_rows, level, gain)
    )
    operands = operands + flat(swap_all((x4, z4)))
    _, sibling, density, cube_diag = call_kernel(
        "late_cube", functools.partial(late_kernel, steps[3], slots_at[1]), shape, (table, info, gain),
        operands, totals, (cube_diag, level_rows, level),
        (jax.ShapeDtypeStruct(shape, jnp.bfloat16), jax.ShapeDtypeStruct((height, width), jnp.float32), lines),
        (HERE, HERE, VMEM),
        work_scratch(half, width, 6, 4)
        + [
            pltpu.SemaphoreType.DMA((2,)),
            pltpu.VMEM(shape, jnp.bfloat16),
            pltpu.VMEM(shape, jnp.bfloat16),
            pltpu.SemaphoreType.DMA,
            pltpu.VMEM((half, 128), jnp.float32),
        ],
    )
    sibling = over_rep(sibling)
    cube_diag = cube_diag + over_rep(cube_diag)
    from_near = lax.ppermute(cube_diag, "sec", [(i, i ^ 1) for i in range(4)])
    density = density_rest(info, gain, h_core, sibling, level, density, 0, 3)
    from_near, density = after(from_near, density)
    cube_diag = cube_diag + from_near
    from_far = lax.ppermute(cube_diag, "sec", [(i, i ^ 2) for i in range(4)])
    density = density_rest(info, gain, h_core, sibling, level, density, 3, 5)
    from_far, density = after(from_far, density)
    forces = pull_terms(gain, centers, above, cube_diag, from_far, weights, mm_coords, mm_charges)
    return (density, forces)


def solution(mesh):
    in_specs = (
        P(("groups", "sec"), ("col", "rep")),
        P(None, "groups"),
        P(None, ("groups", "sec", "col", "rep")),
        P(("groups", "sec", "col", "rep")),
    )
    out_specs = (P(("groups", "sec"), ("col", "rep")), P(None, ("groups", "sec", "col", "rep")))
    sizes = dict(mesh.shape)
    small = (sizes["sec"], sizes["col"], sizes["rep"]) == (4, 2, 2)
    body = functools.partial(gossip_shards if small else gather_shards, sizes)
    return jax.shard_map(body, mesh=mesh, in_specs=in_specs, out_specs=out_specs, check_vma=False)
```

```python
import functools

import jax
import jax.numpy as jnp
from jax import lax
from jax.experimental import pallas as pl
from jax.experimental.pallas import tpu as pltpu
from jax.sharding import PartitionSpec as P

PART = ("sec", "col", "rep")


def potential_kernel(spots_ref, points_ref, out_ref):
    count = points_ref.shape[0]
    width = spots_ref.shape[1]
    sx, sy, sz = (spots_ref[k : k + 1, :] for k in range(3))

    def step(index, accum):
        rows = points_ref[pl.ds(pl.multiple_of(index * 8, 8), 8), :]
        dx = sx - rows[:, 0:1]
        dy = sy - rows[:, 1:2]
        dz = sz - rows[:, 2:3]
        dist = dx * dx + dy * dy + dz * dz + 1.0
        return accum + rows[:, 3:4] * lax.rsqrt(dist)

    total = lax.fori_loop(0, count // 8, step, jnp.zeros((8, width), jnp.float32), unroll=4)
    out_ref[...] = jnp.sum(total, 0, keepdims=True)


def potential_terms(centers, mm_coords, mm_charges):
    total = centers.shape[1]
    count = mm_coords.shape[1]
    width = 1024 if total % 1024 == 0 else total
    points = jnp.concatenate([mm_coords, mm_charges[None]], 0).T
    return pl.pallas_call(
        potential_kernel,
        grid=(total // width,),
        out_shape=jax.ShapeDtypeStruct((1, total), jnp.float32),
        in_specs=[
            pl.BlockSpec((3, width), lambda i: (0, i)),
            pl.BlockSpec((count, 4), lambda i: (0, 0)),
        ],
        out_specs=pl.BlockSpec((1, width), lambda i: (0, i)),
        name="potential",
    )(centers, points)


def force_kernel(spots_ref, occ_ref, points_ref, out_ref):
    total = spots_ref.shape[1]
    rows = points_ref[...]
    px, py, pz, charge = (rows[:, k : k + 1] for k in range(4))
    count = rows.shape[0]

    def step(index, accum):
        lanes = pl.ds(pl.multiple_of(index * 128, 128), 128)
        dx = px - spots_ref[0:1, lanes]
        dy = py - spots_ref[1:2, lanes]
        dz = pz - spots_ref[2:3, lanes]
        inv = lax.rsqrt(dx * dx + dy * dy + dz * dz + 1.0)
        weight = occ_ref[:, lanes] * inv * (inv * inv)
        return (accum[0] + dx * weight, accum[1] + dy * weight, accum[2] + dz * weight)

    zero = jnp.zeros((count, 128), jnp.float32)
    sums = lax.fori_loop(0, total // 128, step, (zero, zero, zero), unroll=4)
    for k in range(3):
        out_ref[:, k : k + 1] = -charge * jnp.sum(sums[k], 1, keepdims=True)


def force_terms(centers, occupation, mm_coords, mm_charges):
    total = centers.shape[1]
    count = mm_coords.shape[1]
    width = 32
    points = jnp.concatenate([mm_coords, mm_charges[None]], 0).T
    summed = pl.pallas_call(
        force_kernel,
        grid=(count // width,),
        out_shape=jax.ShapeDtypeStruct((count, 4), jnp.float32),
        in_specs=[
            pl.BlockSpec((3, total), lambda i: (0, 0)),
            pl.BlockSpec((1, total), lambda i: (0, 0)),
            pl.BlockSpec((width, 4), lambda i: (i, 0)),
        ],
        out_specs=pl.BlockSpec((width, 4), lambda i: (i, 0)),
        name="forces",
    )(centers, occupation, points)
    return summed[:, :3].T


def butterfly_sum(value, sizes, axes=("rep", "col", "sec")):
    for axis in axes:
        size = sizes[axis]
        if size & (size - 1):
            value = lax.psum(value, axis)
            continue
        hop = 1
        while hop < size:
            value = value + lax.ppermute(value, axis, [(i, i ^ hop) for i in range(size)])
            hop *= 2
    return value


def fold_with(left, piece):
    return jnp.dot(left, piece, preferred_element_type=jnp.float32)


def gather_shards(sizes, h_core, centers, mm_coords, mm_charges):
    row_count, col_count = h_core.shape
    total = centers.shape[1]
    row_start = lax.axis_index("sec") * row_count
    col_start = lax.axis_index(("col", "rep")) * col_count
    rows_glob = row_start + lax.broadcasted_iota(jnp.int32, (row_count, col_count), 0)
    cols_glob = col_start + lax.broadcasted_iota(jnp.int32, (row_count, col_count), 1)
    on_diag = rows_glob == cols_glob
    off = jnp.where(on_diag, jnp.zeros((), h_core.dtype), h_core)
    row_panel = lax.all_gather(off, ("col", "rep"), axis=1, tiled=True)
    col_panel = lax.all_gather(off, "sec", axis=0, tiled=True)

    wide = h_core.astype(jnp.float32)
    own_diag = jnp.sum(jnp.where(on_diag, wide, 0.0), 0)
    own_off = jnp.sum(jnp.where(on_diag, 0.0, wide * wide))
    terms = potential_terms(centers, mm_coords, mm_charges)[0]
    own_cols = lax.dynamic_slice_in_dim(terms, col_start, col_count, 0) + own_diag
    terms = lax.dynamic_update_slice_in_dim(terms, own_cols, col_start, 0)
    sums = butterfly_sum(jnp.concatenate([terms, jnp.full((128,), own_off)]), sizes)
    diag_vals, off_total = sums[:total], sums[total]
    mean_level = jnp.sum(diag_vals) / total
    level = diag_vals - mean_level
    spread = jnp.sqrt((off_total + jnp.sum(level * level)) / total + 1e-05)
    gain = 1.0 / (3.0 * spread)

    level_rows = lax.dynamic_slice_in_dim(level, row_start, row_count, 0)[:, None]
    level_cols = lax.dynamic_slice_in_dim(level, col_start, col_count, 0)[None, :]
    off_wide = off.astype(jnp.float32)
    square = fold_with(row_panel, col_panel)
    square = square + off_wide * (level_rows + level_cols) + jnp.where(on_diag, level_rows * level_rows, 0.0)
    shifted = off_wide + jnp.where(on_diag, level_rows, 0.0)
    square_b = square.astype(jnp.bfloat16)
    square_panel = lax.all_gather(square_b, ("col", "rep"), axis=1, tiled=True)
    own_cube = jnp.sum(square * shifted, 0)
    cube_diag = lax.dynamic_update_slice_in_dim(jnp.zeros((total,), jnp.float32), own_cube, col_start, 0)
    cube_diag = butterfly_sum(cube_diag, sizes)
    occupation = 0.5 - 1.5 * gain * level + 2.0 * gain**3 * cube_diag
    forces = force_terms(centers, occupation[None], mm_coords, mm_charges)

    cube = fold_with(square_panel, col_panel) + square_b.astype(jnp.float32) * level_cols
    density = jnp.where(on_diag, 0.5, 0.0) - 1.5 * gain * shifted + 2.0 * gain**3 * cube
    return (density, forces)


ROUND = ((0, 1), (1, 2), (2, 3), (3, 0))
BACK = ((0, 3), (3, 2), (2, 1), (1, 0))
Z_MOVES = ((ROUND, BACK), (BACK, ROUND), (ROUND, BACK), (ROUND, BACK))
OWN0, OWN1, X1, Z1, X2, Z2, X3, Z3, X4, Z4 = range(10)
X_SENDS = ((OWN1, OWN0, OWN1, OWN0), (OWN0, OWN1, OWN0, OWN1), (Z2,) * 4, (Z3, Z1, Z1, Z3))
Z_SENDS = ((OWN0, OWN1, OWN0, OWN1), (OWN1, X1, X1, OWN0), (X2,) * 4, (Z3, Z1, Z1, Z3))
SLOT_STAGE = (0, 0, 0, 0, 1, 1, 2, 2, 3, 3)
LEFT_SLOTS = (OWN0, OWN1, X1, X2)
LEFT_STAGE = (0, 0, 0, 1)
FIELDS = 10
NOTHING, MULTIPLY, FINISH, LEVEL, SEND, ZERO = range(6)
BLOCK_BIT, LEFT_BIT = 0, 8


def block_places():
    chips = [(z, x) for z in range(4) for x in range(2)]
    held = {(z, x): [(z, 2 * x), (z, 2 * x + 1)] for z, x in chips}
    for step in range(4):
        arrived = {}
        for z, x in chips:
            before = next(start for start, to in Z_MOVES[step][x] if to == z)
            arrived[(z, x)] = [held[(z, 1 - x)][X_SENDS[step][z]], held[(before, x)][Z_SENDS[step][before]]]
        for chip in chips:
            held[chip] = held[chip] + arrived[chip]
    return [held[chip] for chip in chips]


def rows_of(products, length, lefts, ahead):
    seen, firsts = set(), []
    for kind, left, block, flip, total, column in products:
        bits = []
        if kind in (MULTIPLY, FINISH, LEVEL):
            loaded_left = block if kind == FINISH else left
            if loaded_left in lefts:
                bits.append(LEFT_BIT + loaded_left)
        if kind == MULTIPLY:
            bits.append(BLOCK_BIT + block)
        firsts.append([bit for bit in dict.fromkeys(bits) if bit not in seen])
        seen.update(bits)
    mask = lambda bits: sum(1 << bit for bit in bits)
    waves = [k for k, first in enumerate(firsts) if first]
    starts = [[] for _ in products]
    for number, k in enumerate(waves):
        at = 0 if number <= ahead else waves[number - ahead]
        starts[at] += firsts[k]
    rows = []
    for k, (kind, left, block, flip, total, column) in enumerate(products):
        rows.append([kind, left, block, flip, total, mask(firsts[k]), column, mask(starts[k]), 0, 0])
    return rows + [[NOTHING] + [0] * (FIELDS - 1)] * (length - len(rows))


def device_lists():
    devices = []
    for chip, slots in enumerate(block_places()):
        assert len({tuple(sorted(place)) for place in slots}) == 10
        row, col = divmod(chip, 2)
        assert all(slots[s][0] == row for s in LEFT_SLOTS)
        lefts = [slots[s][1] for s in LEFT_SLOTS]
        stages = [[], [], [], []]
        for slot, (first, second) in enumerate(slots):
            for inner, outer, flip in [(first, second, 0), (second, first, 1)][: 1 if first == second else 2]:
                left = lefts.index(inner)
                stage = max(LEFT_STAGE[left], SLOT_STAGE[slot])
                base = (0, 0, X3, X4)[stage]
                key = max(slot, LEFT_SLOTS[left])
                stages[stage].append((key, (MULTIPLY, left, slot - base, flip, outer, 0)))
        stages = [[product for _, product in sorted(stage)] for stage in stages]
        first, touched = [], set()
        for product in stages[0]:
            if product[4] not in touched:
                first.append((ZERO, 0, 0, 0, product[4], 0))
            touched.add(product[4])
            first.append(product)
        first += [(ZERO, 0, 0, 0, total, 0) for total in range(4) if total not in touched]
        open_columns = sorted({product[4] for product in stages[3]})
        done_columns = [column for column in range(4) if column not in open_columns]
        assert len(open_columns) == 2

        def find(inner, outer):
            if (inner, outer) in slots:
                return slots.index((inner, outer)), 0
            return slots.index((outer, inner)), 1

        for core in range(2):
            early, early_slots = list(stages[2]), []
            early += [(ZERO, 0, 0, 0, 4 + which, 0) for which in range(2)]
            for k, column in enumerate(done_columns):
                early.append((FINISH, 4 + k, lefts.index(column), int(column == row), column, column))
            for which in range(2):
                for k, column in enumerate(done_columns):
                    slot, flip = find(column, 2 * col + which)
                    early.append((MULTIPLY, 4 + k, 2 + len(early_slots), flip, 4 + which, 0))
                    early_slots.append(slot)
                    if column == 2 * col + which:
                        early.append((LEVEL, 4 + k, 0, 0, 4 + which, column))
            late, late_slots = [], []
            for product in stages[3]:
                left = open_columns.index(lefts[product[1]])
                late.append((MULTIPLY, left) + product[2:])
            for k, column in enumerate(open_columns):
                late.append((FINISH, 2 + k, k, int(column == row), column, column))
            for k, which in enumerate((1 - core, core)):
                for m, column in enumerate(open_columns):
                    slot, flip = find(column, 2 * col + which)
                    late.append((MULTIPLY, 2 + m, 2 + len(late_slots), flip, 4 + which, 0))
                    late_slots.append(slot)
                    if column == 2 * col + which:
                        late.append((LEVEL, 2 + m, 0, 0, 4 + which, column))
                if k == 0:
                    late.append((SEND, 0, 0, 0, 4 + which, 0))
            own_rows = lambda slot: int(slot != core)
            straight = core == X_SENDS[0][row]
            second, last = Z_SENDS[1][row], X_SENDS[3][row]
            info = [
                core, row, col, core * 640,
                own_rows(X_SENDS[1][row]), (2 if straight else 3) if second == X1 else own_rows(second),
                0 if last == Z3 else (1 if straight else 2), int(straight),
            ] + [lefts.index(column) for column in open_columns] + open_columns
            devices.append(
                dict(
                    kernels=[first, stages[1], early, late],
                    slots=[early_slots, late_slots],
                    info=info,
                )
            )
    return devices


CORE, ROW, COL, FIRST_ROW, SEND_X2, SEND_Z2, SEND_LAST, STRAIGHT, OPEN_LEFT, OPEN = (*range(9), 10)


def device_tables(half):
    devices = device_lists()
    steps, rows = [], [[] for _ in devices]
    for kernel, (lefts, ahead) in enumerate((((0, 1, 2), 2), (range(4), 2), (range(4), 2), ((0, 1), 1))):
        length = max(len(device["kernels"][kernel]) for device in devices)
        steps.append((len(rows[0]), length))
        for row, device in zip(rows, devices):
            for fields in rows_of(device["kernels"][kernel], length, lefts, ahead):
                row += fields
    slots = []
    for kernel in range(2):
        slots.append(len(rows[0]))
        for row, device in zip(rows, devices):
            row += device["slots"][kernel]
    for device in devices:
        device["info"][FIRST_ROW] = device["info"][CORE] * half
    return [device["info"] for device in devices], rows, steps, slots


def bit_set(mask, bit):
    return jnp.bitwise_and(mask, jnp.int32(1 << bit)) != 0


class Worker:
    def __init__(self, table_ref, core, half, block_ref, block_sem, left_ref, left_sem, total_ref):
        self.table_ref, self.core, self.half = table_ref, core, half
        self.block_ref, self.block_sem = block_ref, block_sem
        self.left_ref, self.left_sem = left_ref, left_sem
        self.total_ref = total_ref
        self.near = pl.ds(pl.multiple_of(core * half, half), half)
        self.far = pl.ds(pl.multiple_of((1 - core) * half, half), half)
        self.blocks, self.lefts, self.send = {}, {}, None
        self.levels = None

    def load_halves(self, position, near_ref, far_ref):
        pltpu.make_async_copy(near_ref, self.block_ref.at[position, self.near], self.block_sem.at[position, 0]).start()
        pltpu.make_async_copy(far_ref, self.block_ref.at[position, self.far], self.block_sem.at[position, 1]).start()

    def load_block(self, position, slot, sources):
        self.blocks[position] = functools.partial(self.start_block, position, slot, sources)

    def start_block(self, position, slot, sources):
        for number, choices in sources.items():
            if isinstance(slot, int) and slot != number:
                continue
            for condition, near_ref, far_ref in choices:
                condition = slot == number if condition is None else jnp.logical_and(slot == number, condition)
                load = functools.partial(self.load_halves, position, near_ref, far_ref)
                if isinstance(condition, bool):
                    load()
                else:
                    pl.when(condition)(load)

    def own_sources(self, whole_ref, got_ref, other_ref):
        own = (whole_ref.at[self.near], whole_ref.at[self.far])
        return {
            slot: [(self.core == slot, *own), (self.core != slot, got_ref, other_ref)] for slot in (OWN0, OWN1)
        }

    def first_sources(self, straight, first, second, sibling_first, sibling_second):
        crossed = jnp.logical_not(straight)
        return {
            X1: [(straight, first, sibling_second), (crossed, second, sibling_first)],
            Z1: [(straight, sibling_first, second), (crossed, sibling_second, first)],
        }

    def load_left(self, index, number, refs):
        self.lefts[index] = functools.partial(self.start_left, index, number, refs)

    def left_places(self, refs):
        whole_ref, got_ref, straight, first, second = refs[:5]
        places = [(self.core, None, whole_ref.at[self.near]), (1 - self.core, None, got_ref)]
        places += [(2, straight, first), (2, jnp.logical_not(straight), second)]
        return places + [(3, None, ref) for ref in refs[5:]]

    def start_left(self, index, number, refs):
        for at, condition, ref in self.left_places(refs):
            if isinstance(at, int) and isinstance(number, int) and at != number:
                continue
            here = at == number
            if condition is not None:
                here = jnp.logical_and(here, condition)
            copy = functools.partial(self.copy_left, index, ref)
            if isinstance(here, bool):
                copy()
            else:
                pl.when(here)(copy)

    def copy_left(self, index, ref):
        pltpu.make_async_copy(ref, self.left_ref.at[index], self.left_sem.at[index]).start()

    def load_rows(self, refs):
        for k in range(len(refs) - 2):
            self.load_left(k, k, refs)

    def start(self, mask):
        for base, loads in ((LEFT_BIT, self.lefts), (BLOCK_BIT, self.blocks)):
            for index, load in loads.items():
                pl.when(bit_set(mask, base + index))(load)

    def wait(self, mask):
        half_block = self.block_ref.at[0, pl.ds(0, self.half)]
        for position in self.blocks:
            @pl.when(bit_set(mask, BLOCK_BIT + position))
            def _():
                for part in range(2):
                    pltpu.make_async_copy(half_block, half_block, self.block_sem.at[position, part]).wait()
        for index in self.lefts:
            @pl.when(bit_set(mask, LEFT_BIT + index))
            def _():
                pltpu.make_async_copy(self.left_ref.at[0], self.left_ref.at[0], self.left_sem.at[index]).wait()

    def multiply(self, field):
        total, left, block = self.total_ref.at[field[4]], self.left_ref.at[field[1]], self.block_ref.at[field[2]]

        @pl.when(field[3] == 0)
        def _():
            total[...] += jnp.dot(left[...], block[...], preferred_element_type=jnp.float32)

        @pl.when(field[3] == 1)
        def _():
            total[...] += lax.dot_general(
                left[...], block[...], (((1,), (1,)), ((), ())), preferred_element_type=jnp.float32
            )

    def tiles(self, cols_ref, column):
        lines = self.block_ref.shape[2] // 128
        return [jnp.broadcast_to(cols_ref[pl.ds(column * lines + m, 1), :], (16, 128)) for m in range(lines)]

    def finish(self, field):
        rows_ref, cols_ref, diag_ref = self.levels
        half = self.half
        total, left, made = self.total_ref.at[field[4]], self.left_ref.at[field[2]], self.left_ref.at[field[1]]
        cols = self.tiles(cols_ref, field[6])

        def one(index, carry):
            rows = pl.ds(pl.multiple_of(index * 16, 16), 16)
            level = rows_ref[rows, :]
            share = jnp.zeros((16, 128), jnp.float32)
            for m, col in enumerate(cols):
                at = slice(m * 128, (m + 1) * 128)
                ham = left[rows, at].astype(jnp.float32)
                square = total[rows, at] + ham * (level + col)
                made[rows, at] = square.astype(jnp.bfloat16)
                share = share + square * ham
            diag_ref[rows, :] += share
            return carry

        lax.fori_loop(0, half // 16, one, 0, unroll=2)

        @pl.when(field[3] == 1)
        def _():
            eye = lax.broadcasted_iota(jnp.int32, (128, 128), 0) == lax.broadcasted_iota(jnp.int32, (128, 128), 1)

            def fix(index, carry):
                rows = pl.ds(pl.multiple_of(index * 128, 128), 128)
                at = pl.ds(pl.multiple_of(self.core * half + index * 128, 128), 128)
                col = cols_ref[pl.ds((2 * field[6] + self.core) * (half // 128) + index, 1), :]
                level = rows_ref[rows, :]
                ham = left[rows, at].astype(jnp.float32)
                square = total[rows, at] + ham * (level + col)
                full = square + jnp.where(eye, level * level, 0.0)
                made[rows, at] = full.astype(jnp.bfloat16)
                diag_ref[rows, :] += jnp.where(eye, full * (ham + level) - square * ham, 0.0)
                return carry

            lax.fori_loop(0, half // 128, fix, 0)

    def add_level(self, field):
        cols = self.tiles(self.levels[1], field[6])
        total, left = self.total_ref.at[field[4]], self.left_ref.at[field[1]]

        def one(index, carry):
            rows = pl.ds(pl.multiple_of(index * 16, 16), 16)
            for m, col in enumerate(cols):
                at = slice(m * 128, (m + 1) * 128)
                total[rows, at] += left[rows, at].astype(jnp.float32) * col
            return carry

        lax.fori_loop(0, self.half // 16, one, 0, unroll=2)

    def clear(self, field):
        self.total_ref[field[4]] = jnp.zeros_like(self.total_ref[0])

    def run(self, start_count):
        start, count = start_count
        works = [(MULTIPLY, self.multiply), (ZERO, self.clear)]
        if self.levels is not None:
            works += [(FINISH, self.finish), (LEVEL, self.add_level)]
        if self.send is not None:
            works.append((SEND, self.send))

        def step(index, carry):
            field = [self.table_ref[start + index * FIELDS + k] for k in range(8)]
            pl.when(field[7] != 0)(functools.partial(self.start, field[7]))
            pl.when(field[5] != 0)(functools.partial(self.wait, field[5]))
            for kind, work in works:
                pl.when(field[0] == kind)(functools.partial(work, field))
            return carry

        lax.fori_loop(0, count, step, 0)


def take_inputs(refs, last):
    count = 7 + 2 * max(last - Z1, 0)
    return list(refs[:count]), list(refs[count:])


def use_inputs(worker, info_ref, inputs):
    own, first, rest = inputs[:3], inputs[3:7], inputs[7:]
    straight = info_ref[STRAIGHT] == 1
    sources = {**worker.own_sources(*own), **worker.first_sources(straight, *first)}
    for k in range(len(rest) // 2):
        sources[X2 + k] = [(None, rest[2 * k], rest[2 * k + 1])]
    return [own[0], own[1], straight, first[0], first[1]] + rest[:1], sources


def square_kernel(first, steps, left_count, slots, table_ref, info_ref, *refs):
    inputs, refs = take_inputs(refs, slots[-1])
    refs = refs[0 if first else 2 :]
    total_ref, token_ref, block_ref, block_sem, left_ref, left_sem = refs
    half = left_ref.shape[1]
    worker = Worker(table_ref, info_ref[CORE], half, block_ref, block_sem, left_ref, left_sem, total_ref)
    row_refs, sources = use_inputs(worker, info_ref, inputs)
    worker.load_rows(row_refs[: left_count + 2])
    for position, slot in enumerate(slots):
        worker.load_block(position, slot, sources)
    worker.run(steps)
    token_ref[...] = jnp.zeros_like(token_ref)


def early_kernel(steps, slots_at, table_ref, info_ref, *refs):
    inputs, refs = take_inputs(refs, Z3)
    _, _, level_rows_ref, level_ref, total_ref, diag_ref = (refs.pop(0) for _ in range(6))
    block_ref, block_sem, left_ref, left_sem = refs
    half = left_ref.shape[1]
    worker = Worker(table_ref, info_ref[CORE], half, block_ref, block_sem, left_ref, left_sem, total_ref)
    worker.levels = (level_rows_ref, level_ref, diag_ref)
    row_refs, sources = use_inputs(worker, info_ref, inputs)
    worker.load_rows(row_refs)
    worker.load_block(0, X3, sources)
    worker.load_block(1, Z3, sources)
    for k in range(4):
        worker.load_block(2 + k, table_ref[slots_at + k], sources)
    diag_ref[...] = jnp.zeros_like(diag_ref)
    worker.run(steps)


def late_kernel(steps, slots_at, table_ref, info_ref, gain_ref, *refs):
    inputs, refs = take_inputs(refs, Z4)
    _, old_diag_ref, level_rows_ref, level_ref, total_ref, cube_ref, density_ref, cube_diag_ref = (
        refs.pop(0) for _ in range(8)
    )
    block_ref, block_sem, left_ref, left_sem, out_sem, sent_ref, ham_ref, ham_sem, diag_ref = refs
    half, width = left_ref.shape[1:]
    core, row, col = info_ref[CORE], info_ref[ROW], info_ref[COL]
    worker = Worker(table_ref, core, half, block_ref, block_sem, left_ref, left_sem, total_ref)
    worker.levels = (level_rows_ref, level_ref, diag_ref)
    row_refs, sources = use_inputs(worker, info_ref, inputs)
    worker.load_block(0, X4, sources)
    worker.load_block(1, Z4, sources)
    for k in range(2):
        worker.load_left(k, info_ref[OPEN_LEFT + k], row_refs)
    for k in range(4):
        worker.load_block(2 + k, table_ref[slots_at + k], sources)
    ham_copy = pltpu.make_async_copy(row_refs[0].at[worker.near], ham_ref, ham_sem)
    sent_copy = pltpu.make_async_copy(sent_ref, cube_ref, out_sem.at[0])
    parts = 5
    rows_each = half // parts

    def density_copy(part):
        rows = pl.ds(pl.multiple_of(part * rows_each, rows_each), rows_each)
        to = pl.ds(pl.multiple_of(core * half + part * rows_each, rows_each), rows_each)
        return pltpu.make_async_copy(total_ref.at[4 + core, rows], density_ref.at[to], out_sem.at[1])

    def send(field):
        sent_ref[...] = total_ref[field[4]].astype(sent_ref.dtype)
        sent_copy.start()
        ham_copy.start()

    worker.send = send
    diag_ref[...] = old_diag_ref[...]
    worker.run(steps)
    ham_copy.wait()
    gain = gain_ref[0]
    linear, cubic = -1.5 * gain, 2.0 * (gain * gain * gain)

    eye = lax.broadcasted_iota(jnp.int32, (128, 128), 0) == lax.broadcasted_iota(jnp.int32, (128, 128), 1)

    def one_part(part, carry):
        def one(index, carry):
            rows = pl.ds(pl.multiple_of(part * rows_each + index * 16, 16), 16)
            for m in range(width // 128):
                at = slice(m * 128, (m + 1) * 128)
                cube = total_ref[4 + core, rows, at]
                total_ref[4 + core, rows, at] = linear * ham_ref[rows, at].astype(jnp.float32) + cubic * cube
            return carry

        lax.fori_loop(0, rows_each // 16, one, 0, unroll=2)

        @pl.when(row == 2 * col + core)
        def _():
            rows = pl.ds(pl.multiple_of(part * rows_each, rows_each), rows_each)
            at = pl.ds(pl.multiple_of(core * half + part * rows_each, rows_each), rows_each)
            total_ref[4 + core, rows, at] += jnp.where(eye, 0.5 + linear * level_rows_ref[rows, :], 0.0)

        density_copy(part).start()
        return carry

    lax.fori_loop(0, parts, one_part, 0)
    lines = half // 128
    cube_diag_ref[...] = jnp.zeros_like(cube_diag_ref)
    for k in range(lines):
        share = jnp.sum(diag_ref[pl.ds(k * 128, 128), :].T, 0, keepdims=True)
        cube_diag_ref[pl.ds((2 * row + core) * lines + k, 1), :] = share
    sent_copy.wait()
    for part in range(parts):
        density_copy(part).wait()


HERE = pl.BlockSpec(memory_space=pltpu.HBM)
SCALARS = pl.BlockSpec(memory_space=pltpu.SMEM)
VMEM = pl.BlockSpec(memory_space=pltpu.VMEM)
VMEM_BYTES = 38 * 2**20


def in_hbm(values):
    return [pltpu.with_memory_space_constraint(value, pltpu.HBM) for value in values]


def work_scratch(half, width, blocks, lefts):
    return [
        pltpu.VMEM((blocks, 2 * half, width), jnp.bfloat16),
        pltpu.SemaphoreType.DMA((blocks, 2)),
        pltpu.VMEM((lefts, half, width), jnp.bfloat16),
        pltpu.SemaphoreType.DMA((lefts,)),
    ]


def call_kernel(name, kernel, shape, scalars, operands, totals, in_vmem, out_shape, out_specs, scratch):
    first = len(scalars) + len(operands)
    held = [] if totals is None else [pltpu.with_memory_space_constraint(totals, pltpu.VMEM)]
    return pl.pallas_call(
        kernel,
        out_shape=(pltpu.VMEM((6,) + shape, jnp.float32),) + tuple(out_shape),
        in_specs=[SCALARS] * len(scalars) + [HERE] * len(operands) + [VMEM] * (len(held) + len(in_vmem)),
        out_specs=(VMEM,) + tuple(out_specs),
        scratch_shapes=scratch,
        input_output_aliases={first: 0} if held else {},
        compiler_params=pltpu.CompilerParams(vmem_limit_bytes=VMEM_BYTES),
        name=name,
    )(*scalars, *in_hbm(operands), *held, *in_vmem)


def pick_kernel(choices, whole, count, info_ref, *refs):
    sources, outs, in_sem = refs[:count], refs[count:-1], refs[-1]
    parts = in_sem.shape[1]
    size = outs[0].shape[0] // parts
    for part in range(parts):
        for k, choice in enumerate(choices):
            to = outs[k].at[pl.ds(part * size, size)]
            for number, source in enumerate(sources):
                @pl.when(info_ref[choice] == number)
                def _():
                    first = part * size
                    if number < whole:
                        first = pl.multiple_of(info_ref[FIRST_ROW] + first, size)
                    pltpu.make_async_copy(source.at[pl.ds(first, size)], to, in_sem.at[k, part]).start()
    for part in range(parts):
        for k, out_ref in enumerate(outs):
            to = out_ref.at[pl.ds(part * size, size)]
            pltpu.make_async_copy(to, to, in_sem.at[k, part]).wait()


def pick(info, choices, sources, whole, shape, fresh=0):
    held = [pltpu.with_memory_space_constraint(value, pltpu.VMEM) for value in sources[:fresh]]
    parts = 4
    return pl.pallas_call(
        functools.partial(pick_kernel, choices, whole, len(sources)),
        out_shape=[pltpu.VMEM(shape, sources[0].dtype)] * len(choices),
        in_specs=[SCALARS] + [VMEM] * fresh + [HERE] * (len(sources) - fresh),
        out_specs=[VMEM] * len(choices),
        scratch_shapes=[pltpu.SemaphoreType.DMA((len(choices), parts))],
        compiler_params=pltpu.CompilerParams(vmem_limit_bytes=8 * 2**20),
        name="pick",
    )(info, *held, *in_hbm(sources[fresh:]))


def pairs_kernel(spots_ref, points_ref, out_ref, weight_ref, wide_ref):
    count, width = points_ref.shape[0], spots_ref.shape[1]
    tiles = width // 128

    @pl.when(pl.program_id(0) == 0)
    def _():
        for k in range(4):
            wide_ref[k] = jnp.broadcast_to(points_ref[:, k : k + 1], (count, 128))

    lanes = [slice(m * 128, (m + 1) * 128) for m in range(tiles)]
    spots = [[jnp.broadcast_to(spots_ref[k : k + 1, at], (16, 128)) for k in range(3)] for at in lanes]

    def step(group, sums):
        rows = pl.ds(pl.multiple_of(group * 16, 16), 16)
        px, py, pz, charge = (wide_ref[k, rows, :] for k in range(4))
        sums = list(sums)
        for m, at in enumerate(lanes):
            dx, dy, dz = spots[m][0] - px, spots[m][1] - py, spots[m][2] - pz
            inv = lax.rsqrt(dx * dx + dy * dy + dz * dz + 1.0)
            sums[m] = sums[m] + charge * inv
            weight_ref[rows, at] = (inv * (inv * inv)).astype(jnp.bfloat16)
        return tuple(sums)

    zeros = tuple(jnp.zeros((16, 128), jnp.float32) for _ in range(tiles))
    sums = lax.fori_loop(0, count // 16, step, zeros, unroll=2)
    for m, at in enumerate(lanes):
        out_ref[:, at] = jnp.sum(sums[m], 0, keepdims=True)


def pair_terms(centers, points):
    total, count = centers.shape[1], points.shape[0]
    width = 512
    part = jax.ShapeDtypeStruct((count, total), jnp.bfloat16)
    return pl.pallas_call(
        pairs_kernel,
        grid=(total // width,),
        out_shape=(jax.ShapeDtypeStruct((1, total), jnp.float32), part),
        in_specs=[pl.BlockSpec((3, width), lambda i: (0, i)), pl.BlockSpec((count, 4), lambda i: (0, 0))],
        out_specs=[pl.BlockSpec((1, width), lambda i: (0, i))] + [pl.BlockSpec((count, width), lambda i: (0, i))],
        scratch_shapes=[pltpu.VMEM((4, count, 128), jnp.float32)],
        compiler_params=pltpu.CompilerParams(vmem_limit_bytes=VMEM_BYTES),
        name="pairs",
    )(centers, points)


def levels_kernel(info_ref, near_ref, far_ref, gain_ref, level_ref, above_ref, rows_ref):
    lines = level_ref.shape[0]
    sums = near_ref[...] + far_ref[...]
    potential, diag = sums[0:lines], sums[lines : 2 * lines] + sums[0:lines]
    total = float(lines * 128)
    mean = jnp.sum(diag) / total
    above = diag - mean
    squares = (jnp.sum(sums[2 * lines : 2 * lines + 1]) / 128.0 + jnp.sum(above * above)) / total
    spread = jnp.sqrt(jnp.full((8, 128), squares + 1e-05, jnp.float32))
    gain_ref[0] = jnp.max(1.0 / (3.0 * spread))
    level_ref[...] = potential - mean
    above_ref[...] = above
    half = rows_ref.shape[0]
    first = (2 * info_ref[ROW] + info_ref[CORE]) * (half // 128)
    for k in range(half // 128):
        line = level_ref[pl.ds(first + k, 1), :]
        rows_ref[pl.ds(k * 128, 128), :] = jnp.broadcast_to(line, (128, 128)).T


def level_terms(info, parts, lines, half):
    line = jax.ShapeDtypeStruct((lines, 128), jnp.float32)
    return pl.pallas_call(
        levels_kernel,
        out_shape=(jax.ShapeDtypeStruct((1,), jnp.float32), line, line, jax.ShapeDtypeStruct((half, 128), jnp.float32)),
        in_specs=[SCALARS] + [VMEM] * 2,
        out_specs=(SCALARS, VMEM, VMEM, VMEM),
        compiler_params=pltpu.CompilerParams(vmem_limit_bytes=4 * 2**20),
        name="levels",
    )(info, *parts)


MIDDLE = 10.0


def pull_kernel(gain_ref, spots_ref, above_ref, near_ref, far_ref, weight_ref, coords_ref, charge_ref, out_ref, total_ref):
    gain = gain_ref[0]
    lines = 10
    width = lines * 128

    def one(index, carry):
        lanes = pl.ds(pl.multiple_of(index * width, width), width)
        pieces = []
        for m in range(lines):
            line = pl.ds(index * lines + m, 1)
            cube = near_ref[line, :] + far_ref[line, :]
            pieces.append(0.5 - 1.5 * gain * above_ref[line, :] + 2.0 * (gain * gain * gain) * cube)
        occ = jnp.concatenate(pieces, 1)
        weights = [occ] + [occ * (spots_ref[k : k + 1, lanes] - MIDDLE) for k in range(3)]
        stacked = jnp.concatenate(weights + [jnp.zeros((4, width), jnp.float32)], 0)
        high = stacked.astype(jnp.bfloat16)
        low = (stacked - high.astype(jnp.float32)).astype(jnp.bfloat16)
        both = jnp.concatenate([high, low, jnp.zeros((128 - 16, width), jnp.bfloat16)], 0)
        total_ref[...] += lax.dot_general(
            weight_ref[:, lanes], both, (((1,), (1,)), ((), ())), preferred_element_type=jnp.float32
        )
        return carry

    total_ref[...] = jnp.zeros_like(total_ref)
    lax.fori_loop(0, spots_ref.shape[1] // width, one, 0)
    sums = total_ref[...].T
    sums = sums[0:8] + sums[8:16]
    for k in range(3):
        pull = (coords_ref[k : k + 1, :] - MIDDLE) * sums[0:1] - sums[k + 1 : k + 2]
        out_ref[k : k + 1, :] = -charge_ref[...] * pull


def pull_terms(gain, centers, above, near, far, weights, mm_coords, mm_charges):
    count = mm_coords.shape[1]
    return pl.pallas_call(
        pull_kernel,
        out_shape=jax.ShapeDtypeStruct((3, count), jnp.float32),
        in_specs=[SCALARS] + [VMEM] * 7,
        out_specs=VMEM,
        scratch_shapes=[pltpu.VMEM((count, 128), jnp.float32)],
        compiler_params=pltpu.CompilerParams(vmem_limit_bytes=16 * 2**20),
        name="pull",
    )(
        gain, centers, above, near, far, pltpu.with_memory_space_constraint(weights, pltpu.VMEM), mm_coords,
        mm_charges[None],
    )


def density_kernel(start, steps, info_ref, gain_ref, ham_ref, far_ref, level_ref, _, out_ref):
    index = pl.program_id(0)
    core, row, col = info_ref[CORE], info_ref[ROW], info_ref[COL]
    gain = gain_ref[0]
    height, width = out_ref.shape
    linear, cubic = -1.5 * gain, 2.0 * (gain * gain * gain)
    first = ((1 - core) * steps + start + index) * height

    def one(k, carry):
        rows = pl.ds(pl.multiple_of(k * 16, 16), 16)
        for m in range(width // 128):
            at = slice(m * 128, (m + 1) * 128)
            cube = far_ref[rows, at].astype(jnp.float32)
            out_ref[rows, at] = linear * ham_ref[rows, at].astype(jnp.float32) + cubic * cube
        return carry

    lax.fori_loop(0, height // 16, one, 0, unroll=2)

    @pl.when(row == 2 * col + core)
    def _():
        eye = lax.broadcasted_iota(jnp.int32, (128, 128), 0) == lax.broadcasted_iota(jnp.int32, (128, 128), 1)

        def fix(k, carry):
            rows = pl.ds(pl.multiple_of(k * 128, 128), 128)
            at = pl.ds(pl.multiple_of(first + k * 128, 128), 128)
            line = pl.ds((2 * col + core) * (width // 128) + first // 128 + k, 1)
            out_ref[rows, at] += jnp.where(eye, 0.5 + linear * level_ref[line, :], 0.0)
            return carry

        lax.fori_loop(0, height // 128, fix, 0)


def density_rest(info, gain, ham, far, level, density, start, stop):
    height, width = ham.shape
    chunk = 128
    steps = far.shape[0] // chunk
    return pl.pallas_call(
        functools.partial(density_kernel, start, steps),
        grid_spec=pltpu.PrefetchScalarGridSpec(
            num_scalar_prefetch=1,
            grid=(stop - start,),
            in_specs=[
                SCALARS,
                pl.BlockSpec((chunk, width), lambda i, info: ((1 - info[CORE]) * steps + start + i, 0)),
                pl.BlockSpec((chunk, width), lambda i, info: (start + i, 0)),
                pl.BlockSpec(level.shape, lambda i, info: (0, 0)),
                HERE,
            ],
            out_specs=pl.BlockSpec((chunk, width), lambda i, info: ((1 - info[CORE]) * steps + start + i, 0)),
        ),
        out_shape=jax.ShapeDtypeStruct((height, width), jnp.float32),
        input_output_aliases={5: 0},
        compiler_params=pltpu.CompilerParams(vmem_limit_bytes=VMEM_BYTES),
        name="density",
    )(info, gain, ham, far, level, density)


def gossip_shards(sizes, h_core, centers, mm_coords, mm_charges):
    height, width = h_core.shape
    half = height // 2
    total, count = centers.shape[1], mm_coords.shape[1]
    row, col, core = (lax.axis_index(name) for name in ("sec", "col", "rep"))
    row_start = row * height
    col_start = (2 * col + core) * width
    infos, rows, steps, slots_at = device_tables(half)
    device = 4 * row + 2 * col + core
    info, table = (
        lax.dynamic_index_in_dim(jnp.asarray(values, jnp.int32), device, 0, keepdims=False) for values in (infos, rows)
    )

    def over_rep(value):
        return lax.ppermute(value, "rep", [(0, 1), (1, 0)])

    def over_col(value):
        return lax.ppermute(value, "col", [(0, 1), (1, 0)])

    def over_sec(value, step):
        moves = [(2 * start + x, 2 * to + x) for x in range(2) for start, to in Z_MOVES[step][x]]
        return lax.ppermute(value, ("sec", "col"), moves)

    def over_both(value, own):
        moves = []
        for z, x, c in ((z, x, c) for z in range(4) for x in range(2) for c in range(2)):
            if (c if own else 1 - c) == X_SENDS[0][z]:
                to = (z, 1 - x, c)
            else:
                to = (dict(Z_MOVES[0][x])[z], x, 1 - c)
            moves.append((4 * z + 2 * x + c, 4 * to[0] + 2 * to[1] + to[2]))
        return lax.ppermute(value, ("sec", "col", "rep"), moves)

    def swap_all(values):
        return [(value, over_rep(value)) for value in values]

    def flat(groups):
        return [value for group in groups for value in group]

    def after(arrived, work):
        return lax.optimization_barrier((arrived, work))

    shape = (half, width)
    near = lax.dynamic_slice_in_dim(h_core, core * half, half, 0)
    far = lax.dynamic_slice_in_dim(h_core, (1 - core) * half, half, 0)
    got = over_rep(far)
    firsts = (over_both(near, True), over_both(got, False))
    other = over_rep(near)
    points = jnp.concatenate([mm_coords, mm_charges[None]], 0).T
    terms, weights = pair_terms(centers, points)
    rows_glob = row_start + lax.broadcasted_iota(jnp.int32, (height, width), 0)
    cols_glob = col_start + lax.broadcasted_iota(jnp.int32, (height, width), 1)
    on_diag = rows_glob == cols_glob
    wide = h_core.astype(jnp.float32)
    own_diag = jnp.sum(jnp.where(on_diag, wide, 0.0), 0)
    own_off = jnp.sum(jnp.where(on_diag, 0.0, wide * wide))
    diag = lax.dynamic_update_slice_in_dim(jnp.zeros((total,), jnp.float32), own_diag, col_start, 0)
    packed = jnp.concatenate([terms[0], diag, jnp.full((8 * 128,), own_off)]).reshape(-1, 128)
    packed = packed + over_rep(packed)
    from_col = over_col(packed)
    (firsts, from_col), (packed, weights, table, other) = after((firsts, from_col), (packed, weights, table, other))
    own_parts = [h_core, got, other]
    sends = pick(info, (SEND_X2, SEND_Z2), (h_core, got) + tuple(firsts), 1, shape)
    firsts, sends = lax.optimization_barrier((list(firsts), sends))
    z2 = over_sec(sends[1], 1)
    x2 = over_col(sends[0])
    packed = packed + from_col
    from_near = lax.ppermute(packed, "sec", [(i, i ^ 1) for i in range(4)])
    operands = own_parts + firsts + [over_rep(first) for first in firsts]

    def grow_square(stage, left_count, slots, totals, token):
        kernel = functools.partial(square_kernel, totals is None, steps[stage], left_count, slots)
        return call_kernel(
            f"square_{stage}", kernel, shape, (table, info), operands + ([] if token is None else [token]), totals, (),
            (jax.ShapeDtypeStruct((8, 128), jnp.float32),), (VMEM,), work_scratch(half, width, len(slots), 4),
        )

    totals, token = grow_square(0, 3, (OWN0, OWN1, X1, Z1), None, None)
    (x2, z2, from_near), (token, packed) = after((x2, z2, from_near), (token, packed))
    z3 = over_sec(x2, 2)
    x3 = over_col(z2)
    operands = operands + flat(swap_all((x2, z2)))
    totals, token = grow_square(1, 4, (OWN0, OWN1, X1, Z1, X2, Z2), totals, token)
    packed = packed + from_near
    from_far = lax.ppermute(packed, "sec", [(i, i ^ 2) for i in range(4)])
    (x3, z3, from_far), (token, packed) = after((x3, z3, from_far), (token, packed))
    last_send = pick(info, (SEND_LAST,), [z3] + operands[5:7], 0, shape, 1)[0]
    (x3, z3), last_send = after((x3, z3), last_send)
    z4 = over_sec(last_send, 3)
    x4 = over_col(last_send)
    operands = operands + flat(swap_all((x3, z3)))
    gain, level, above, level_rows = level_terms(info, [packed, from_far], total // 128, half)
    lines = jax.ShapeDtypeStruct((total // 128, 128), jnp.float32)
    share = jax.ShapeDtypeStruct((half, 128), jnp.float32)
    totals, cube_diag = call_kernel(
        "early_cube", functools.partial(early_kernel, steps[2], slots_at[0]), shape, (table, info),
        operands + [token], totals, (level_rows, level),
        (share,), (VMEM,), work_scratch(half, width, 6, 6),
    )
    (x4, z4), (cube_diag, above, level_rows, level, gain) = after(
        (x4, z4), (cube_diag, above, level_rows, level, gain)
    )
    operands = operands + flat(swap_all((x4, z4)))
    _, sibling, density, cube_diag = call_kernel(
        "late_cube", functools.partial(late_kernel, steps[3], slots_at[1]), shape, (table, info, gain),
        operands, totals, (cube_diag, level_rows, level),
        (jax.ShapeDtypeStruct(shape, jnp.bfloat16), jax.ShapeDtypeStruct((height, width), jnp.float32), lines),
        (HERE, HERE, VMEM),
        work_scratch(half, width, 6, 4)
        + [
            pltpu.SemaphoreType.DMA((2,)),
            pltpu.VMEM(shape, jnp.bfloat16),
            pltpu.VMEM(shape, jnp.bfloat16),
            pltpu.SemaphoreType.DMA,
            pltpu.VMEM((half, 128), jnp.float32),
        ],
    )
    sibling = over_rep(sibling)
    cube_diag = cube_diag + over_rep(cube_diag)
    from_near = lax.ppermute(cube_diag, "sec", [(i, i ^ 1) for i in range(4)])
    density = density_rest(info, gain, h_core, sibling, level, density, 0, 3)
    from_near, density = after(from_near, density)
    cube_diag = cube_diag + from_near
    from_far = lax.ppermute(cube_diag, "sec", [(i, i ^ 2) for i in range(4)])
    density = density_rest(info, gain, h_core, sibling, level, density, 3, 5)
    from_far, density = after(from_far, density)
    forces = pull_terms(gain, centers, above, cube_diag, from_far, weights, mm_coords, mm_charges)
    return (density, forces)


def solution(mesh):
    in_specs = (
        P(("groups", "sec"), ("col", "rep")),
        P(None, "groups"),
        P(None, ("groups", "sec", "col", "rep")),
        P(("groups", "sec", "col", "rep")),
    )
    out_specs = (P(("groups", "sec"), ("col", "rep")), P(None, ("groups", "sec", "col", "rep")))
    sizes = dict(mesh.shape)
    small = (sizes["sec"], sizes["col"], sizes["rep"]) == (4, 2, 2)
    body = functools.partial(gossip_shards if small else gather_shards, sizes)
    return jax.shard_map(body, mesh=mesh, in_specs=in_specs, out_specs=out_specs, check_vma=False)
```
